32 devices in a mesh: tx: 4 (over x, core), rx: 8 (over z, y).
Axes of the slice: x: 2, y: 2, z: 4, core: 2. Of those that a mesh axis runs over, the one named last changes fastest.
Arguments:
- records: bfloat16 [40, 256, 4096], P(None, 'tx', 'rx'), may hold values from -6 to 6
- active: int32 [256, 64], P('tx', 'rx'), may hold values 0 or 1
- green: bfloat16 [4, 2, 4096, 4096], P(None, None, 'rx', 'tx'), may hold values from -0.0625 to 0.0625
- background: bfloat16 [256, 4, 2, 4096], P('rx', None, None, 'tx'), may hold values from -0.125 to 0.125
Outputs:
- gradient: float32 [4096], P('tx')
The draws below stay inside these ranges and needn't reach their ends.
All inputs are finite; a program needn't handle non-finite values. No bound on the sum of `active` on one device may be relied on, other than what follows from the above.
Results may differ from the reference program's by a relative error of at most 0.004.
Values may be sent and summed in bfloat16 or wider, within the bound.
No kernel may reach another device: no remote copies, remote signals or barrier semaphores. Data moves between devices by JAX's collectives and lax.ppermute only.
A program may use at most 128 MiB of HBM per device.

```python
import math
import jax
import jax.numpy as jnp
from jax import lax

FREQS = 4
GATES = 40
CELLS = 4096
TRANS = 256
BLOCK = 64
RECV = 4096


def with_ends(array, rng, smallest, top_value):
    extent = array.shape
    place = [jax.random.randint(jax.random.fold_in(rng, axis), (), 0, extent[axis]) for axis in range(len(extent))]
    array = array.at[tuple(place)].set(smallest)
    longest = extent.index(max(extent))
    place[longest] = (place[longest] + 1) % extent[longest]
    return array.at[tuple(place)].set(top_value)


def raised(result, own_key, source, target, blocks, factor):
    def block_of(dim):
        return (jnp.arange(result.shape[dim]) // (result.shape[dim] // blocks)).reshape((-1,) + (1,) * (result.ndim - 1 - dim))

    one_side = jax.random.permutation(own_key, blocks)[block_of(target)]
    other_side = (block_of(target) + blocks // 2) % blocks
    return jnp.where((block_of(source) == one_side) | (block_of(source) == other_side), factor * result, result)


def block_levels(rng, extent, split, low, largest):
    level, own = 1.0, jax.random.fold_in(rng, 6)
    for dim, parts in split:
        draws = jnp.exp(jax.random.uniform(jax.random.fold_in(own, dim), (parts,), jnp.float32, low / len(split), largest / len(split)))
        level = level * jnp.repeat(draws, extent[dim] // parts).reshape([-1 if axis == dim else 1 for axis in range(len(extent))])
    return level


def scatter_about(rng, extent, spread, reach, shards=(), kind=jnp.bfloat16):
    gain = block_levels(rng, extent, shards, -0.22, 0.18) if shards else 1.0
    drawn = jax.random.normal(rng, extent, jnp.float32) * spread * gain
    return jnp.minimum(jnp.maximum(drawn, -reach), reach).astype(kind)


def noise_with(key, dims, scale, reach, pieces, heavy, kind=jnp.bfloat16):
    drawn = scale * jax.random.normal(key, dims, jnp.float32)
    if pieces:
        drawn = drawn * block_levels(key, dims, pieces, -0.22, 0.18)
    return jnp.clip(raised(drawn, jax.random.fold_in(key, 3), *heavy), -reach, reach).astype(kind)


def setup_inputs(seed: int = 0) -> dict:
    keys = jax.random.split(jax.random.key(seed), 5)
    return {
        "records": noise_with(keys[0], (GATES, TRANS, RECV), 1.0, 6.0, ((1, 4), (2, 8)), (2, 1, 8, 2.0)),
        "active": with_ends((jax.random.randint(keys[1], (TRANS, RECV // BLOCK), 0, 3) < 2).astype(jnp.int32), jax.random.fold_in(keys[1], 1), 0, 1),
        "green": scatter_about(keys[2], (FREQS, 2, RECV, CELLS), (2 * RECV) ** -0.5, 0.0625, ((2, 8), (3, 4))),
        "background": scatter_about(keys[3], (TRANS, FREQS, 2, CELLS), (2 * FREQS * TRANS) ** -0.5, 0.125, ((0, 8), (3, 4))),
    }


def cosine_table():
    gate_index = jnp.arange(GATES, dtype=jnp.float32)
    freq_index = jnp.arange(FREQS, dtype=jnp.float32)
    phases = jnp.pi * (2.0 * gate_index[None, :] + 1.0) * (1.0 + 3.0 * freq_index[:, None]) / (2.0 * GATES)
    weight_scale = jnp.sqrt(2.0 / GATES)
    stacked = jnp.stack([jnp.cos(phases) * weight_scale, -jnp.sin(phases) * weight_scale], axis=1)
    return stacked.reshape(2 * FREQS, GATES).astype(jnp.bfloat16)

def reference(records, active, green, background):
    table_f32 = cosine_table().astype(jnp.float32)
    recv_block = math.gcd(RECV, 2048)

    def add_block(block_index, adjoint):
        first_recv = (block_index * recv_block).astype(jnp.int32)
        record_block = lax.dynamic_slice_in_dim(records, first_recv, recv_block, 2)
        active_block = lax.dynamic_slice_in_dim(active, (first_recv // BLOCK).astype(jnp.int32), recv_block // BLOCK, 1)
        shaped = record_block.reshape(GATES, TRANS, recv_block // BLOCK, BLOCK)
        masked = (shaped * active_block.astype(records.dtype)[None, :, :, None]).reshape(GATES, TRANS, recv_block)
        spectrum = jnp.einsum('cg,gsr->scr', table_f32, masked.astype(jnp.float32)).astype(jnp.bfloat16)
        spectrum = lax.optimization_barrier(spectrum).astype(jnp.float32).reshape(TRANS, FREQS, 2, recv_block)
        green_block = lax.dynamic_slice_in_dim(green, first_recv, recv_block, 2).astype(jnp.float32)
        real_real = jnp.einsum('sfr,frm->sfm', spectrum[:, :, 0], green_block[:, 0])
        imag_imag = jnp.einsum('sfr,frm->sfm', spectrum[:, :, 1], green_block[:, 1])
        real_imag = jnp.einsum('sfr,frm->sfm', spectrum[:, :, 0], green_block[:, 1])
        imag_real = jnp.einsum('sfr,frm->sfm', spectrum[:, :, 1], green_block[:, 0])
        return adjoint + jnp.stack([real_real - imag_imag, real_imag + imag_real], axis=2)
    adjoint = lax.fori_loop(0, RECV // recv_block, add_block, jnp.zeros((TRANS, FREQS, 2, CELLS), jnp.float32))
    background_f32 = background.astype(jnp.float32)
    products = background_f32[:, :, 0] * adjoint[:, :, 0] - background_f32[:, :, 1] * adjoint[:, :, 1]
    return lax.optimization_barrier(jnp.sum(products, axis=(0, 1)))
```

```python
import functools

import jax
import jax.numpy as jnp
import numpy as np
from jax import lax
from jax.experimental import pallas as pl
from jax.experimental.pallas import tpu as pltpu
from jax.sharding import PartitionSpec as P

ROWS = 16


def spread_table(gate_count, freq_count):
    gates = np.arange(gate_count, dtype=np.float32)
    freqs = np.arange(freq_count, dtype=np.float32)
    phases = (
        np.float32(np.pi)
        * (np.float32(2) * gates[None, :] + np.float32(1))
        * (np.float32(1) + np.float32(3) * freqs[:, None])
        / np.float32(2 * gate_count)
    )
    scale = np.sqrt(np.float32(2.0 / gate_count))
    table = np.stack([np.cos(phases) * scale, -np.sin(phases) * scale], axis=1)
    table = table.reshape(2 * freq_count, gate_count).astype(jnp.bfloat16).astype(np.float32)
    return np.kron(table, np.eye(ROWS, dtype=np.float32)).astype(jnp.bfloat16)


def spectra_kernel(table_ref, active_ref, records_ref, out_ref):
    gates, rows, recv = records_ref.shape
    blocks = active_ref.shape[1]
    flat = records_ref[...].reshape(gates * rows, recv)
    sums = jnp.dot(table_ref[...], flat, preferred_element_type=jnp.float32)
    block_of = lax.broadcasted_iota(jnp.int32, (blocks, recv), 1) // (recv // blocks)
    spread = (block_of == lax.broadcasted_iota(jnp.int32, (blocks, recv), 0)).astype(jnp.float32)
    mask = jnp.dot(
        active_ref[...].astype(jnp.float32), spread, preferred_element_type=jnp.float32
    )
    channels = out_ref.shape[0]
    out_ref[...] = (sums.reshape(channels, rows, recv) * mask[None]).astype(out_ref.dtype)


def spectra_of(records, active, freq_count):
    gates, trans, recv = records.shape
    blocks = active.shape[1]
    channels = 2 * freq_count
    table = jnp.asarray(spread_table(gates, freq_count))
    return pl.pallas_call(
        spectra_kernel,
        grid=(trans // ROWS,),
        in_specs=[
            pl.BlockSpec(table.shape, lambda i: (0, 0)),
            pl.BlockSpec((ROWS, blocks), lambda i: (i, 0)),
            pl.BlockSpec((gates, ROWS, recv), lambda i: (0, i, 0)),
        ],
        out_specs=pl.BlockSpec((channels, ROWS, recv), lambda i: (0, i, 0)),
        out_shape=jax.ShapeDtypeStruct((channels, trans, recv), jnp.bfloat16),
        compiler_params=pltpu.CompilerParams(vmem_limit_bytes=24 << 20),
        cost_estimate=pl.CostEstimate(
            flops=2 * channels * ROWS * gates * trans * recv,
            bytes_accessed=2 * (gates + channels) * trans * recv,
            transcendentals=0,
        ),
        name="spectra",
    )(table, active, records)


def adjoint_kernel(*refs):
    spectra_refs, green_ref, out_ref = refs[:-2], refs[-2], refs[-1]
    rows = spectra_refs[0].shape[2]
    green = green_ref[0]
    real = jnp.concatenate([ref[0, 0] for ref in spectra_refs], axis=0)
    imag = jnp.concatenate([ref[0, 1] for ref in spectra_refs], axis=0)
    for part, left in enumerate(
        (jnp.concatenate([real, -imag], axis=1), jnp.concatenate([-imag, -real], axis=1))
    ):
        sums = jnp.dot(left, green, preferred_element_type=jnp.float32)
        for slot in range(len(spectra_refs)):
            out_ref[0, part, slot] = sums[slot * rows : (slot + 1) * rows]


def adjoint_of(pieces, green):
    freqs, _, recv, cells = green.shape
    rows = pieces[0].shape[1]
    pieces = [piece.reshape(freqs, 2, rows, recv) for piece in pieces]
    count = len(pieces)
    return pl.pallas_call(
        adjoint_kernel,
        grid=(freqs,),
        in_specs=[pl.BlockSpec((1, 2, rows, recv), lambda f: (f, 0, 0, 0))] * count
        + [pl.BlockSpec((1, 2 * recv, cells), lambda f: (f, 0, 0))],
        out_specs=pl.BlockSpec((1, 2, count, rows, cells), lambda f: (f, 0, 0, 0, 0)),
        out_shape=jax.ShapeDtypeStruct((freqs, 2, count, rows, cells), jnp.float32),
        compiler_params=pltpu.CompilerParams(vmem_limit_bytes=40 << 20),
        cost_estimate=pl.CostEstimate(
            flops=8 * freqs * count * rows * recv * cells,
            bytes_accessed=4 * freqs * recv * cells + 8 * freqs * count * rows * cells,
            transcendentals=0,
        ),
        name="adjoint",
    )(*pieces, green.reshape(freqs, 2 * recv, cells))


def weigh_kernel(last, place_ref, mine_ref, other_ref, field_ref, field_other_ref, sum_ref, out_ref, total):
    del place_ref
    step = pl.program_id(0)

    @pl.when(step == 0)
    def _():
        total[...] = sum_ref[...]

    cells = total.shape[1]
    sums = total[...]
    for adjoint, field in ((mine_ref, field_ref), (other_ref, field_other_ref)):
        terms = adjoint[0, :, 0].reshape(-1, cells) * field[0].reshape(-1, cells).astype(jnp.float32)
        sums = sums + jnp.sum(terms.reshape(-1, 8, cells), axis=0)
    total[...] = sums

    @pl.when(step == pl.num_programs(0) - 1)
    def _():
        if last:
            out_ref[...] = jnp.sum(total[...], axis=0, keepdims=True)
        else:
            out_ref[...] = total[...]


def weigh(adjoint, place, mine, other, sums, last):
    freqs, _, blocks, rows, cells = adjoint.shape
    field = pl.BlockSpec((1, 2, rows, cells), lambda f, place: (f, 0, 0, 0))
    out_rows = 1 if last else 8
    return pl.pallas_call(
        functools.partial(weigh_kernel, last),
        grid_spec=pltpu.PrefetchScalarGridSpec(
            num_scalar_prefetch=1,
            grid=(freqs,),
            in_specs=[
                pl.BlockSpec((1, 2, 1, rows, cells), lambda f, place: (f, 0, place[0], 0, 0)),
                pl.BlockSpec((1, 2, 1, rows, cells), lambda f, place: (f, 0, place[1], 0, 0)),
                field,
                field,
                pl.BlockSpec((8, cells), lambda f, place: (0, 0)),
            ],
            out_specs=pl.BlockSpec((out_rows, cells), lambda f, place: (0, 0)),
            scratch_shapes=[pltpu.VMEM((8, cells), jnp.float32)],
        ),
        out_shape=jax.ShapeDtypeStruct((out_rows, cells), jnp.float32),
        compiler_params=pltpu.CompilerParams(vmem_limit_bytes=16 << 20),
        cost_estimate=pl.CostEstimate(
            flops=8 * freqs * rows * cells,
            bytes_accessed=24 * freqs * rows * cells,
            transcendentals=0,
        ),
        name="weigh",
    )(place, adjoint, adjoint, mine, other, sums)


def box_shards(records, active, green, background):
    freqs = green.shape[0]
    along_y = [(r, r ^ 1) for r in range(8)]
    z_pairs = [(r, r ^ 2) for r in range(8)]
    z_middle = [(r, r ^ 6) for r in range(2, 6)]
    z_outward = [(2, 0), (3, 1), (4, 6), (5, 7)]
    core = [(t, t ^ 1) for t in range(4)]
    along_x = [(t, t ^ 2) for t in range(4)]
    send = lax.ppermute

    me_tx, me_rx = lax.axis_index("tx"), lax.axis_index("rx")
    me_z, me_y = me_rx // 2, me_rx % 2
    middle = (me_z == 1) | (me_z == 2)

    own = background.transpose(1, 2, 0, 3)
    near = send(own, "rx", z_pairs)
    across = send(own, "rx", z_middle)
    own_y = send(own, "rx", along_y)

    spectra = spectra_of(records, active, freqs)
    spectra_x = send(spectra, "tx", along_x)
    spectra_core = send(spectra, "tx", core)

    near_y = send(near, "rx", along_y)
    across_out = send(across, "rx", z_outward)
    far = send(near, "rx", z_middle)
    spectra_both = send(spectra_x, "tx", core)
    mid = jnp.where(middle, across, across_out)
    mid_y = send(mid, "rx", along_y)
    far_out = send(far, "rx", z_outward)
    end = jnp.where(middle, far, far_out)
    end_y = send(end, "rx", along_y)

    adjoint = adjoint_of([spectra, spectra_core, spectra_x, spectra_both], green)
    freqs, _, groups, rows, cells = adjoint.shape
    adjoint = adjoint.reshape(freqs, 2, 2 * groups, rows // 2, cells)

    lower = me_z < 2
    owners = (
        (me_z, own, own_y),
        (me_z ^ 1, near, near_y),
        (jnp.where(lower, 2, 1), mid, mid_y),
        (jnp.where(lower, 3, 0), end, end_y),
    )
    sums = jnp.zeros((8, cells), jnp.float32)
    for step, (owner, mine, other) in enumerate(owners):
        slot = (owner ^ me_tx) * 2
        place = jnp.stack([slot + me_y, slot + 1 - me_y]).astype(jnp.int32)
        sums = weigh(adjoint, place, mine, other, sums, step == len(owners) - 1)
    sums = sums.reshape(cells)
    for bit in (1, 2, 4):
        sums = sums + send(sums, "rx", [(r, r ^ bit) for r in range(8)])
    return sums


def plain_shards(records, active, green, background):
    freqs = green.shape[0]
    spectra = spectra_of(records, active, freqs)
    pieces = lax.all_gather(spectra, "tx", axis=0)
    adjoint = adjoint_of([pieces[t] for t in range(pieces.shape[0])], green)
    freqs, _, groups, rows, cells = adjoint.shape
    adjoint = adjoint.reshape(freqs, 2, groups * rows, cells)
    fields = lax.all_gather(background, "rx", axis=0, tiled=True)
    fields = fields.transpose(1, 2, 0, 3).astype(jnp.float32)
    return lax.psum(jnp.sum(adjoint * fields, axis=(0, 1, 2)), "rx")


def solution(mesh):
    placed = (
        P(None, "tx", "rx"),
        P("tx", "rx"),
        P(None, None, "rx", "tx"),
        P("rx", None, None, "tx"),
    )
    body = box_shards if (mesh.shape["tx"], mesh.shape["rx"]) == (4, 8) else plain_shards
    return jax.shard_map(body, mesh=mesh, in_specs=placed, out_specs=P("tx"), check_vma=False)
```

```python
import functools

import jax
import jax.numpy as jnp
import numpy as np
from jax import lax
from jax.experimental import pallas as pl
from jax.experimental.pallas import tpu as pltpu
from jax.sharding import PartitionSpec as P

ROWS = 16


def spread_table(gate_count, freq_count):
    gates = np.arange(gate_count, dtype=np.float32)
    freqs = np.arange(freq_count, dtype=np.float32)
    phases = (
        np.float32(np.pi)
        * (np.float32(2) * gates[None, :] + np.float32(1))
        * (np.float32(1) + np.float32(3) * freqs[:, None])
        / np.float32(2 * gate_count)
    )
    scale = np.sqrt(np.float32(2.0 / gate_count))
    table = np.stack([np.cos(phases) * scale, -np.sin(phases) * scale], axis=1)
    table = table.reshape(2 * freq_count, gate_count).astype(jnp.bfloat16).astype(np.float32)
    return np.kron(table, np.eye(ROWS, dtype=np.float32)).astype(jnp.bfloat16)


def spectra_kernel(table_ref, active_ref, records_ref, out_ref):
    gates, rows, recv = records_ref.shape
    blocks = active_ref.shape[1]
    flat = records_ref[...].reshape(gates * rows, recv)
    sums = jnp.dot(table_ref[...], flat, preferred_element_type=jnp.float32)
    block_of = lax.broadcasted_iota(jnp.int32, (blocks, recv), 1) // (recv // blocks)
    spread = (block_of == lax.broadcasted_iota(jnp.int32, (blocks, recv), 0)).astype(jnp.float32)
    mask = jnp.dot(
        active_ref[...].astype(jnp.float32), spread, preferred_element_type=jnp.float32
    )
    channels = out_ref.shape[0]
    out_ref[...] = (sums.reshape(channels, rows, recv) * mask[None]).astype(out_ref.dtype)


def spectra_of(records, active, freq_count):
    gates, trans, recv = records.shape
    blocks = active.shape[1]
    channels = 2 * freq_count
    table = jnp.asarray(spread_table(gates, freq_count))
    return pl.pallas_call(
        spectra_kernel,
        grid=(trans // ROWS,),
        in_specs=[
            pl.BlockSpec(table.shape, lambda i: (0, 0)),
            pl.BlockSpec((ROWS, blocks), lambda i: (i, 0)),
            pl.BlockSpec((gates, ROWS, recv), lambda i: (0, i, 0)),
        ],
        out_specs=pl.BlockSpec((channels, ROWS, recv), lambda i: (0, i, 0)),
        out_shape=jax.ShapeDtypeStruct((channels, trans, recv), jnp.bfloat16),
        compiler_params=pltpu.CompilerParams(vmem_limit_bytes=16 << 20),
        cost_estimate=pl.CostEstimate(
            flops=2 * channels * ROWS * gates * trans * recv,
            bytes_accessed=2 * (gates + channels) * trans * recv,
            transcendentals=0,
        ),
        name="spectra",
    )(table, active, pltpu.with_memory_space_constraint(records, pltpu.HBM))


def adjoint_kernel(*refs):
    spectra_refs, green_ref, out_ref = refs[:-2], refs[-2], refs[-1]
    rows = spectra_refs[0].shape[2]
    green = green_ref[0]
    real = jnp.concatenate([ref[0, 0] for ref in spectra_refs], axis=0)
    imag = jnp.concatenate([ref[0, 1] for ref in spectra_refs], axis=0)
    for part, left in enumerate(
        (jnp.concatenate([real, -imag], axis=1), jnp.concatenate([-imag, -real], axis=1))
    ):
        sums = jnp.dot(left, green, preferred_element_type=jnp.float32)
        for slot in range(len(spectra_refs)):
            out_ref[0, part, slot] = sums[slot * rows : (slot + 1) * rows]


def adjoint_of(pieces, green):
    freqs, _, recv, cells = green.shape
    rows = pieces[0].shape[1]
    pieces = [piece.reshape(freqs, 2, rows, recv) for piece in pieces]
    count = len(pieces)
    return pl.pallas_call(
        adjoint_kernel,
        grid=(freqs,),
        in_specs=[pl.BlockSpec((1, 2, rows, recv), lambda f: (f, 0, 0, 0))] * count
        + [pl.BlockSpec((1, 2 * recv, cells), lambda f: (f, 0, 0))],
        out_specs=pl.BlockSpec((1, 2, count, rows, cells), lambda f: (f, 0, 0, 0, 0)),
        out_shape=pltpu.VMEM((freqs, 2, count, rows, cells), jnp.float32),
        compiler_params=pltpu.CompilerParams(vmem_limit_bytes=20 << 20),
        cost_estimate=pl.CostEstimate(
            flops=8 * freqs * count * rows * recv * cells,
            bytes_accessed=4 * freqs * recv * cells + 8 * freqs * count * rows * cells,
            transcendentals=0,
        ),
        name="adjoint",
    )(*pieces, pltpu.with_memory_space_constraint(green.reshape(freqs, 2 * recv, cells), pltpu.HBM))


def in_vmem(kernel, scalars, operands, shape, dtype, name):
    return pl.pallas_call(
        kernel,
        in_specs=[pl.BlockSpec(memory_space=pltpu.SMEM)]
        + [pl.BlockSpec(memory_space=pltpu.VMEM)] * len(operands),
        out_specs=pl.BlockSpec(memory_space=pltpu.VMEM),
        out_shape=pltpu.VMEM(shape, dtype),
        compiler_params=pltpu.CompilerParams(vmem_limit_bytes=16 << 20),
        cost_estimate=pl.CostEstimate(
            flops=4 * sum(operand.size for operand in operands[1:]),
            bytes_accessed=4 * sum(operand.size for operand in operands[1:]),
            transcendentals=0,
        ),
        name=name,
    )(
        jnp.stack(scalars).astype(jnp.int32),
        *[pltpu.with_memory_space_constraint(operand, pltpu.VMEM) for operand in operands],
    )


def weigh_kernel(count, paired, extra, last, place_ref, adjoint_ref, *refs):
    field_refs, (sum_ref, out_ref) = list(refs[:-2]), refs[-2:]
    extra_ref = field_refs.pop() if extra else None
    freqs, parts, _, cells = field_refs[0].shape
    second = place_ref[count] != 0
    sums = sum_ref[...]
    position = 0
    for number in range(count):
        place = place_ref[number]
        for freq in range(freqs):
            for part in range(parts):
                weights = adjoint_ref[freq, part, place]
                if extra and number == count - 1:
                    weights = weights + extra_ref[freq, part].astype(jnp.float32)
                field = field_refs[position][freq, part].astype(jnp.float32)
                if number == paired:
                    other = field_refs[position + 1][freq, part].astype(jnp.float32)
                    field = jnp.where(second, other, field)
                terms = weights * field
                sums = sums + jnp.sum(terms.reshape(-1, 8, cells), axis=0)
        position += 1 + (number == paired)
    out_ref[...] = jnp.sum(sums, axis=0, keepdims=True) if last else sums


def pick_kernel(flag_ref, first_ref, second_ref, out_ref):
    @pl.when(flag_ref[0] == 0)
    def _():
        out_ref[...] = first_ref[...]

    @pl.when(flag_ref[0] != 0)
    def _():
        out_ref[...] = second_ref[...]


def block_kernel(place_ref, adjoint_ref, out_ref):
    out_ref[...] = adjoint_ref[:, :, place_ref[0]].astype(out_ref.dtype)


def box_shards(records, active, green, background):
    freqs = green.shape[0]
    along_y = [(r, r ^ 1) for r in range(8)]
    z_pairs = [(r, r ^ 2) for r in range(8)]
    z_middle = [(r, r ^ 6) for r in range(2, 6)]
    z_outward = [(2, 0), (3, 1), (4, 6), (5, 7)]
    z_inward = [(there, here) for here, there in z_outward]
    core = [(t, t ^ 1) for t in range(4)]
    along_x = [(t, t ^ 2) for t in range(4)]
    send, tie = lax.ppermute, lax.optimization_barrier

    me_tx, me_rx = lax.axis_index("tx"), lax.axis_index("rx")
    me_z, me_y = me_rx // 2, me_rx % 2
    middle = (me_z == 1) | (me_z == 2)
    lower = me_z < 2

    own = background.transpose(1, 2, 0, 3)
    near = send(own, "rx", z_pairs)
    across = send(own, "rx", z_middle)
    own_y = send(own, "rx", along_y)

    spectra = spectra_of(records, active, freqs)
    spectra_x = send(spectra, "tx", along_x)
    spectra_core = send(spectra, "tx", core)

    near, across, own_y, spectra_core = tie((near, across, own_y, spectra_core))
    across_out = send(across, "rx", z_outward)
    far = send(near, "rx", z_middle)
    near_y = send(near, "rx", along_y)

    spectra_both = send(spectra_x, "tx", core)
    adjoint = adjoint_of([spectra, spectra_core, spectra_x, spectra_both], green)
    freqs, _, groups, rows, cells = adjoint.shape
    adjoint = adjoint.reshape(freqs, 2, 2 * groups, rows // 2, cells)

    def place_of(z, y):
        return (z ^ me_tx) * 2 + y

    mid_z, far_z, other_y = jnp.where(lower, 2, 1), jnp.where(lower, 3, 0), 1 - me_y
    far_place = place_of(far_z, other_y)
    partial = in_vmem(block_kernel, [far_place], [adjoint], own.shape, own.dtype, "block")
    partial, far, near_y, across_out = tie((partial, far, near_y, across_out))
    partial = send(partial, "rx", z_inward)
    far_out = send(far, "rx", z_outward)
    far_both = send(near_y, "rx", z_middle)
    mid = in_vmem(pick_kernel, [middle], [across_out, across], own.shape, own.dtype, "pick")
    mid_y = send(mid, "rx", along_y)

    zero = jnp.zeros((), jnp.int32)
    places = [place_of(me_z, me_y), place_of(me_z, other_y), place_of(me_z ^ 1, me_y), place_of(me_z ^ 1, other_y)]
    sums = in_vmem(
        functools.partial(weigh_kernel, 5, -1, False, False),
        places + [place_of(mid_z, me_y), zero],
        [adjoint, own, own_y, near, near_y, mid, jnp.zeros((8, cells), jnp.float32)],
        (8, cells),
        jnp.float32,
        "weigh",
    )
    sums = in_vmem(
        functools.partial(weigh_kernel, 3, 1, True, True),
        [place_of(mid_z, other_y), place_of(far_z, me_y), far_place, middle],
        [adjoint, mid_y, far_out, far, far_both, partial, sums],
        (1, cells),
        jnp.float32,
        "weigh",
    )
    sums = sums.reshape(cells)
    for bit in (1, 2, 4):
        sums = sums + send(sums, "rx", [(r, r ^ bit) for r in range(8)])
    return sums


def plain_shards(records, active, green, background):
    freqs = green.shape[0]
    spectra = spectra_of(records, active, freqs)
    pieces = lax.all_gather(spectra, "tx", axis=0)
    adjoint = adjoint_of([pieces[t] for t in range(pieces.shape[0])], green)
    freqs, _, groups, rows, cells = adjoint.shape
    adjoint = adjoint.reshape(freqs, 2, groups * rows, cells)
    fields = lax.all_gather(background, "rx", axis=0, tiled=True)
    fields = fields.transpose(1, 2, 0, 3).astype(jnp.float32)
    return lax.psum(jnp.sum(adjoint * fields, axis=(0, 1, 2)), "rx")


def solution(mesh):
    placed = (
        P(None, "tx", "rx"),
        P("tx", "rx"),
        P(None, None, "rx", "tx"),
        P("rx", None, None, "tx"),
    )
    body = box_shards if (mesh.shape["tx"], mesh.shape["rx"]) == (4, 8) else plain_shards
    return jax.shard_map(body, mesh=mesh, in_specs=placed, out_specs=P("tx"), check_vma=False)
```

```python
import functools

import jax
import jax.numpy as jnp
import numpy as np
from jax import lax
from jax.experimental import pallas as pl
from jax.experimental.pallas import tpu as pltpu
from jax.sharding import PartitionSpec as P

ROWS = 16


def spread_table(gate_count, freq_count):
    gates = np.arange(gate_count, dtype=np.float32)
    freqs = np.arange(freq_count, dtype=np.float32)
    phases = (
        np.float32(np.pi)
        * (np.float32(2) * gates[None, :] + np.float32(1))
        * (np.float32(1) + np.float32(3) * freqs[:, None])
        / np.float32(2 * gate_count)
    )
    scale = np.sqrt(np.float32(2.0 / gate_count))
    table = np.stack([np.cos(phases) * scale, -np.sin(phases) * scale], axis=1)
    table = table.reshape(2 * freq_count, gate_count).astype(jnp.bfloat16).astype(np.float32)
    return np.kron(table, np.eye(ROWS, dtype=np.float32)).astype(jnp.bfloat16)


def spectra_kernel(table_ref, active_ref, records_ref, out_ref, mask_ref):
    gates, rows, recv = records_ref.shape
    blocks = active_ref.shape[0]
    step = pl.program_id(0)

    @pl.when(step == 0)
    def _():
        block_of = lax.broadcasted_iota(jnp.int32, (blocks, recv), 1) // (recv // blocks)
        spread = (block_of == lax.broadcasted_iota(jnp.int32, (blocks, recv), 0)).astype(jnp.float32)
        mask_ref[...] = lax.dot_general(
            active_ref[...].astype(jnp.float32),
            spread,
            (((0,), (0,)), ((), ())),
            preferred_element_type=jnp.float32,
        )

    flat = records_ref[...].reshape(gates * rows, recv)
    sums = jnp.dot(table_ref[...], flat, preferred_element_type=jnp.float32)
    mask = mask_ref[pl.ds(pl.multiple_of(step * rows, rows), rows)]
    channels = out_ref.shape[0]
    out_ref[...] = (sums.reshape(channels, rows, recv) * mask[None]).astype(out_ref.dtype)


def in_hbm(array):
    return pltpu.with_memory_space_constraint(array, pltpu.HBM)


def spectra_of(records, active, freq_count):
    gates, trans, recv = records.shape
    blocks = active.shape[1]
    channels = 2 * freq_count
    table = jnp.asarray(spread_table(gates, freq_count))
    return pl.pallas_call(
        spectra_kernel,
        grid=(trans // ROWS,),
        in_specs=[
            pl.BlockSpec(table.shape, lambda i: (0, 0)),
            pl.BlockSpec((blocks, trans), lambda i: (0, 0)),
            pl.BlockSpec((gates, ROWS, recv), lambda i: (0, i, 0)),
        ],
        out_specs=pl.BlockSpec((channels, ROWS, recv), lambda i: (0, i, 0)),
        out_shape=jax.ShapeDtypeStruct((channels, trans, recv), jnp.bfloat16),
        scratch_shapes=[pltpu.VMEM((trans, recv), jnp.float32)],
        compiler_params=pltpu.CompilerParams(vmem_limit_bytes=16 << 20),
        cost_estimate=pl.CostEstimate(
            flops=2 * channels * ROWS * gates * trans * recv,
            bytes_accessed=2 * (gates + channels) * trans * recv,
            transcendentals=0,
        ),
        name="spectra",
    )(in_hbm(table), active.T, in_hbm(records))


def adjoint_kernel(count, *refs):
    spectra_refs, green_ref, out_ref = refs[:count], refs[count], refs[-1]
    rows = spectra_refs[0].shape[2]
    real = jnp.concatenate([ref[0, 0] for ref in spectra_refs], axis=0)
    imag = jnp.concatenate([ref[0, 1] for ref in spectra_refs], axis=0)
    left = jnp.concatenate(
        [jnp.concatenate([real, -imag], axis=1), jnp.concatenate([-imag, -real], axis=1)], axis=0
    )
    sums = jnp.dot(left, green_ref[0], preferred_element_type=jnp.float32)
    out_ref[0] = sums.reshape(2, count, rows, -1)


def adjoint_of(pieces, green, base=None, groups=None):
    freqs, _, recv, cells = green.shape
    rows = pieces[0].shape[1]
    pieces = [piece.reshape(freqs, 2, rows, recv) for piece in pieces]
    count = len(pieces)
    groups = groups or count
    place = 0 if base is None else 1
    shape = (freqs, 2, groups, rows, cells)
    bases = [] if base is None else [pltpu.with_memory_space_constraint(base, pltpu.VMEM)]
    return pl.pallas_call(
        functools.partial(adjoint_kernel, count),
        grid=(freqs,),
        in_specs=[pl.BlockSpec((1, 2, rows, recv), lambda f: (f, 0, 0, 0))] * count
        + [pl.BlockSpec((1, 2 * recv, cells), lambda f: (f, 0, 0))]
        + [pl.BlockSpec(memory_space=pl.ANY)] * len(bases),
        out_specs=pl.BlockSpec((1, 2, count, rows, cells), lambda f: (f, 0, place, 0, 0)),
        out_shape=pltpu.VMEM(shape, jnp.float32),
        input_output_aliases={count + 1: 0} if bases else {},
        compiler_params=pltpu.CompilerParams(vmem_limit_bytes=20 << 20),
        cost_estimate=pl.CostEstimate(
            flops=8 * freqs * count * rows * recv * cells,
            bytes_accessed=4 * freqs * recv * cells + 8 * freqs * count * rows * cells,
            transcendentals=0,
        ),
        name="adjoint",
    )(*pieces, in_hbm(green.reshape(freqs, 2 * recv, cells)), *bases)


def in_vmem(kernel, scalars, operands, shape, dtype, name):
    return pl.pallas_call(
        kernel,
        in_specs=[pl.BlockSpec(memory_space=pltpu.SMEM)]
        + [pl.BlockSpec(memory_space=pltpu.VMEM)] * len(operands),
        out_specs=pl.BlockSpec(memory_space=pltpu.VMEM),
        out_shape=pltpu.VMEM(shape, dtype),
        compiler_params=pltpu.CompilerParams(vmem_limit_bytes=16 << 20),
        cost_estimate=pl.CostEstimate(
            flops=4 * sum(operand.size for operand in operands[1:]),
            bytes_accessed=4 * sum(operand.size for operand in operands[1:]),
            transcendentals=0,
        ),
        name=name,
    )(scalars, *[pltpu.with_memory_space_constraint(operand, pltpu.VMEM) for operand in operands])


OWN, OWN_Y, NEAR, NEAR_Y, MID, MID_Y, FAR, FAR_Y, MIDDLE = range(9)


def weigh_kernel(terms, first, last, scalar_ref, adjoint_ref, *refs):
    refs, out_ref = list(refs[:-1]), refs[-1]
    sums = 0.0 if first else refs.pop()[...]
    freqs, parts, _, cells = refs[0].shape
    middle = scalar_ref[MIDDLE] != 0
    for number, choices in terms:
        block = scalar_ref[number]
        field_refs = [refs.pop(0) for _ in range(choices)]
        extra_ref = refs.pop(0) if number == FAR_Y else None
        for freq in range(freqs):
            for part in range(parts):
                weights = adjoint_ref[freq, part, block]
                if extra_ref is not None:
                    weights = weights + extra_ref[freq, part].astype(jnp.float32)
                field = field_refs[0][freq, part].astype(jnp.float32)
                if choices == 2:
                    other = field_refs[1][freq, part].astype(jnp.float32)
                    field = jnp.where(middle, other, field)
                sums = sums + jnp.sum((weights * field).reshape(-1, 8, cells), axis=0)
    out_ref[...] = jnp.sum(sums, axis=0, keepdims=True) if last else sums


def pick_kernel(scalar_ref, first_ref, second_ref, out_ref):
    @pl.when(scalar_ref[MIDDLE] == 0)
    def _():
        out_ref[...] = first_ref[...]

    @pl.when(scalar_ref[MIDDLE] != 0)
    def _():
        out_ref[...] = second_ref[...]


def block_kernel(scalar_ref, adjoint_ref, out_ref):
    out_ref[...] = adjoint_ref[:, :, scalar_ref[FAR_Y]].astype(out_ref.dtype)


def box_shards(records, active, green, background):
    freqs, _, _, cells = green.shape
    along_y = [(r, r ^ 1) for r in range(8)]
    z_pairs = [(r, r ^ 2) for r in range(8)]
    z_middle = [(r, r ^ 6) for r in range(2, 6)]
    z_outward = [(2, 0), (3, 1), (4, 6), (5, 7)]
    z_inward = [(there, here) for here, there in z_outward]
    core = [(t, t ^ 1) for t in range(4)]
    along_x = [(t, t ^ 2) for t in range(4)]
    send, tie = lax.ppermute, lax.optimization_barrier

    me_tx, me_rx = lax.axis_index("tx"), lax.axis_index("rx")
    me_z, me_y = me_rx // 2, me_rx % 2
    lower = me_z < 2
    mid_z, far_z = jnp.where(lower, 2, 1), jnp.where(lower, 3, 0)
    scalars = jnp.stack(
        [(z ^ me_tx) * 2 + y for z in (me_z, me_z ^ 1, mid_z, far_z) for y in (me_y, 1 - me_y)]
        + [(me_z == 1) | (me_z == 2)]
    ).astype(jnp.int32)

    own = background.transpose(1, 2, 0, 3)
    own, scalars, records = tie((own, scalars, records))
    near = send(own, "rx", z_pairs)
    across = send(own, "rx", z_middle)
    own_y = send(own, "rx", along_y)

    spectra = spectra_of(records, active, freqs)
    spectra_x = send(spectra, "tx", along_x)
    spectra_core = send(spectra, "tx", core)

    near, across, own_y, spectra_core = tie((near, across, own_y, spectra_core))
    across_out = send(across, "rx", z_outward)
    far = send(near, "rx", z_middle)
    near_y = send(near, "rx", along_y)

    adjoint = adjoint_of([spectra, spectra_core], green, groups=4)
    spectra_x, adjoint = tie((spectra_x, adjoint))
    spectra_both = send(spectra_x, "tx", core)
    adjoint = adjoint_of([spectra_x, spectra_both], green, adjoint, groups=4)
    adjoint = adjoint.reshape((freqs, 2, 8) + own.shape[2:])

    partial = in_vmem(block_kernel, scalars, [adjoint], own.shape, own.dtype, "block")
    partial, far, near_y, across_out = tie((partial, far, near_y, across_out))
    partial = send(partial, "rx", z_inward)
    far_out = send(far, "rx", z_outward)
    far_both = send(near_y, "rx", z_middle)
    mid = in_vmem(pick_kernel, scalars, [across_out, across], own.shape, own.dtype, "pick")
    mid_y = send(mid, "rx", along_y)

    sums = in_vmem(
        functools.partial(weigh_kernel, ((OWN, 1), (OWN_Y, 1), (NEAR, 1), (NEAR_Y, 1), (MID, 1)), True, False),
        scalars,
        [adjoint, own, own_y, near, near_y, mid],
        (8, cells),
        jnp.float32,
        "weigh",
    )
    sums = in_vmem(
        functools.partial(weigh_kernel, ((MID_Y, 1), (FAR, 2), (FAR_Y, 1)), False, True),
        scalars,
        [adjoint, mid_y, far_out, far, far_both, partial, sums],
        (1, cells),
        jnp.float32,
        "weigh",
    )
    sums = sums.reshape(cells)
    for bit in (1, 2, 4):
        sums = sums + send(sums, "rx", [(r, r ^ bit) for r in range(8)])
    return sums


def plain_shards(records, active, green, background):
    freqs = green.shape[0]
    spectra = spectra_of(records, active, freqs)
    pieces = lax.all_gather(spectra, "tx", axis=0)
    adjoint = adjoint_of([pieces[t] for t in range(pieces.shape[0])], green)
    freqs, _, groups, rows, cells = adjoint.shape
    adjoint = adjoint.reshape(freqs, 2, groups * rows, cells)
    fields = lax.all_gather(background, "rx", axis=0, tiled=True)
    fields = fields.transpose(1, 2, 0, 3).astype(jnp.float32)
    return lax.psum(jnp.sum(adjoint * fields, axis=(0, 1, 2)), "rx")


def solution(mesh):
    placed = (
        P(None, "tx", "rx"),
        P("tx", "rx"),
        P(None, None, "rx", "tx"),
        P("rx", None, None, "tx"),
    )
    body = box_shards if (mesh.shape["tx"], mesh.shape["rx"]) == (4, 8) else plain_shards
    return jax.shard_map(body, mesh=mesh, in_specs=placed, out_specs=P("tx"), check_vma=False)
```

```python
import functools

import jax
import jax.numpy as jnp
import numpy as np
from jax import lax
from jax.experimental import pallas as pl
from jax.experimental.pallas import tpu as pltpu
from jax.sharding import PartitionSpec as P

ROWS = 16


def spread_table(gate_count, freq_count):
    gates = np.arange(gate_count, dtype=np.float32)
    freqs = np.arange(freq_count, dtype=np.float32)
    phases = (
        np.float32(np.pi)
        * (np.float32(2) * gates[None, :] + np.float32(1))
        * (np.float32(1) + np.float32(3) * freqs[:, None])
        / np.float32(2 * gate_count)
    )
    scale = np.sqrt(np.float32(2.0 / gate_count))
    table = np.stack([np.cos(phases) * scale, -np.sin(phases) * scale], axis=1)
    table = table.reshape(2 * freq_count, gate_count).astype(jnp.bfloat16).astype(np.float32)
    return np.kron(table, np.eye(ROWS, dtype=np.float32)).astype(jnp.bfloat16)


def spectra_kernel(table_ref, active_ref, records_ref, out_ref, mask_ref):
    gates, rows, recv = records_ref.shape
    blocks = active_ref.shape[0]
    step = pl.program_id(0)

    @pl.when(step == 0)
    def _():
        block_of = lax.broadcasted_iota(jnp.int32, (blocks, recv), 1) // (recv // blocks)
        spread = (block_of == lax.broadcasted_iota(jnp.int32, (blocks, recv), 0)).astype(jnp.float32)
        mask_ref[...] = lax.dot_general(
            active_ref[...].astype(jnp.float32),
            spread,
            (((0,), (0,)), ((), ())),
            preferred_element_type=jnp.float32,
        )

    flat = records_ref[...].reshape(gates * rows, recv)
    sums = jnp.dot(table_ref[...], flat, preferred_element_type=jnp.float32)
    mask = mask_ref[pl.ds(pl.multiple_of(step * rows, rows), rows)]
    channels = out_ref.shape[0]
    out_ref[...] = (sums.reshape(channels, rows, recv) * mask[None]).astype(out_ref.dtype)


def in_hbm(array):
    return pltpu.with_memory_space_constraint(array, pltpu.HBM)


def spectra_of(records, active, freq_count):
    gates, trans, recv = records.shape
    blocks = active.shape[1]
    channels = 2 * freq_count
    table = jnp.asarray(spread_table(gates, freq_count))
    return pl.pallas_call(
        spectra_kernel,
        grid=(trans // ROWS,),
        in_specs=[
            pl.BlockSpec(table.shape, lambda i: (0, 0)),
            pl.BlockSpec((blocks, trans), lambda i: (0, 0)),
            pl.BlockSpec((gates, ROWS, recv), lambda i: (0, i, 0)),
        ],
        out_specs=pl.BlockSpec((channels, ROWS, recv), lambda i: (0, i, 0)),
        out_shape=jax.ShapeDtypeStruct((channels, trans, recv), jnp.bfloat16),
        scratch_shapes=[pltpu.VMEM((trans, recv), jnp.float32)],
        compiler_params=pltpu.CompilerParams(vmem_limit_bytes=16 << 20),
        cost_estimate=pl.CostEstimate(
            flops=2 * channels * ROWS * gates * trans * recv,
            bytes_accessed=2 * (gates + channels) * trans * recv,
            transcendentals=0,
        ),
        name="spectra",
    )(in_hbm(table), in_hbm(active.T), in_hbm(records))


def adjoint_kernel(count, *refs):
    spectra_refs, green_ref, out_ref = refs[:count], refs[count], refs[-1]
    rows = spectra_refs[0].shape[2]
    real = jnp.concatenate([ref[0, 0] for ref in spectra_refs], axis=0)
    imag = jnp.concatenate([ref[0, 1] for ref in spectra_refs], axis=0)
    left = jnp.concatenate(
        [jnp.concatenate([real, -imag], axis=1), jnp.concatenate([-imag, -real], axis=1)], axis=0
    )
    sums = jnp.dot(left, green_ref[0], preferred_element_type=jnp.float32)
    out_ref[0] = sums.reshape(2, count, rows, -1)


def adjoint_of(pieces, green, base=None, groups=None):
    freqs, _, recv, cells = green.shape
    rows = pieces[0].shape[1]
    pieces = [piece.reshape(freqs, 2, rows, recv) for piece in pieces]
    count = len(pieces)
    groups = groups or count
    place = 0 if base is None else 1
    shape = (freqs, 2, groups, rows, cells)
    bases = [] if base is None else [pltpu.with_memory_space_constraint(base, pltpu.VMEM)]
    return pl.pallas_call(
        functools.partial(adjoint_kernel, count),
        grid=(freqs,),
        in_specs=[pl.BlockSpec((1, 2, rows, recv), lambda f: (f, 0, 0, 0))] * count
        + [pl.BlockSpec((1, 2 * recv, cells), lambda f: (f, 0, 0))]
        + [pl.BlockSpec(memory_space=pl.ANY)] * len(bases),
        out_specs=pl.BlockSpec((1, 2, count, rows, cells), lambda f: (f, 0, place, 0, 0)),
        out_shape=pltpu.VMEM(shape, jnp.float32),
        input_output_aliases={count + 1: 0} if bases else {},
        compiler_params=pltpu.CompilerParams(vmem_limit_bytes=20 << 20),
        cost_estimate=pl.CostEstimate(
            flops=8 * freqs * count * rows * recv * cells,
            bytes_accessed=4 * freqs * recv * cells + 8 * freqs * count * rows * cells,
            transcendentals=0,
        ),
        name="adjoint",
    )(*pieces, in_hbm(green.reshape(freqs, 2 * recv, cells)), *bases)


def in_vmem(kernel, scalars, operands, shape, dtype, name):
    return pl.pallas_call(
        kernel,
        in_specs=[pl.BlockSpec(memory_space=pltpu.SMEM)]
        + [pl.BlockSpec(memory_space=pltpu.VMEM)] * len(operands),
        out_specs=pl.BlockSpec(memory_space=pltpu.VMEM),
        out_shape=pltpu.VMEM(shape, dtype),
        compiler_params=pltpu.CompilerParams(vmem_limit_bytes=16 << 20),
        cost_estimate=pl.CostEstimate(
            flops=4 * sum(operand.size for operand in operands[1:]),
            bytes_accessed=4 * sum(operand.size for operand in operands[1:]),
            transcendentals=0,
        ),
        name=name,
    )(scalars, *[pltpu.with_memory_space_constraint(operand, pltpu.VMEM) for operand in operands])


OWN, OWN_Y, NEAR, NEAR_Y, MID, MID_Y, FAR, FAR_Y, MIDDLE = range(9)


def weigh_kernel(terms, first, last, scalar_ref, adjoint_ref, *refs):
    refs, out_ref = list(refs[:-1]), refs[-1]
    sums = 0.0 if first else refs.pop()[...]
    freqs, parts, _, cells = refs[0].shape
    middle = scalar_ref[MIDDLE] != 0
    for number, choices in terms:
        block = scalar_ref[number]
        field_refs = [refs.pop(0) for _ in range(choices)]
        extra_ref = refs.pop(0) if number == FAR_Y else None
        for freq in range(freqs):
            for part in range(parts):
                weights = adjoint_ref[freq, part, block]
                if extra_ref is not None:
                    weights = weights + extra_ref[freq, part].astype(jnp.float32)
                field = field_refs[0][freq, part].astype(jnp.float32)
                if choices == 2:
                    other = field_refs[1][freq, part].astype(jnp.float32)
                    field = jnp.where(middle, other, field)
                sums = sums + jnp.sum((weights * field).reshape(-1, 8, cells), axis=0)
    out_ref[...] = jnp.sum(sums, axis=0, keepdims=True) if last else sums


def pick_kernel(scalar_ref, first_ref, second_ref, out_ref):
    @pl.when(scalar_ref[MIDDLE] == 0)
    def _():
        out_ref[...] = first_ref[...]

    @pl.when(scalar_ref[MIDDLE] != 0)
    def _():
        out_ref[...] = second_ref[...]


def block_kernel(scalar_ref, adjoint_ref, out_ref):
    out_ref[...] = adjoint_ref[:, :, scalar_ref[FAR_Y]].astype(out_ref.dtype)


def box_shards(records, active, green, background):
    freqs, _, _, cells = green.shape
    along_y = [(r, r ^ 1) for r in range(8)]
    z_pairs = [(r, r ^ 2) for r in range(8)]
    z_middle = [(r, r ^ 6) for r in range(2, 6)]
    z_outward = [(2, 0), (3, 1), (4, 6), (5, 7)]
    z_inward = [(there, here) for here, there in z_outward]
    core = [(t, t ^ 1) for t in range(4)]
    along_x = [(t, t ^ 2) for t in range(4)]
    send, tie = lax.ppermute, lax.optimization_barrier

    me_tx, me_rx = lax.axis_index("tx"), lax.axis_index("rx")
    me_z, me_y = me_rx // 2, me_rx % 2
    lower = me_z < 2
    mid_z, far_z = jnp.where(lower, 2, 1), jnp.where(lower, 3, 0)
    scalars = jnp.stack(
        [(z ^ me_tx) * 2 + y for z in (me_z, me_z ^ 1, mid_z, far_z) for y in (me_y, 1 - me_y)]
        + [(me_z == 1) | (me_z == 2)]
    ).astype(jnp.int32)

    own = background.transpose(1, 2, 0, 3)
    own, scalars, records = tie((own, scalars, records))
    spectra = spectra_of(records, active, freqs)
    spectra_x = send(spectra, "tx", along_x)
    spectra_core = send(spectra, "tx", core)

    own, _ = tie((own, spectra))
    near = send(own, "rx", z_pairs)
    across = send(own, "rx", z_middle)
    own_y = send(own, "rx", along_y)
    adjoint = adjoint_of([spectra, spectra_core], green, groups=4)
    near, across, own_y, adjoint, spectra_x = tie((near, across, own_y, adjoint, spectra_x))

    spectra_both = send(spectra_x, "tx", core)
    across_out = send(across, "rx", z_outward)
    far = send(near, "rx", z_middle)
    near_y = send(near, "rx", along_y)

    adjoint = adjoint_of([spectra_x, spectra_both], green, adjoint, groups=4)
    adjoint = adjoint.reshape((freqs, 2, 8) + own.shape[2:])

    partial = in_vmem(block_kernel, scalars, [adjoint], own.shape, own.dtype, "block")
    partial = send(partial, "rx", z_inward)
    far_out = send(far, "rx", z_outward)
    far_both = send(near_y, "rx", z_middle)
    mid = in_vmem(pick_kernel, scalars, [across_out, across], own.shape, own.dtype, "pick")
    mid_y = send(mid, "rx", along_y)

    sums = in_vmem(
        functools.partial(weigh_kernel, ((OWN, 1), (OWN_Y, 1), (NEAR, 1), (NEAR_Y, 1), (MID, 1)), True, False),
        scalars,
        [adjoint, own, own_y, near, near_y, mid],
        (8, cells),
        jnp.float32,
        "weigh",
    )
    sums = in_vmem(
        functools.partial(weigh_kernel, ((MID_Y, 1), (FAR, 2), (FAR_Y, 1)), False, True),
        scalars,
        [adjoint, mid_y, far_out, far, far_both, partial, sums],
        (1, cells),
        jnp.float32,
        "weigh",
    )
    sums = sums.reshape(cells)
    for bit in (1, 2, 4):
        sums = sums + send(sums, "rx", [(r, r ^ bit) for r in range(8)])
    return sums


def plain_shards(records, active, green, background):
    freqs = green.shape[0]
    spectra = spectra_of(records, active, freqs)
    pieces = lax.all_gather(spectra, "tx", axis=0)
    adjoint = adjoint_of([pieces[t] for t in range(pieces.shape[0])], green)
    freqs, _, groups, rows, cells = adjoint.shape
    adjoint = adjoint.reshape(freqs, 2, groups * rows, cells)
    fields = lax.all_gather(background, "rx", axis=0, tiled=True)
    fields = fields.transpose(1, 2, 0, 3).astype(jnp.float32)
    return lax.psum(jnp.sum(adjoint * fields, axis=(0, 1, 2)), "rx")


def solution(mesh):
    placed = (
        P(None, "tx", "rx"),
        P("tx", "rx"),
        P(None, None, "rx", "tx"),
        P("rx", None, None, "tx"),
    )
    body = box_shards if (mesh.shape["tx"], mesh.shape["rx"]) == (4, 8) else plain_shards
    return jax.shard_map(body, mesh=mesh, in_specs=placed, out_specs=P("tx"), check_vma=False)
```

```python
import functools

import jax
import jax.numpy as jnp
import numpy as np
from jax import lax
from jax.experimental import pallas as pl
from jax.experimental.pallas import tpu as pltpu
from jax.sharding import PartitionSpec as P

ROWS = 16


def spread_table(gate_count, freq_count):
    gates = np.arange(gate_count, dtype=np.float32)
    freqs = np.arange(freq_count, dtype=np.float32)
    phases = (
        np.float32(np.pi)
        * (np.float32(2) * gates[None, :] + np.float32(1))
        * (np.float32(1) + np.float32(3) * freqs[:, None])
        / np.float32(2 * gate_count)
    )
    scale = np.sqrt(np.float32(2.0 / gate_count))
    table = np.stack([np.cos(phases) * scale, -np.sin(phases) * scale], axis=1)
    table = table.reshape(2 * freq_count, gate_count).astype(jnp.bfloat16).astype(np.float32)
    return np.kron(table, np.eye(ROWS, dtype=np.float32)).astype(jnp.bfloat16)


def spectra_kernel(table_ref, active_ref, records_ref, out_ref, mask_ref):
    gates, rows, recv = records_ref.shape
    blocks = active_ref.shape[0]
    step = pl.program_id(0)

    @pl.when(step == 0)
    def _():
        block_of = lax.broadcasted_iota(jnp.int32, (blocks, recv), 1) // (recv // blocks)
        spread = (block_of == lax.broadcasted_iota(jnp.int32, (blocks, recv), 0)).astype(jnp.float32)
        mask_ref[...] = lax.dot_general(
            active_ref[...].astype(jnp.float32),
            spread,
            (((0,), (0,)), ((), ())),
            preferred_element_type=jnp.float32,
        )

    flat = records_ref[...].reshape(gates * rows, recv)
    sums = jnp.dot(table_ref[...], flat, preferred_element_type=jnp.float32)
    mask = mask_ref[pl.ds(pl.multiple_of(step * rows, rows), rows)]
    channels = out_ref.shape[0]
    out_ref[...] = (sums.reshape(channels, rows, recv) * mask[None]).astype(out_ref.dtype)


def in_hbm(array):
    return pltpu.with_memory_space_constraint(array, pltpu.HBM)


def spectra_of(records, active, freq_count):
    gates, trans, recv = records.shape
    blocks = active.shape[1]
    channels = 2 * freq_count
    table = jnp.asarray(spread_table(gates, freq_count))
    return pl.pallas_call(
        spectra_kernel,
        grid=(trans // ROWS,),
        in_specs=[
            pl.BlockSpec(table.shape, lambda i: (0, 0)),
            pl.BlockSpec((blocks, trans), lambda i: (0, 0)),
            pl.BlockSpec((gates, ROWS, recv), lambda i: (0, i, 0)),
        ],
        out_specs=pl.BlockSpec((channels, ROWS, recv), lambda i: (0, i, 0)),
        out_shape=jax.ShapeDtypeStruct((channels, trans, recv), jnp.bfloat16),
        scratch_shapes=[pltpu.VMEM((trans, recv), jnp.float32)],
        compiler_params=pltpu.CompilerParams(vmem_limit_bytes=16 << 20),
        cost_estimate=pl.CostEstimate(
            flops=2 * channels * ROWS * gates * trans * recv,
            bytes_accessed=2 * (gates + channels) * trans * recv,
            transcendentals=0,
        ),
        name="spectra",
    )(in_hbm(table), in_hbm(active.T), in_hbm(records))


def complex_rows(spectra_refs, freq):
    real = jnp.concatenate([ref[freq, 0] for ref in spectra_refs], axis=0)
    imag = jnp.concatenate([ref[freq, 1] for ref in spectra_refs], axis=0)
    return jnp.concatenate(
        [jnp.concatenate([real, -imag], axis=1), jnp.concatenate([-imag, -real], axis=1)], axis=0
    )


def adjoint_kernel(count, green_hbm_ref, *refs):
    spectra_refs, (out_ref, green_ref, arrived) = refs[:count], refs[count:]
    freqs, _, rows, _ = spectra_refs[0].shape

    def fetch(freq):
        return pltpu.make_async_copy(green_hbm_ref.at[freq], green_ref.at[freq], arrived.at[freq])

    for freq in range(freqs):
        fetch(freq).start()

    @pl.loop(0, freqs)
    def _(freq):
        fetch(freq).wait()
        left = complex_rows(spectra_refs, freq)
        sums = jnp.dot(left, green_ref[freq], preferred_element_type=jnp.float32)
        out_ref[freq, :, :count] = sums.reshape(2, count, rows, -1)


def adjoint_rest_kernel(count, half, scalar_ref, green_ref, base_ref, *refs):
    spectra_refs, (out_ref, block_ref) = refs[:count], refs[count:]
    del base_ref
    freqs, _, rows, _ = spectra_refs[0].shape
    block = scalar_ref[FAR_Y]
    group, first = block // 2, pl.multiple_of((block % 2) * half, half)

    @pl.loop(0, freqs)
    def _(freq):
        left = complex_rows(spectra_refs, freq)
        sums = jnp.dot(left, green_ref[freq], preferred_element_type=jnp.float32)
        out_ref[freq, :, count:] = sums.reshape(2, count, rows, -1)
        block_ref[freq] = out_ref[freq, :, group, pl.ds(first, half)].astype(block_ref.dtype)


def in_vmem_all(arrays):
    return [pltpu.with_memory_space_constraint(array, pltpu.VMEM) for array in arrays]


def adjoint_of(pieces, green, groups):
    freqs, _, recv, cells = green.shape
    rows, count = pieces[0].shape[1], len(pieces)
    green = green.reshape(freqs, 2 * recv, cells)
    return pl.pallas_call(
        functools.partial(adjoint_kernel, count),
        in_specs=[pl.BlockSpec(memory_space=pltpu.HBM)]
        + [pl.BlockSpec(memory_space=pltpu.VMEM)] * count,
        out_specs=[pl.BlockSpec(memory_space=pltpu.VMEM)] * 2,
        out_shape=[
            pltpu.VMEM((freqs, 2, groups, rows, cells), jnp.float32),
            pltpu.VMEM(green.shape, green.dtype),
        ],
        scratch_shapes=[pltpu.SemaphoreType.DMA((freqs,))],
        compiler_params=pltpu.CompilerParams(vmem_limit_bytes=4 * count << 20),
        cost_estimate=pl.CostEstimate(
            flops=8 * freqs * count * rows * recv * cells,
            bytes_accessed=4 * freqs * recv * cells,
            transcendentals=0,
        ),
        name="adjoint",
    )(in_hbm(green), *in_vmem_all([piece.reshape(freqs, 2, rows, recv) for piece in pieces]))


def adjoint_rest(scalars, pieces, green, base):
    freqs, _, groups, rows, cells = base.shape
    recv, count = pieces[0].shape[2], len(pieces)
    half = rows // 2
    pieces = [piece.reshape(freqs, 2, rows, recv) for piece in pieces]
    return pl.pallas_call(
        functools.partial(adjoint_rest_kernel, count, half),
        in_specs=[pl.BlockSpec(memory_space=pltpu.SMEM)]
        + [pl.BlockSpec(memory_space=pltpu.VMEM)] * (count + 2),
        out_specs=[pl.BlockSpec(memory_space=pltpu.VMEM)] * 2,
        out_shape=[
            pltpu.VMEM(base.shape, base.dtype),
            pltpu.VMEM((freqs, 2, half, cells), jnp.bfloat16),
        ],
        input_output_aliases={2: 0},
        compiler_params=pltpu.CompilerParams(vmem_limit_bytes=8 << 20),
        cost_estimate=pl.CostEstimate(
            flops=8 * freqs * count * rows * recv * cells,
            bytes_accessed=4 * freqs * recv * cells,
            transcendentals=0,
        ),
        name="adjoint_rest",
    )(scalars, *in_vmem_all([green, base, *pieces]))


def in_vmem(kernel, scalars, operands, shape, dtype, name):
    return pl.pallas_call(
        kernel,
        in_specs=[pl.BlockSpec(memory_space=pltpu.SMEM)]
        + [pl.BlockSpec(memory_space=pltpu.VMEM)] * len(operands),
        out_specs=pl.BlockSpec(memory_space=pltpu.VMEM),
        out_shape=pltpu.VMEM(shape, dtype),
        compiler_params=pltpu.CompilerParams(vmem_limit_bytes=4 << 20),
        cost_estimate=pl.CostEstimate(
            flops=4 * sum(operand.size for operand in operands[1:]),
            bytes_accessed=4 * sum(operand.size for operand in operands[1:]),
            transcendentals=0,
        ),
        name=name,
    )(scalars, *in_vmem_all(operands))


OWN, OWN_Y, NEAR, NEAR_Y, MID, MID_Y, FAR, FAR_Y, MIDDLE = range(9)


def weigh_kernel(terms, first, last, scalar_ref, adjoint_ref, *refs):
    refs, out_ref = list(refs[:-1]), refs[-1]
    sums = 0.0 if first else refs.pop()[...]
    freqs, parts, _, cells = refs[0].shape
    middle = scalar_ref[MIDDLE] != 0
    for number, choices in terms:
        block = scalar_ref[number]
        field_refs = [refs.pop(0) for _ in range(choices)]
        extra_ref = refs.pop(0) if number == FAR_Y else None
        for freq in range(freqs):
            for part in range(parts):
                weights = adjoint_ref[freq, part, block]
                if extra_ref is not None:
                    weights = weights + extra_ref[freq, part].astype(jnp.float32)
                field = field_refs[0][freq, part].astype(jnp.float32)
                if choices == 2:
                    other = field_refs[1][freq, part].astype(jnp.float32)
                    field = jnp.where(middle, other, field)
                sums = sums + jnp.sum((weights * field).reshape(-1, 8, cells), axis=0)
    out_ref[...] = jnp.sum(sums, axis=0, keepdims=True) if last else sums


def pick_kernel(scalar_ref, first_ref, second_ref, out_ref):
    @pl.when(scalar_ref[MIDDLE] == 0)
    def _():
        out_ref[...] = first_ref[...]

    @pl.when(scalar_ref[MIDDLE] != 0)
    def _():
        out_ref[...] = second_ref[...]


def box_shards(records, active, green, background):
    freqs, _, _, cells = green.shape
    along_y = [(r, r ^ 1) for r in range(8)]
    z_pairs = [(r, r ^ 2) for r in range(8)]
    z_middle = [(r, r ^ 6) for r in range(2, 6)]
    z_outward = [(2, 0), (3, 1), (4, 6), (5, 7)]
    z_inward = [(there, here) for here, there in z_outward]
    core = [(t, t ^ 1) for t in range(4)]
    along_x = [(t, t ^ 2) for t in range(4)]
    along_both = [(t, t ^ 3) for t in range(4)]
    send, tie = lax.ppermute, lax.optimization_barrier

    me_tx, me_rx = lax.axis_index("tx"), lax.axis_index("rx")
    me_z, me_y = me_rx // 2, me_rx % 2
    lower = me_z < 2
    mid_z, far_z = jnp.where(lower, 2, 1), jnp.where(lower, 3, 0)
    scalars = jnp.stack(
        [(z ^ me_tx) * 2 + y for z in (me_z, me_z ^ 1, mid_z, far_z) for y in (me_y, 1 - me_y)]
        + [(me_z == 1) | (me_z == 2)]
    ).astype(jnp.int32)

    own = background.transpose(1, 2, 0, 3)
    own, scalars, records = tie((own, scalars, records))
    near = send(own, "rx", z_pairs)
    across = send(own, "rx", z_middle)
    own_y = send(own, "rx", along_y)

    spectra = spectra_of(records, active, freqs)
    spectra_x = send(spectra, "tx", along_x)
    spectra_core = send(spectra, "tx", core)
    spectra_both = send(spectra, "tx", along_both)
    adjoint, green_kept = adjoint_of([spectra, spectra_core], green, 4)
    near, across, own_y, adjoint = tie((near, across, own_y, adjoint))

    across_out = send(across, "rx", z_outward)
    far = send(near, "rx", z_middle)
    near_y = send(near, "rx", along_y)

    adjoint, partial = adjoint_rest(scalars, [spectra_x, spectra_both], green_kept, adjoint)
    adjoint = adjoint.reshape((freqs, 2, 8) + own.shape[2:])

    partial = send(partial, "rx", z_inward)
    far_out = send(far, "rx", z_outward)
    far_both = send(near_y, "rx", z_middle)
    mid = in_vmem(pick_kernel, scalars, [across_out, across], own.shape, own.dtype, "pick")
    mid_y = send(mid, "rx", along_y)

    sums = in_vmem(
        functools.partial(weigh_kernel, ((OWN, 1), (OWN_Y, 1), (NEAR, 1), (NEAR_Y, 1), (MID, 1)), True, False),
        scalars,
        [adjoint, own, own_y, near, near_y, mid],
        (8, cells),
        jnp.float32,
        "weigh",
    )
    sums = in_vmem(
        functools.partial(weigh_kernel, ((MID_Y, 1), (FAR, 2), (FAR_Y, 1)), False, True),
        scalars,
        [adjoint, mid_y, far_out, far, far_both, partial, sums],
        (1, cells),
        jnp.float32,
        "weigh",
    )
    sums = sums.reshape(cells)
    for bit in (1, 2, 4):
        sums = sums + send(sums, "rx", [(r, r ^ bit) for r in range(8)])
    return sums


def plain_shards(records, active, green, background):
    freqs = green.shape[0]
    spectra = spectra_of(records, active, freqs)
    pieces = lax.all_gather(spectra, "tx", axis=0)
    adjoint, _ = adjoint_of([pieces[t] for t in range(pieces.shape[0])], green, pieces.shape[0])
    freqs, _, groups, rows, cells = adjoint.shape
    adjoint = adjoint.reshape(freqs, 2, groups * rows, cells)
    fields = lax.all_gather(background, "rx", axis=0, tiled=True)
    fields = fields.transpose(1, 2, 0, 3).astype(jnp.float32)
    return lax.psum(jnp.sum(adjoint * fields, axis=(0, 1, 2)), "rx")


def solution(mesh):
    placed = (
        P(None, "tx", "rx"),
        P("tx", "rx"),
        P(None, None, "rx", "tx"),
        P("rx", None, None, "tx"),
    )
    body = box_shards if (mesh.shape["tx"], mesh.shape["rx"]) == (4, 8) else plain_shards
    return jax.shard_map(body, mesh=mesh, in_specs=placed, out_specs=P("tx"), check_vma=False)
```

```python
import functools

import jax
import jax.numpy as jnp
import numpy as np
from jax import lax
from jax.experimental import pallas as pl
from jax.experimental.pallas import tpu as pltpu
from jax.sharding import PartitionSpec as P

ROWS = 16


def spread_table(gate_count, freq_count):
    gates = np.arange(gate_count, dtype=np.float32)
    freqs = np.arange(freq_count, dtype=np.float32)
    phases = (
        np.float32(np.pi)
        * (np.float32(2) * gates[None, :] + np.float32(1))
        * (np.float32(1) + np.float32(3) * freqs[:, None])
        / np.float32(2 * gate_count)
    )
    scale = np.sqrt(np.float32(2.0 / gate_count))
    table = np.stack([np.cos(phases) * scale, -np.sin(phases) * scale], axis=1)
    table = table.reshape(2 * freq_count, gate_count).astype(jnp.bfloat16).astype(np.float32)
    return np.kron(table, np.eye(ROWS, dtype=np.float32)).astype(jnp.bfloat16)


def spectra_kernel(table_hbm, active_hbm, records_hbm, out_ref, table_ref, active_ref, records_ref, mask_ref, arrived):
    gates, trans, recv = records_ref.shape
    blocks, channels = active_ref.shape[0], out_ref.shape[0]
    steps = trans // ROWS

    def rows(step):
        return pl.ds(pl.multiple_of(step * ROWS, ROWS), ROWS)

    def fetch(step):
        return pltpu.make_async_copy(
            records_hbm.at[:, rows(step)], records_ref.at[:, rows(step)], arrived.at[step]
        )

    fetch_active = pltpu.make_async_copy(active_hbm, active_ref, arrived.at[steps])
    fetch_table = pltpu.make_async_copy(table_hbm, table_ref, arrived.at[steps + 1])
    fetch_active.start()
    fetch_table.start()
    for step in range(steps):
        fetch(step).start()

    fetch_active.wait()
    block_of = lax.broadcasted_iota(jnp.int32, (blocks, recv), 1) // (recv // blocks)
    spread = (block_of == lax.broadcasted_iota(jnp.int32, (blocks, recv), 0)).astype(jnp.float32)
    mask_ref[...] = lax.dot_general(
        active_ref[...].astype(jnp.float32),
        spread,
        (((0,), (0,)), ((), ())),
        preferred_element_type=jnp.float32,
    )
    fetch_table.wait()

    @pl.loop(0, steps)
    def _(step):
        fetch(step).wait()
        flat = records_ref[:, rows(step)].reshape(gates * ROWS, recv)
        sums = jnp.dot(table_ref[...], flat, preferred_element_type=jnp.float32)
        masked = sums.reshape(channels, ROWS, recv) * mask_ref[rows(step)][None]
        out_ref[:, rows(step)] = masked.astype(out_ref.dtype)


def in_hbm(array):
    return pltpu.with_memory_space_constraint(array, pltpu.HBM)


def spectra_of(records, active, freq_count):
    gates, trans, recv = records.shape
    blocks = active.shape[1]
    channels = 2 * freq_count
    table = jnp.asarray(spread_table(gates, freq_count))
    return pl.pallas_call(
        spectra_kernel,
        in_specs=[pl.BlockSpec(memory_space=pltpu.HBM)] * 3,
        out_specs=pl.BlockSpec(memory_space=pltpu.VMEM),
        out_shape=pltpu.VMEM((channels, trans, recv), jnp.bfloat16),
        scratch_shapes=[
            pltpu.VMEM(table.shape, table.dtype),
            pltpu.VMEM((blocks, trans), jnp.int32),
            pltpu.VMEM(records.shape, records.dtype),
            pltpu.VMEM((trans, recv), jnp.float32),
            pltpu.SemaphoreType.DMA((trans // ROWS + 2,)),
        ],
        compiler_params=pltpu.CompilerParams(vmem_limit_bytes=16 << 20),
        cost_estimate=pl.CostEstimate(
            flops=2 * channels * ROWS * gates * trans * recv,
            bytes_accessed=2 * (gates + channels) * trans * recv,
            transcendentals=0,
        ),
        name="spectra",
    )(in_hbm(table), in_hbm(active.T), in_hbm(records))


def complex_rows(spectra_refs, freq):
    real = jnp.concatenate([ref[freq, 0] for ref in spectra_refs], axis=0)
    imag = jnp.concatenate([ref[freq, 1] for ref in spectra_refs], axis=0)
    return jnp.concatenate(
        [jnp.concatenate([real, -imag], axis=1), jnp.concatenate([-imag, -real], axis=1)], axis=0
    )


def adjoint_kernel(count, half, scalar_ref, green_hbm, *refs):
    spectra_refs, (out_ref, block_ref, green_ref, arrived) = refs[:count], refs[count:]
    freqs, _, rows, _ = spectra_refs[0].shape
    block = scalar_ref[FAR_Y]
    group, first = block // 2, pl.multiple_of((block % 2) * half, half)

    def fetch(freq):
        return pltpu.make_async_copy(green_hbm.at[freq], green_ref.at[freq], arrived.at[freq])

    for freq in range(freqs):
        fetch(freq).start()

    @pl.loop(0, freqs)
    def _(freq):
        fetch(freq).wait()
        left = complex_rows(spectra_refs, freq)
        sums = jnp.dot(left, green_ref[freq], preferred_element_type=jnp.float32)
        out_ref[freq] = sums.reshape(2, count, rows, -1)
        block_ref[freq] = out_ref[freq, :, group, pl.ds(first, half)].astype(block_ref.dtype)


def in_vmem_all(arrays):
    return [pltpu.with_memory_space_constraint(array, pltpu.VMEM) for array in arrays]


def adjoint_of(scalars, pieces, green):
    freqs, _, recv, cells = green.shape
    rows, count = pieces[0].shape[1], len(pieces)
    half = rows // 2
    green = green.reshape(freqs, 2 * recv, cells)
    return pl.pallas_call(
        functools.partial(adjoint_kernel, count, half),
        in_specs=[pl.BlockSpec(memory_space=pltpu.SMEM), pl.BlockSpec(memory_space=pltpu.HBM)]
        + [pl.BlockSpec(memory_space=pltpu.VMEM)] * count,
        out_specs=[pl.BlockSpec(memory_space=pltpu.VMEM)] * 2,
        out_shape=[
            pltpu.VMEM((freqs, 2, count, rows, cells), jnp.float32),
            pltpu.VMEM((freqs, 2, half, cells), jnp.bfloat16),
        ],
        scratch_shapes=[pltpu.VMEM(green.shape, green.dtype), pltpu.SemaphoreType.DMA((freqs,))],
        compiler_params=pltpu.CompilerParams(vmem_limit_bytes=24 << 20),
        cost_estimate=pl.CostEstimate(
            flops=8 * freqs * count * rows * recv * cells,
            bytes_accessed=4 * freqs * recv * cells,
            transcendentals=0,
        ),
        name="adjoint",
    )(scalars, in_hbm(green), *in_vmem_all([piece.reshape(freqs, 2, rows, recv) for piece in pieces]))


def in_vmem(kernel, scalars, operands, shape, dtype, name):
    return pl.pallas_call(
        kernel,
        in_specs=[pl.BlockSpec(memory_space=pltpu.SMEM)]
        + [pl.BlockSpec(memory_space=pltpu.VMEM)] * len(operands),
        out_specs=pl.BlockSpec(memory_space=pltpu.VMEM),
        out_shape=pltpu.VMEM(shape, dtype),
        compiler_params=pltpu.CompilerParams(vmem_limit_bytes=4 << 20),
        cost_estimate=pl.CostEstimate(
            flops=4 * sum(operand.size for operand in operands[1:]),
            bytes_accessed=4 * sum(operand.size for operand in operands[1:]),
            transcendentals=0,
        ),
        name=name,
    )(scalars, *in_vmem_all(operands))


OWN, OWN_Y, NEAR, NEAR_Y, MID, MID_Y, FAR, FAR_Y, MIDDLE = range(9)


def weigh_kernel(terms, first, last, scalar_ref, adjoint_ref, *refs):
    refs, out_ref = list(refs[:-1]), refs[-1]
    sums = 0.0 if first else refs.pop()[...]
    freqs, parts, _, cells = refs[0].shape
    middle = scalar_ref[MIDDLE] != 0
    for number, choices in terms:
        block = scalar_ref[number]
        field_refs = [refs.pop(0) for _ in range(choices)]
        extra_ref = refs.pop(0) if number == FAR_Y else None
        for freq in range(freqs):
            for part in range(parts):
                weights = adjoint_ref[freq, part, block]
                if extra_ref is not None:
                    weights = weights + extra_ref[freq, part].astype(jnp.float32)
                field = field_refs[0][freq, part].astype(jnp.float32)
                if choices == 2:
                    other = field_refs[1][freq, part].astype(jnp.float32)
                    field = jnp.where(middle, other, field)
                sums = sums + jnp.sum((weights * field).reshape(-1, 8, cells), axis=0)
    out_ref[...] = jnp.sum(sums, axis=0, keepdims=True) if last else sums


def pick_kernel(scalar_ref, first_ref, second_ref, out_ref):
    @pl.when(scalar_ref[MIDDLE] == 0)
    def _():
        out_ref[...] = first_ref[...]

    @pl.when(scalar_ref[MIDDLE] != 0)
    def _():
        out_ref[...] = second_ref[...]


def box_shards(records, active, green, background):
    freqs, _, _, cells = green.shape
    along_y = [(r, r ^ 1) for r in range(8)]
    z_pairs = [(r, r ^ 2) for r in range(8)]
    z_middle = [(r, r ^ 6) for r in range(2, 6)]
    z_outward = [(2, 0), (3, 1), (4, 6), (5, 7)]
    z_inward = [(there, here) for here, there in z_outward]
    core = [(t, t ^ 1) for t in range(4)]
    along_x = [(t, t ^ 2) for t in range(4)]
    send, tie = lax.ppermute, lax.optimization_barrier

    me_tx, me_rx = lax.axis_index("tx"), lax.axis_index("rx")
    me_z, me_y = me_rx // 2, me_rx % 2
    lower = me_z < 2
    mid_z, far_z = jnp.where(lower, 2, 1), jnp.where(lower, 3, 0)
    scalars = jnp.stack(
        [(z ^ me_tx) * 2 + y for z in (me_z, me_z ^ 1, mid_z, far_z) for y in (me_y, 1 - me_y)]
        + [(me_z == 1) | (me_z == 2)]
    ).astype(jnp.int32)

    own = background.transpose(1, 2, 0, 3)
    own, scalars, records = tie((own, scalars, records))
    spectra = spectra_of(records, active, freqs)
    spectra_x = send(spectra, "tx", along_x)
    spectra_core = send(spectra, "tx", core)
    spectra_both = send(spectra_x, "tx", core)

    own, _ = tie((own, spectra))
    near = send(own, "rx", z_pairs)
    across = send(own, "rx", z_middle)
    own_y = send(own, "rx", along_y)
    near, across, own_y, spectra_core = tie((near, across, own_y, spectra_core))

    across_out = send(across, "rx", z_outward)
    far = send(near, "rx", z_middle)
    near_y = send(near, "rx", along_y)

    adjoint, partial = adjoint_of(scalars, [spectra, spectra_core, spectra_x, spectra_both], green)
    across_out, partial = tie((across_out, partial))
    adjoint = adjoint.reshape((freqs, 2, 8) + own.shape[2:])

    partial = send(partial, "rx", z_inward)
    far_out = send(far, "rx", z_outward)
    far_both = send(near_y, "rx", z_middle)
    mid = in_vmem(pick_kernel, scalars, [across_out, across], own.shape, own.dtype, "pick")
    mid_y = send(mid, "rx", along_y)

    sums = in_vmem(
        functools.partial(weigh_kernel, ((OWN, 1), (OWN_Y, 1), (NEAR, 1), (NEAR_Y, 1), (MID, 1)), True, False),
        scalars,
        [adjoint, own, own_y, near, near_y, mid],
        (8, cells),
        jnp.float32,
        "weigh",
    )
    sums = in_vmem(
        functools.partial(weigh_kernel, ((MID_Y, 1), (FAR, 2), (FAR_Y, 1)), False, True),
        scalars,
        [adjoint, mid_y, far_out, far, far_both, partial, sums],
        (1, cells),
        jnp.float32,
        "weigh",
    )
    sums = sums.reshape(cells)
    for bit in (1, 2, 4):
        sums = sums + send(sums, "rx", [(r, r ^ bit) for r in range(8)])
    return sums


def plain_shards(records, active, green, background):
    freqs = green.shape[0]
    spectra = spectra_of(records, active, freqs)
    pieces = lax.all_gather(spectra, "tx", axis=0)
    scalars = jnp.zeros(MIDDLE + 1, jnp.int32)
    adjoint, _ = adjoint_of(scalars, [pieces[t] for t in range(pieces.shape[0])], green)
    freqs, _, groups, rows, cells = adjoint.shape
    adjoint = adjoint.reshape(freqs, 2, groups * rows, cells)
    fields = lax.all_gather(background, "rx", axis=0, tiled=True)
    fields = fields.transpose(1, 2, 0, 3).astype(jnp.float32)
    return lax.psum(jnp.sum(adjoint * fields, axis=(0, 1, 2)), "rx")


def solution(mesh):
    placed = (
        P(None, "tx", "rx"),
        P("tx", "rx"),
        P(None, None, "rx", "tx"),
        P("rx", None, None, "tx"),
    )
    body = box_shards if (mesh.shape["tx"], mesh.shape["rx"]) == (4, 8) else plain_shards
    return jax.shard_map(body, mesh=mesh, in_specs=placed, out_specs=P("tx"), check_vma=False)
```

```python
import functools

import jax
import jax.numpy as jnp
import numpy as np
from jax import lax
from jax.experimental import pallas as pl
from jax.experimental.pallas import tpu as pltpu
from jax.sharding import PartitionSpec as P

ROWS = 16


def spread_table(gate_count, freq_count):
    gates = np.arange(gate_count, dtype=np.float32)
    freqs = np.arange(freq_count, dtype=np.float32)
    phases = (
        np.float32(np.pi)
        * (np.float32(2) * gates[None, :] + np.float32(1))
        * (np.float32(1) + np.float32(3) * freqs[:, None])
        / np.float32(2 * gate_count)
    )
    scale = np.sqrt(np.float32(2.0 / gate_count))
    table = np.stack([np.cos(phases) * scale, -np.sin(phases) * scale], axis=1)
    table = table.reshape(2 * freq_count, gate_count).astype(jnp.bfloat16).astype(np.float32)
    return np.kron(table, np.eye(ROWS, dtype=np.float32)).astype(jnp.bfloat16)


def spectra_kernel(table_hbm, active_hbm, records_hbm, out_ref, table_ref, active_ref, records_ref, mask_ref, arrived):
    gates, trans, recv = records_ref.shape
    blocks, channels = active_ref.shape[0], out_ref.shape[0]
    steps = trans // ROWS

    def rows(step):
        return pl.ds(pl.multiple_of(step * ROWS, ROWS), ROWS)

    def fetch(step):
        return pltpu.make_async_copy(
            records_hbm.at[:, rows(step)], records_ref.at[:, rows(step)], arrived.at[step]
        )

    fetch_active = pltpu.make_async_copy(active_hbm, active_ref, arrived.at[steps])
    fetch_table = pltpu.make_async_copy(table_hbm, table_ref, arrived.at[steps + 1])
    fetch_active.start()
    fetch_table.start()
    for step in range(steps):
        fetch(step).start()

    fetch_active.wait()
    block_of = lax.broadcasted_iota(jnp.int32, (blocks, recv), 1) // (recv // blocks)
    spread = (block_of == lax.broadcasted_iota(jnp.int32, (blocks, recv), 0)).astype(jnp.float32)
    mask_ref[...] = lax.dot_general(
        active_ref[...].astype(jnp.float32),
        spread,
        (((0,), (0,)), ((), ())),
        preferred_element_type=jnp.float32,
    )
    fetch_table.wait()

    @pl.loop(0, steps)
    def _(step):
        fetch(step).wait()
        flat = records_ref[:, rows(step)].reshape(gates * ROWS, recv)
        sums = jnp.dot(table_ref[...], flat, preferred_element_type=jnp.float32)
        masked = sums.reshape(channels, ROWS, recv) * mask_ref[rows(step)][None]
        out_ref[:, rows(step)] = masked.astype(out_ref.dtype)


def in_hbm(array):
    return pltpu.with_memory_space_constraint(array, pltpu.HBM)


def spectra_of(records, active, freq_count):
    gates, trans, recv = records.shape
    blocks = active.shape[1]
    channels = 2 * freq_count
    table = jnp.asarray(spread_table(gates, freq_count))
    return pl.pallas_call(
        spectra_kernel,
        in_specs=[pl.BlockSpec(memory_space=pltpu.HBM)] * 3,
        out_specs=pl.BlockSpec(memory_space=pltpu.VMEM),
        out_shape=pltpu.VMEM((channels, trans, recv), jnp.bfloat16),
        scratch_shapes=[
            pltpu.VMEM(table.shape, table.dtype),
            pltpu.VMEM((blocks, trans), jnp.int32),
            pltpu.VMEM(records.shape, records.dtype),
            pltpu.VMEM((trans, recv), jnp.float32),
            pltpu.SemaphoreType.DMA((trans // ROWS + 2,)),
        ],
        compiler_params=pltpu.CompilerParams(vmem_limit_bytes=16 << 20),
        cost_estimate=pl.CostEstimate(
            flops=2 * channels * ROWS * gates * trans * recv,
            bytes_accessed=2 * (gates + channels) * trans * recv,
            transcendentals=0,
        ),
        name="spectra",
    )(in_hbm(table), in_hbm(active.T), in_hbm(records))


def complex_rows(spectra_refs, freq):
    real = jnp.concatenate([ref[freq, 0] for ref in spectra_refs], axis=0)
    imag = jnp.concatenate([ref[freq, 1] for ref in spectra_refs], axis=0)
    return jnp.concatenate(
        [jnp.concatenate([real, -imag], axis=1), jnp.concatenate([-imag, -real], axis=1)], axis=0
    )


def adjoint_kernel(count, green_hbm_ref, *refs):
    spectra_refs, (out_ref, green_ref, arrived) = refs[:count], refs[count:]
    freqs, _, rows, _ = spectra_refs[0].shape

    def fetch(freq):
        return pltpu.make_async_copy(green_hbm_ref.at[freq], green_ref.at[freq], arrived.at[freq])

    for freq in range(freqs):
        fetch(freq).start()

    @pl.loop(0, freqs)
    def _(freq):
        fetch(freq).wait()
        left = complex_rows(spectra_refs, freq)
        sums = jnp.dot(left, green_ref[freq], preferred_element_type=jnp.float32)
        out_ref[freq, :, :count] = sums.reshape(2, count, rows, -1)


def adjoint_rest_kernel(count, half, scalar_ref, green_ref, base_ref, *refs):
    spectra_refs, (out_ref, block_ref) = refs[:count], refs[count:]
    del base_ref
    freqs, _, rows, _ = spectra_refs[0].shape
    block = scalar_ref[FAR_Y]
    group, first = block // 2, pl.multiple_of((block % 2) * half, half)

    @pl.loop(0, freqs)
    def _(freq):
        left = complex_rows(spectra_refs, freq)
        sums = jnp.dot(left, green_ref[freq], preferred_element_type=jnp.float32)
        out_ref[freq, :, count:] = sums.reshape(2, count, rows, -1)
        block_ref[freq] = out_ref[freq, :, group, pl.ds(first, half)].astype(block_ref.dtype)


def in_vmem_all(arrays):
    return [pltpu.with_memory_space_constraint(array, pltpu.VMEM) for array in arrays]


def adjoint_of(pieces, green, groups):
    freqs, _, recv, cells = green.shape
    rows, count = pieces[0].shape[1], len(pieces)
    green = green.reshape(freqs, 2 * recv, cells)
    return pl.pallas_call(
        functools.partial(adjoint_kernel, count),
        in_specs=[pl.BlockSpec(memory_space=pltpu.HBM)]
        + [pl.BlockSpec(memory_space=pltpu.VMEM)] * count,
        out_specs=[pl.BlockSpec(memory_space=pltpu.VMEM)] * 2,
        out_shape=[
            pltpu.VMEM((freqs, 2, groups, rows, cells), jnp.float32),
            pltpu.VMEM(green.shape, green.dtype),
        ],
        scratch_shapes=[pltpu.SemaphoreType.DMA((freqs,))],
        compiler_params=pltpu.CompilerParams(vmem_limit_bytes=4 * count << 20),
        cost_estimate=pl.CostEstimate(
            flops=8 * freqs * count * rows * recv * cells,
            bytes_accessed=4 * freqs * recv * cells,
            transcendentals=0,
        ),
        name="adjoint",
    )(in_hbm(green), *in_vmem_all([piece.reshape(freqs, 2, rows, recv) for piece in pieces]))


def adjoint_rest(scalars, pieces, green, base):
    freqs, _, groups, rows, cells = base.shape
    recv, count = pieces[0].shape[2], len(pieces)
    half = rows // 2
    pieces = [piece.reshape(freqs, 2, rows, recv) for piece in pieces]
    return pl.pallas_call(
        functools.partial(adjoint_rest_kernel, count, half),
        in_specs=[pl.BlockSpec(memory_space=pltpu.SMEM)]
        + [pl.BlockSpec(memory_space=pltpu.VMEM)] * (count + 2),
        out_specs=[pl.BlockSpec(memory_space=pltpu.VMEM)] * 2,
        out_shape=[
            pltpu.VMEM(base.shape, base.dtype),
            pltpu.VMEM((freqs, 2, half, cells), jnp.bfloat16),
        ],
        input_output_aliases={2: 0},
        compiler_params=pltpu.CompilerParams(vmem_limit_bytes=8 << 20),
        cost_estimate=pl.CostEstimate(
            flops=8 * freqs * count * rows * recv * cells,
            bytes_accessed=4 * freqs * recv * cells,
            transcendentals=0,
        ),
        name="adjoint_rest",
    )(scalars, *in_vmem_all([green, base, *pieces]))


def in_vmem(kernel, scalars, operands, shape, dtype, name):
    return pl.pallas_call(
        kernel,
        in_specs=[pl.BlockSpec(memory_space=pltpu.SMEM)]
        + [pl.BlockSpec(memory_space=pltpu.VMEM)] * len(operands),
        out_specs=pl.BlockSpec(memory_space=pltpu.VMEM),
        out_shape=pltpu.VMEM(shape, dtype),
        compiler_params=pltpu.CompilerParams(vmem_limit_bytes=4 << 20),
        cost_estimate=pl.CostEstimate(
            flops=4 * sum(operand.size for operand in operands[1:]),
            bytes_accessed=4 * sum(operand.size for operand in operands[1:]),
            transcendentals=0,
        ),
        name=name,
    )(scalars, *in_vmem_all(operands))


OWN, OWN_Y, NEAR, NEAR_Y, MID, MID_Y, FAR, FAR_Y, MIDDLE = range(9)


def weigh_kernel(terms, first, last, scalar_ref, adjoint_ref, *refs):
    refs, out_ref = list(refs[:-1]), refs[-1]
    sums = 0.0 if first else refs.pop()[...]
    freqs, parts, _, cells = refs[0].shape
    middle = scalar_ref[MIDDLE] != 0
    for number, choices in terms:
        block = scalar_ref[number]
        field_refs = [refs.pop(0) for _ in range(choices)]
        extra_ref = refs.pop(0) if number == FAR_Y else None
        for freq in range(freqs):
            for part in range(parts):
                weights = adjoint_ref[freq, part, block]
                if extra_ref is not None:
                    weights = weights + extra_ref[freq, part].astype(jnp.float32)
                field = field_refs[0][freq, part].astype(jnp.float32)
                if choices == 2:
                    other = field_refs[1][freq, part].astype(jnp.float32)
                    field = jnp.where(middle, other, field)
                sums = sums + jnp.sum((weights * field).reshape(-1, 8, cells), axis=0)
    out_ref[...] = jnp.sum(sums, axis=0, keepdims=True) if last else sums


def pick_kernel(scalar_ref, first_ref, second_ref, out_ref):
    @pl.when(scalar_ref[MIDDLE] == 0)
    def _():
        out_ref[...] = first_ref[...]

    @pl.when(scalar_ref[MIDDLE] != 0)
    def _():
        out_ref[...] = second_ref[...]


def box_shards(records, active, green, background):
    freqs, _, _, cells = green.shape
    along_y = [(r, r ^ 1) for r in range(8)]
    z_pairs = [(r, r ^ 2) for r in range(8)]
    z_middle = [(r, r ^ 6) for r in range(2, 6)]
    z_outward = [(2, 0), (3, 1), (4, 6), (5, 7)]
    core = [(t, t ^ 1) for t in range(4)]
    along_x = [(t, t ^ 2) for t in range(4)]
    along_both = [(t, t ^ 3) for t in range(4)]
    send, tie = lax.ppermute, lax.optimization_barrier

    me_tx, me_rx = lax.axis_index("tx"), lax.axis_index("rx")
    me_z, me_y = me_rx // 2, me_rx % 2
    lower = me_z < 2
    mid_z, far_z = jnp.where(lower, 2, 1), jnp.where(lower, 3, 0)
    scalars = jnp.stack(
        [(z ^ me_tx) * 2 + y for z in (me_z, me_z ^ 1, mid_z, far_z) for y in (me_y, 1 - me_y)]
        + [(me_z == 1) | (me_z == 2)]
    ).astype(jnp.int32)

    own = background.transpose(1, 2, 0, 3)
    own, scalars, records = tie((own, scalars, records))
    spectra = spectra_of(records, active, freqs)
    spectra_both = send(spectra, "tx", along_both)
    spectra_x = send(spectra, "tx", along_x)
    spectra_core = send(spectra, "tx", core)
    near = send(own, "rx", z_pairs)
    across = send(own, "rx", z_middle)
    own_y = send(own, "rx", along_y)
    near, across, own_y, spectra = tie((near, across, own_y, spectra))

    across_out = send(across, "rx", z_outward)
    far = send(near, "rx", z_middle)
    near_y = send(near, "rx", along_y)

    adjoint, green_kept = adjoint_of([spectra, spectra_core], green, 4)
    adjoint, partial = adjoint_rest(scalars, [spectra_x, spectra_both], green_kept, adjoint)
    adjoint = adjoint.reshape((freqs, 2, 8) + own.shape[2:])

    swap = in_vmem(pick_kernel, scalars, [partial, far], own.shape, own.dtype, "pick")
    swap = send(swap, "rx", z_pairs)
    far_both = send(near_y, "rx", z_middle)
    mid = in_vmem(pick_kernel, scalars, [across_out, across], own.shape, own.dtype, "pick")
    mid_y = send(mid, "rx", along_y)

    sums = in_vmem(
        functools.partial(weigh_kernel, ((OWN, 1), (OWN_Y, 1), (NEAR, 1), (NEAR_Y, 1), (MID, 1)), True, False),
        scalars,
        [adjoint, own, own_y, near, near_y, mid],
        (8, cells),
        jnp.float32,
        "weigh",
    )
    sums = in_vmem(
        functools.partial(weigh_kernel, ((MID_Y, 1), (FAR, 2), (FAR_Y, 1)), False, True),
        scalars,
        [adjoint, mid_y, swap, far, far_both, swap, sums],
        (1, cells),
        jnp.float32,
        "weigh",
    )
    sums = sums.reshape(cells)
    for bit in (1, 2, 4):
        sums = sums + send(sums, "rx", [(r, r ^ bit) for r in range(8)])
    return sums


def plain_shards(records, active, green, background):
    freqs = green.shape[0]
    spectra = spectra_of(records, active, freqs)
    pieces = lax.all_gather(spectra, "tx", axis=0)
    adjoint, _ = adjoint_of([pieces[t] for t in range(pieces.shape[0])], green, pieces.shape[0])
    freqs, _, groups, rows, cells = adjoint.shape
    adjoint = adjoint.reshape(freqs, 2, groups * rows, cells)
    fields = lax.all_gather(background, "rx", axis=0, tiled=True)
    fields = fields.transpose(1, 2, 0, 3).astype(jnp.float32)
    return lax.psum(jnp.sum(adjoint * fields, axis=(0, 1, 2)), "rx")


def solution(mesh):
    placed = (
        P(None, "tx", "rx"),
        P("tx", "rx"),
        P(None, None, "rx", "tx"),
        P("rx", None, None, "tx"),
    )
    body = box_shards if (mesh.shape["tx"], mesh.shape["rx"]) == (4, 8) else plain_shards
    return jax.shard_map(body, mesh=mesh, in_specs=placed, out_specs=P("tx"), check_vma=False)
```

```python
import functools

import jax
import jax.numpy as jnp
import numpy as np
from jax import lax
from jax.experimental import pallas as pl
from jax.experimental.pallas import tpu as pltpu
from jax.sharding import PartitionSpec as P

ROWS = 16


def spread_table(gate_count, freq_count):
    gates = np.arange(gate_count, dtype=np.float32)
    freqs = np.arange(freq_count, dtype=np.float32)
    phases = (
        np.float32(np.pi)
        * (np.float32(2) * gates[None, :] + np.float32(1))
        * (np.float32(1) + np.float32(3) * freqs[:, None])
        / np.float32(2 * gate_count)
    )
    scale = np.sqrt(np.float32(2.0 / gate_count))
    table = np.stack([np.cos(phases) * scale, -np.sin(phases) * scale], axis=1)
    table = table.reshape(2 * freq_count, gate_count).astype(jnp.bfloat16).astype(np.float32)
    return np.kron(table, np.eye(ROWS, dtype=np.float32)).astype(jnp.bfloat16)


def spectra_kernel(table_hbm, active_hbm, records_hbm, out_ref, table_ref, active_ref, records_ref, mask_ref, arrived):
    gates, trans, recv = records_ref.shape
    blocks, channels = active_ref.shape[0], out_ref.shape[0]
    steps = trans // ROWS

    def rows(step):
        return pl.ds(pl.multiple_of(step * ROWS, ROWS), ROWS)

    def fetch(step):
        return pltpu.make_async_copy(
            records_hbm.at[:, rows(step)], records_ref.at[:, rows(step)], arrived.at[step]
        )

    fetch_active = pltpu.make_async_copy(active_hbm, active_ref, arrived.at[steps])
    fetch_table = pltpu.make_async_copy(table_hbm, table_ref, arrived.at[steps + 1])
    fetch_active.start()
    fetch_table.start()
    for step in range(steps):
        fetch(step).start()

    fetch_active.wait()
    block_of = lax.broadcasted_iota(jnp.int32, (blocks, recv), 1) // (recv // blocks)
    spread = (block_of == lax.broadcasted_iota(jnp.int32, (blocks, recv), 0)).astype(jnp.float32)
    mask_ref[...] = lax.dot_general(
        active_ref[...].astype(jnp.float32),
        spread,
        (((0,), (0,)), ((), ())),
        preferred_element_type=jnp.float32,
    )
    fetch_table.wait()

    @pl.loop(0, steps)
    def _(step):
        fetch(step).wait()
        flat = records_ref[:, rows(step)].reshape(gates * ROWS, recv)
        sums = jnp.dot(table_ref[...], flat, preferred_element_type=jnp.float32)
        masked = sums.reshape(channels, ROWS, recv) * mask_ref[rows(step)][None]
        out_ref[:, rows(step)] = masked.astype(out_ref.dtype)


def in_hbm(array):
    return pltpu.with_memory_space_constraint(array, pltpu.HBM)


def spectra_of(records, active, freq_count):
    gates, trans, recv = records.shape
    blocks = active.shape[1]
    channels = 2 * freq_count
    table = jnp.asarray(spread_table(gates, freq_count))
    return pl.pallas_call(
        spectra_kernel,
        in_specs=[pl.BlockSpec(memory_space=pltpu.HBM)] * 3,
        out_specs=pl.BlockSpec(memory_space=pltpu.VMEM),
        out_shape=pltpu.VMEM((channels, trans, recv), jnp.bfloat16),
        scratch_shapes=[
            pltpu.VMEM(table.shape, table.dtype),
            pltpu.VMEM((blocks, trans), jnp.int32),
            pltpu.VMEM(records.shape, records.dtype),
            pltpu.VMEM((trans, recv), jnp.float32),
            pltpu.SemaphoreType.DMA((trans // ROWS + 2,)),
        ],
        compiler_params=pltpu.CompilerParams(vmem_limit_bytes=16 << 20),
        cost_estimate=pl.CostEstimate(
            flops=2 * channels * ROWS * gates * trans * recv,
            bytes_accessed=2 * (gates + channels) * trans * recv,
            transcendentals=0,
        ),
        name="spectra",
    )(in_hbm(table), in_hbm(active.T), in_hbm(records))


def complex_rows(spectra_refs, freq):
    real = jnp.concatenate([ref[freq, 0] for ref in spectra_refs], axis=0)
    imag = jnp.concatenate([ref[freq, 1] for ref in spectra_refs], axis=0)
    return jnp.concatenate(
        [jnp.concatenate([real, -imag], axis=1), jnp.concatenate([-imag, -real], axis=1)], axis=0
    )


def adjoint_kernel(count, green_hbm_ref, *refs):
    spectra_refs, (out_ref, green_ref, arrived) = refs[:count], refs[count:]
    freqs, _, rows, _ = spectra_refs[0].shape

    def fetch(freq):
        return pltpu.make_async_copy(green_hbm_ref.at[freq], green_ref.at[freq], arrived.at[freq])

    for freq in range(freqs):
        fetch(freq).start()

    @pl.loop(0, freqs)
    def _(freq):
        fetch(freq).wait()
        left = complex_rows(spectra_refs, freq)
        sums = jnp.dot(left, green_ref[freq], preferred_element_type=jnp.float32)
        out_ref[freq, :, :count] = sums.reshape(2, count, rows, -1)


def adjoint_rest_kernel(count, half, scalar_ref, green_ref, base_ref, *refs):
    spectra_refs, (out_ref, block_ref) = refs[:count], refs[count:]
    del base_ref
    freqs, _, rows, _ = spectra_refs[0].shape
    block = scalar_ref[FAR_Y]
    group, first = block // 2, pl.multiple_of((block % 2) * half, half)

    @pl.loop(0, freqs)
    def _(freq):
        left = complex_rows(spectra_refs, freq)
        sums = jnp.dot(left, green_ref[freq], preferred_element_type=jnp.float32)
        out_ref[freq, :, count:] = sums.reshape(2, count, rows, -1)
        block_ref[freq] = out_ref[freq, :, group, pl.ds(first, half)].astype(block_ref.dtype)


def in_vmem_all(arrays):
    return [pltpu.with_memory_space_constraint(array, pltpu.VMEM) for array in arrays]


def adjoint_of(pieces, green, groups):
    freqs, _, recv, cells = green.shape
    rows, count = pieces[0].shape[1], len(pieces)
    green = green.reshape(freqs, 2 * recv, cells)
    return pl.pallas_call(
        functools.partial(adjoint_kernel, count),
        in_specs=[pl.BlockSpec(memory_space=pltpu.HBM)]
        + [pl.BlockSpec(memory_space=pltpu.VMEM)] * count,
        out_specs=[pl.BlockSpec(memory_space=pltpu.VMEM)] * 2,
        out_shape=[
            pltpu.VMEM((freqs, 2, groups, rows, cells), jnp.float32),
            pltpu.VMEM(green.shape, green.dtype),
        ],
        scratch_shapes=[pltpu.SemaphoreType.DMA((freqs,))],
        compiler_params=pltpu.CompilerParams(vmem_limit_bytes=4 * count << 20),
        cost_estimate=pl.CostEstimate(
            flops=8 * freqs * count * rows * recv * cells,
            bytes_accessed=4 * freqs * recv * cells,
            transcendentals=0,
        ),
        name="adjoint",
    )(in_hbm(green), *in_vmem_all([piece.reshape(freqs, 2, rows, recv) for piece in pieces]))


def adjoint_rest(scalars, pieces, green, base):
    freqs, _, groups, rows, cells = base.shape
    recv, count = pieces[0].shape[2], len(pieces)
    half = rows // 2
    pieces = [piece.reshape(freqs, 2, rows, recv) for piece in pieces]
    return pl.pallas_call(
        functools.partial(adjoint_rest_kernel, count, half),
        in_specs=[pl.BlockSpec(memory_space=pltpu.SMEM)]
        + [pl.BlockSpec(memory_space=pltpu.VMEM)] * (count + 2),
        out_specs=[pl.BlockSpec(memory_space=pltpu.VMEM)] * 2,
        out_shape=[
            pltpu.VMEM(base.shape, base.dtype),
            pltpu.VMEM((freqs, 2, half, cells), jnp.bfloat16),
        ],
        input_output_aliases={2: 0},
        compiler_params=pltpu.CompilerParams(vmem_limit_bytes=8 << 20),
        cost_estimate=pl.CostEstimate(
            flops=8 * freqs * count * rows * recv * cells,
            bytes_accessed=4 * freqs * recv * cells,
            transcendentals=0,
        ),
        name="adjoint_rest",
    )(scalars, *in_vmem_all([green, base, *pieces]))


def in_vmem(kernel, scalars, operands, shape, dtype, name):
    return pl.pallas_call(
        kernel,
        in_specs=[pl.BlockSpec(memory_space=pltpu.SMEM)]
        + [pl.BlockSpec(memory_space=pltpu.VMEM)] * len(operands),
        out_specs=pl.BlockSpec(memory_space=pltpu.VMEM),
        out_shape=pltpu.VMEM(shape, dtype),
        compiler_params=pltpu.CompilerParams(vmem_limit_bytes=4 << 20),
        cost_estimate=pl.CostEstimate(
            flops=4 * sum(operand.size for operand in operands[1:]),
            bytes_accessed=4 * sum(operand.size for operand in operands[1:]),
            transcendentals=0,
        ),
        name=name,
    )(scalars, *in_vmem_all(operands))


OWN, OWN_Y, NEAR, NEAR_Y, MID, MID_Y, FAR, FAR_Y, MIDDLE = range(9)
RECEIVED = -1


def weigh_kernel(terms, first, last, scalar_ref, adjoint_ref, *refs):
    refs, out_ref = list(refs[:-1]), refs[-1]
    sums = 0.0 if first else refs.pop()[...]
    freqs, parts, _, cells = refs[0].shape
    middle = scalar_ref[MIDDLE] != 0
    for number, choices in terms:
        field_refs = [refs.pop(0) for _ in range(choices)]
        block = refs.pop(0) if number == RECEIVED else adjoint_ref.at[:, :, scalar_ref[number]]
        for freq in range(freqs):
            for part in range(parts):
                field = field_refs[0][freq, part].astype(jnp.float32)
                if choices == 2:
                    other = field_refs[1][freq, part].astype(jnp.float32)
                    field = jnp.where(middle, other, field)
                products = block[freq, part].astype(jnp.float32) * field
                sums = sums + jnp.sum(products.reshape(-1, 8, cells), axis=0)
    out_ref[...] = jnp.sum(sums, axis=0, keepdims=True) if last else sums


def pick_kernel(scalar_ref, first_ref, second_ref, out_ref):
    @pl.when(scalar_ref[MIDDLE] == 0)
    def _():
        out_ref[...] = first_ref[...]

    @pl.when(scalar_ref[MIDDLE] != 0)
    def _():
        out_ref[...] = second_ref[...]


def box_shards(records, active, green, background):
    freqs, _, _, cells = green.shape
    along_y = [(r, r ^ 1) for r in range(8)]
    z_pairs = [(r, r ^ 2) for r in range(8)]
    z_middle = [(r, r ^ 6) for r in range(2, 6)]
    z_outward = [(2, 0), (3, 1), (4, 6), (5, 7)]
    core = [(t, t ^ 1) for t in range(4)]
    along_x = [(t, t ^ 2) for t in range(4)]
    send, tie = lax.ppermute, lax.optimization_barrier

    me_tx, me_rx = lax.axis_index("tx"), lax.axis_index("rx")
    me_z, me_y = me_rx // 2, me_rx % 2
    lower = me_z < 2
    mid_z, far_z = jnp.where(lower, 2, 1), jnp.where(lower, 3, 0)
    scalars = jnp.stack(
        [(z ^ me_tx) * 2 + y for z in (me_z, me_z ^ 1, mid_z, far_z) for y in (me_y, 1 - me_y)]
        + [(me_z == 1) | (me_z == 2)]
    ).astype(jnp.int32)

    own = background.transpose(1, 2, 0, 3)
    own, scalars, records = tie((own, scalars, records))
    spectra = spectra_of(records, active, freqs)
    spectra_x = send(spectra, "tx", along_x)
    spectra_core = send(spectra, "tx", core)
    near = send(own, "rx", z_pairs)
    across = send(own, "rx", z_middle)
    own_y = send(own, "rx", along_y)
    near, across, own_y, spectra = tie((near, across, own_y, spectra))

    across_out = send(across, "rx", z_outward)
    far = send(near, "rx", z_middle)
    near_y = send(near, "rx", along_y)

    adjoint, green_kept = adjoint_of([spectra, spectra_core], green, 4)
    spectra_both = send(spectra_x, "tx", core)
    across_out, far, near_y, spectra_both = tie((across_out, far, near_y, spectra_both))
    adjoint, partial = adjoint_rest(scalars, [spectra_x, spectra_both], green_kept, adjoint)
    adjoint = adjoint.reshape((freqs, 2, 8) + own.shape[2:])

    swap = in_vmem(pick_kernel, scalars, [partial, far], own.shape, own.dtype, "pick")
    swap = send(swap, "rx", z_pairs)
    far_both = send(near_y, "rx", z_middle)
    mid = in_vmem(pick_kernel, scalars, [across_out, across], own.shape, own.dtype, "pick")
    mid_y = send(mid, "rx", along_y)

    early = (OWN, OWN_Y, NEAR, NEAR_Y, MID, MID_Y, FAR_Y)
    sums = in_vmem(
        functools.partial(weigh_kernel, tuple((number, 1) for number in early), True, False),
        scalars,
        [adjoint, own, own_y, near, near_y, mid, mid_y, far_both],
        (8, cells),
        jnp.float32,
        "weigh",
    )
    sums = in_vmem(
        functools.partial(weigh_kernel, ((FAR, 2), (RECEIVED, 1)), False, True),
        scalars,
        [adjoint, swap, far, far_both, swap, sums],
        (1, cells),
        jnp.float32,
        "weigh",
    )
    sums = sums.reshape(cells)
    for bit in (1, 2, 4):
        sums = sums + send(sums, "rx", [(r, r ^ bit) for r in range(8)])
    return sums


def plain_shards(records, active, green, background):
    freqs = green.shape[0]
    spectra = spectra_of(records, active, freqs)
    pieces = lax.all_gather(spectra, "tx", axis=0)
    adjoint, _ = adjoint_of([pieces[t] for t in range(pieces.shape[0])], green, pieces.shape[0])
    freqs, _, groups, rows, cells = adjoint.shape
    adjoint = adjoint.reshape(freqs, 2, groups * rows, cells)
    fields = lax.all_gather(background, "rx", axis=0, tiled=True)
    fields = fields.transpose(1, 2, 0, 3).astype(jnp.float32)
    return lax.psum(jnp.sum(adjoint * fields, axis=(0, 1, 2)), "rx")


def solution(mesh):
    placed = (
        P(None, "tx", "rx"),
        P("tx", "rx"),
        P(None, None, "rx", "tx"),
        P("rx", None, None, "tx"),
    )
    body = box_shards if (mesh.shape["tx"], mesh.shape["rx"]) == (4, 8) else plain_shards
    return jax.shard_map(body, mesh=mesh, in_specs=placed, out_specs=P("tx"), check_vma=False)
```

```python
import functools

import jax
import jax.numpy as jnp
import numpy as np
from jax import lax
from jax.experimental import pallas as pl
from jax.experimental.pallas import tpu as pltpu
from jax.sharding import PartitionSpec as P

ROWS = 16


def spread_table(gate_count, freq_count):
    gates = np.arange(gate_count, dtype=np.float32)
    freqs = np.arange(freq_count, dtype=np.float32)
    phases = (
        np.float32(np.pi)
        * (np.float32(2) * gates[None, :] + np.float32(1))
        * (np.float32(1) + np.float32(3) * freqs[:, None])
        / np.float32(2 * gate_count)
    )
    scale = np.sqrt(np.float32(2.0 / gate_count))
    table = np.stack([np.cos(phases) * scale, -np.sin(phases) * scale], axis=1)
    table = table.reshape(2 * freq_count, gate_count).astype(jnp.bfloat16).astype(np.float32)
    return np.kron(table, np.eye(ROWS, dtype=np.float32)).astype(jnp.bfloat16)


def spectra_kernel(table_hbm, active_hbm, records_hbm, out_ref, table_ref, active_ref, records_ref, mask_ref, arrived):
    gates, trans, recv = records_ref.shape
    blocks, channels = active_ref.shape[0], out_ref.shape[0]
    steps = trans // ROWS

    def rows(step):
        return pl.ds(pl.multiple_of(step * ROWS, ROWS), ROWS)

    def fetch(step):
        return pltpu.make_async_copy(
            records_hbm.at[:, rows(step)], records_ref.at[:, rows(step)], arrived.at[step]
        )

    fetch_active = pltpu.make_async_copy(active_hbm, active_ref, arrived.at[steps])
    fetch_table = pltpu.make_async_copy(table_hbm, table_ref, arrived.at[steps + 1])
    fetch_active.start()
    fetch_table.start()
    for step in range(steps):
        fetch(step).start()

    fetch_active.wait()
    block_of = lax.broadcasted_iota(jnp.int32, (blocks, recv), 1) // (recv // blocks)
    spread = (block_of == lax.broadcasted_iota(jnp.int32, (blocks, recv), 0)).astype(jnp.float32)
    mask_ref[...] = lax.dot_general(
        active_ref[...].astype(jnp.float32),
        spread,
        (((0,), (0,)), ((), ())),
        preferred_element_type=jnp.float32,
    )
    fetch_table.wait()

    @pl.loop(0, steps)
    def _(step):
        fetch(step).wait()
        flat = records_ref[:, rows(step)].reshape(gates * ROWS, recv)
        sums = jnp.dot(table_ref[...], flat, preferred_element_type=jnp.float32)
        masked = sums.reshape(channels, ROWS, recv) * mask_ref[rows(step)][None]
        out_ref[:, rows(step)] = masked.astype(out_ref.dtype)


def in_hbm(array):
    return pltpu.with_memory_space_constraint(array, pltpu.HBM)


def spectra_of(records, active, freq_count):
    gates, trans, recv = records.shape
    blocks = active.shape[1]
    channels = 2 * freq_count
    table = jnp.asarray(spread_table(gates, freq_count))
    return pl.pallas_call(
        spectra_kernel,
        in_specs=[pl.BlockSpec(memory_space=pltpu.HBM)] * 3,
        out_specs=pl.BlockSpec(memory_space=pltpu.VMEM),
        out_shape=pltpu.VMEM((channels, trans, recv), jnp.bfloat16),
        scratch_shapes=[
            pltpu.VMEM(table.shape, table.dtype),
            pltpu.VMEM((blocks, trans), jnp.int32),
            pltpu.VMEM(records.shape, records.dtype),
            pltpu.VMEM((trans, recv), jnp.float32),
            pltpu.SemaphoreType.DMA((trans // ROWS + 2,)),
        ],
        compiler_params=pltpu.CompilerParams(vmem_limit_bytes=16 << 20),
        cost_estimate=pl.CostEstimate(
            flops=2 * channels * ROWS * gates * trans * recv,
            bytes_accessed=2 * (gates + channels) * trans * recv,
            transcendentals=0,
        ),
        name="spectra",
    )(in_hbm(table), in_hbm(active.T), in_hbm(records))


def complex_rows(spectra_refs, freq):
    real = jnp.concatenate([ref[freq, 0] for ref in spectra_refs], axis=0)
    imag = jnp.concatenate([ref[freq, 1] for ref in spectra_refs], axis=0)
    return jnp.concatenate(
        [jnp.concatenate([real, -imag], axis=1), jnp.concatenate([-imag, -real], axis=1)], axis=0
    )


def adjoint_kernel(count, green_hbm_ref, *refs):
    spectra_refs, (out_ref, green_ref, arrived) = refs[:count], refs[count:]
    freqs, _, rows, _ = spectra_refs[0].shape

    def fetch(freq):
        return pltpu.make_async_copy(green_hbm_ref.at[freq], green_ref.at[freq], arrived.at[freq])

    for freq in range(freqs):
        fetch(freq).start()

    @pl.loop(0, freqs)
    def _(freq):
        fetch(freq).wait()
        left = complex_rows(spectra_refs, freq)
        sums = jnp.dot(left, green_ref[freq], preferred_element_type=jnp.float32)
        out_ref[freq, :, :count] = sums.reshape(2, count, rows, -1)


def adjoint_rest_kernel(count, half, scalar_ref, green_ref, base_ref, *refs):
    spectra_refs, (out_ref, block_ref) = refs[:count], refs[count:]
    del base_ref
    freqs, _, rows, _ = spectra_refs[0].shape
    block = scalar_ref[FAR_Y]
    group, first = block // 2, pl.multiple_of((block % 2) * half, half)

    @pl.loop(0, freqs)
    def _(freq):
        left = complex_rows(spectra_refs, freq)
        sums = jnp.dot(left, green_ref[freq], preferred_element_type=jnp.float32)
        out_ref[freq, :, count:] = sums.reshape(2, count, rows, -1)
        block_ref[freq] = out_ref[freq, :, group, pl.ds(first, half)].astype(block_ref.dtype)


def in_vmem_all(arrays):
    return [pltpu.with_memory_space_constraint(array, pltpu.VMEM) for array in arrays]


def adjoint_of(pieces, green, groups):
    freqs, _, recv, cells = green.shape
    rows, count = pieces[0].shape[1], len(pieces)
    green = green.reshape(freqs, 2 * recv, cells)
    return pl.pallas_call(
        functools.partial(adjoint_kernel, count),
        in_specs=[pl.BlockSpec(memory_space=pltpu.HBM)]
        + [pl.BlockSpec(memory_space=pltpu.VMEM)] * count,
        out_specs=[pl.BlockSpec(memory_space=pltpu.VMEM)] * 2,
        out_shape=[
            pltpu.VMEM((freqs, 2, groups, rows, cells), jnp.float32),
            pltpu.VMEM(green.shape, green.dtype),
        ],
        scratch_shapes=[pltpu.SemaphoreType.DMA((freqs,))],
        compiler_params=pltpu.CompilerParams(vmem_limit_bytes=4 * count << 20),
        cost_estimate=pl.CostEstimate(
            flops=8 * freqs * count * rows * recv * cells,
            bytes_accessed=4 * freqs * recv * cells,
            transcendentals=0,
        ),
        name="adjoint",
    )(in_hbm(green), *in_vmem_all([piece.reshape(freqs, 2, rows, recv) for piece in pieces]))


def adjoint_rest(scalars, pieces, green, base):
    freqs, _, groups, rows, cells = base.shape
    recv, count = pieces[0].shape[2], len(pieces)
    half = rows // 2
    pieces = [piece.reshape(freqs, 2, rows, recv) for piece in pieces]
    return pl.pallas_call(
        functools.partial(adjoint_rest_kernel, count, half),
        in_specs=[pl.BlockSpec(memory_space=pltpu.SMEM)]
        + [pl.BlockSpec(memory_space=pltpu.VMEM)] * (count + 2),
        out_specs=[pl.BlockSpec(memory_space=pltpu.VMEM)] * 2,
        out_shape=[
            pltpu.VMEM(base.shape, base.dtype),
            pltpu.VMEM((freqs, 2, half, cells), jnp.bfloat16),
        ],
        input_output_aliases={2: 0},
        compiler_params=pltpu.CompilerParams(vmem_limit_bytes=8 << 20),
        cost_estimate=pl.CostEstimate(
            flops=8 * freqs * count * rows * recv * cells,
            bytes_accessed=4 * freqs * recv * cells,
            transcendentals=0,
        ),
        name="adjoint_rest",
    )(scalars, *in_vmem_all([green, base, *pieces]))


def in_vmem(kernel, scalars, operands, shape, dtype, name):
    return pl.pallas_call(
        kernel,
        in_specs=[pl.BlockSpec(memory_space=pltpu.SMEM)]
        + [pl.BlockSpec(memory_space=pltpu.VMEM)] * len(operands),
        out_specs=pl.BlockSpec(memory_space=pltpu.VMEM),
        out_shape=pltpu.VMEM(shape, dtype),
        compiler_params=pltpu.CompilerParams(vmem_limit_bytes=4 << 20),
        cost_estimate=pl.CostEstimate(
            flops=4 * sum(operand.size for operand in operands[1:]),
            bytes_accessed=4 * sum(operand.size for operand in operands[1:]),
            transcendentals=0,
        ),
        name=name,
    )(scalars, *in_vmem_all(operands))


OWN, OWN_Y, NEAR, NEAR_Y, MID, MID_Y, FAR, FAR_Y, MIDDLE = range(9)
RECEIVED = -1


def weigh_kernel(terms, first, last, scalar_ref, adjoint_ref, *refs):
    refs, out_ref = list(refs[:-1]), refs[-1]
    sums = 0.0 if first else refs.pop()[...]
    freqs, parts, _, cells = refs[0].shape
    middle = scalar_ref[MIDDLE] != 0
    for number, choices in terms:
        field_refs = [refs.pop(0) for _ in range(choices)]
        block = refs.pop(0) if number == RECEIVED else adjoint_ref.at[:, :, scalar_ref[number]]
        for freq in range(freqs):
            for part in range(parts):
                field = field_refs[0][freq, part].astype(jnp.float32)
                if choices == 2:
                    other = field_refs[1][freq, part].astype(jnp.float32)
                    field = jnp.where(middle, other, field)
                if number in (FAR_Y, RECEIVED):
                    field = jnp.where(middle, field, 0.0)
                products = block[freq, part].astype(jnp.float32) * field
                sums = sums + jnp.sum(products.reshape(-1, 8, cells), axis=0)
    out_ref[...] = jnp.sum(sums, axis=0, keepdims=True) if last else sums


def pick_kernel(scalar_ref, first_ref, second_ref, out_ref):
    @pl.when(scalar_ref[MIDDLE] == 0)
    def _():
        out_ref[...] = first_ref[...]

    @pl.when(scalar_ref[MIDDLE] != 0)
    def _():
        out_ref[...] = second_ref[...]


def box_shards(records, active, green, background):
    freqs, _, _, cells = green.shape
    along_y = [(r, r ^ 1) for r in range(8)]
    z_pairs = [(r, r ^ 2) for r in range(8)]
    z_middle = [(t * 8 + r, t * 8 + (r ^ 6)) for t in range(4) for r in range(2, 6)]
    z_middle += [(t * 8 + r, (t ^ 1) * 8 + r) for t in range(4) for r in (0, 1, 6, 7)]
    core = [(t, t ^ 1) for t in range(4)]
    along_x = [(t, t ^ 2) for t in range(4)]
    send, tie = lax.ppermute, lax.optimization_barrier

    me_tx, me_rx = lax.axis_index("tx"), lax.axis_index("rx")
    me_z, me_y = me_rx // 2, me_rx % 2
    lower = me_z < 2
    mid_z, far_z = jnp.where(lower, 2, 1), jnp.where(lower, 3, 0)
    scalars = jnp.stack(
        [(z ^ me_tx) * 2 + y for z in (me_z, me_z ^ 1, mid_z, far_z) for y in (me_y, 1 - me_y)]
        + [(me_z == 1) | (me_z == 2)]
    ).astype(jnp.int32)

    own = background.transpose(1, 2, 0, 3)
    own, scalars, records = tie((own, scalars, records))
    spectra = spectra_of(records, active, freqs)
    spectra_x = send(spectra, "tx", along_x)
    spectra_core = send(spectra, "tx", core)
    near = send(own, "rx", z_pairs)
    across = send(own, ("tx", "rx"), z_middle)
    own_y = send(own, "rx", along_y)
    near, across, own_y, spectra = tie((near, across, own_y, spectra))

    across_out = send(across, "rx", z_pairs)
    far = send(near, ("tx", "rx"), z_middle)
    near_y = send(near, "rx", along_y)

    adjoint, green_kept = adjoint_of([spectra, spectra_core], green, 4)
    spectra_both = send(spectra_x, "tx", core)
    across_out, far, near_y, spectra_both = tie((across_out, far, near_y, spectra_both))
    adjoint, partial = adjoint_rest(scalars, [spectra_x, spectra_both], green_kept, adjoint)
    adjoint = adjoint.reshape((freqs, 2, 8) + own.shape[2:])

    swap = in_vmem(pick_kernel, scalars, [partial, far], own.shape, own.dtype, "pick")
    swap = send(swap, "rx", z_pairs)
    far_both = send(near_y, ("tx", "rx"), z_middle)
    mid = in_vmem(pick_kernel, scalars, [across_out, across], own.shape, own.dtype, "pick")
    mid_y = send(mid, "rx", along_y)

    early = (OWN, OWN_Y, NEAR, NEAR_Y, MID, MID_Y, FAR_Y)
    sums = in_vmem(
        functools.partial(weigh_kernel, tuple((number, 1) for number in early), True, False),
        scalars,
        [adjoint, own, own_y, near, near_y, mid, mid_y, far_both],
        (8, cells),
        jnp.float32,
        "weigh",
    )
    sums = in_vmem(
        functools.partial(weigh_kernel, ((FAR, 2), (RECEIVED, 1)), False, True),
        scalars,
        [adjoint, swap, far, far_both, swap, sums],
        (1, cells),
        jnp.float32,
        "weigh",
    )
    sums = sums.reshape(cells)
    for bit in (1, 2, 4):
        sums = sums + send(sums, "rx", [(r, r ^ bit) for r in range(8)])
    return sums


def plain_shards(records, active, green, background):
    freqs = green.shape[0]
    spectra = spectra_of(records, active, freqs)
    pieces = lax.all_gather(spectra, "tx", axis=0)
    adjoint, _ = adjoint_of([pieces[t] for t in range(pieces.shape[0])], green, pieces.shape[0])
    freqs, _, groups, rows, cells = adjoint.shape
    adjoint = adjoint.reshape(freqs, 2, groups * rows, cells)
    fields = lax.all_gather(background, "rx", axis=0, tiled=True)
    fields = fields.transpose(1, 2, 0, 3).astype(jnp.float32)
    return lax.psum(jnp.sum(adjoint * fields, axis=(0, 1, 2)), "rx")


def solution(mesh):
    placed = (
        P(None, "tx", "rx"),
        P("tx", "rx"),
        P(None, None, "rx", "tx"),
        P("rx", None, None, "tx"),
    )
    body = box_shards if (mesh.shape["tx"], mesh.shape["rx"]) == (4, 8) else plain_shards
    return jax.shard_map(body, mesh=mesh, in_specs=placed, out_specs=P("tx"), check_vma=False)
```

```python
import functools

import jax
import jax.numpy as jnp
import numpy as np
from jax import lax
from jax.experimental import pallas as pl
from jax.experimental.pallas import tpu as pltpu
from jax.sharding import PartitionSpec as P

ROWS = 16


def spread_table(gate_count, freq_count):
    gates = np.arange(gate_count, dtype=np.float32)
    freqs = np.arange(freq_count, dtype=np.float32)
    phases = (
        np.float32(np.pi)
        * (np.float32(2) * gates[None, :] + np.float32(1))
        * (np.float32(1) + np.float32(3) * freqs[:, None])
        / np.float32(2 * gate_count)
    )
    scale = np.sqrt(np.float32(2.0 / gate_count))
    table = np.stack([np.cos(phases) * scale, -np.sin(phases) * scale], axis=1)
    table = table.reshape(2 * freq_count, gate_count).astype(jnp.bfloat16).astype(np.float32)
    return np.kron(table, np.eye(ROWS, dtype=np.float32)).astype(jnp.bfloat16)


def spectra_kernel(table_hbm, active_hbm, records_hbm, out_ref, table_ref, active_ref, records_ref, mask_ref, arrived):
    gates, trans, recv = records_ref.shape
    blocks, channels = active_ref.shape[0], out_ref.shape[0]
    steps = trans // ROWS

    def rows(step):
        return pl.ds(pl.multiple_of(step * ROWS, ROWS), ROWS)

    def fetch(step):
        return pltpu.make_async_copy(
            records_hbm.at[:, rows(step)], records_ref.at[:, rows(step)], arrived.at[step]
        )

    fetch_active = pltpu.make_async_copy(active_hbm, active_ref, arrived.at[steps])
    fetch_table = pltpu.make_async_copy(table_hbm, table_ref, arrived.at[steps + 1])
    fetch_active.start()
    fetch_table.start()
    for step in range(steps):
        fetch(step).start()

    fetch_active.wait()
    block_of = lax.broadcasted_iota(jnp.int32, (blocks, recv), 1) // (recv // blocks)
    spread = (block_of == lax.broadcasted_iota(jnp.int32, (blocks, recv), 0)).astype(jnp.float32)
    mask_ref[...] = lax.dot_general(
        active_ref[...].astype(jnp.float32),
        spread,
        (((0,), (0,)), ((), ())),
        preferred_element_type=jnp.float32,
    )
    fetch_table.wait()

    @pl.loop(0, steps)
    def _(step):
        fetch(step).wait()
        flat = records_ref[:, rows(step)].reshape(gates * ROWS, recv)
        sums = jnp.dot(table_ref[...], flat, preferred_element_type=jnp.float32)
        masked = sums.reshape(channels, ROWS, recv) * mask_ref[rows(step)][None]
        out_ref[:, rows(step)] = masked.astype(out_ref.dtype)


def in_hbm(array):
    return pltpu.with_memory_space_constraint(array, pltpu.HBM)


def spectra_of(records, active, freq_count):
    gates, trans, recv = records.shape
    blocks = active.shape[1]
    channels = 2 * freq_count
    table = jnp.asarray(spread_table(gates, freq_count))
    return pl.pallas_call(
        spectra_kernel,
        in_specs=[pl.BlockSpec(memory_space=pltpu.HBM)] * 3,
        out_specs=pl.BlockSpec(memory_space=pltpu.VMEM),
        out_shape=pltpu.VMEM((channels, trans, recv), jnp.bfloat16),
        scratch_shapes=[
            pltpu.VMEM(table.shape, table.dtype),
            pltpu.VMEM((blocks, trans), jnp.int32),
            pltpu.VMEM(records.shape, records.dtype),
            pltpu.VMEM((trans, recv), jnp.float32),
            pltpu.SemaphoreType.DMA((trans // ROWS + 2,)),
        ],
        compiler_params=pltpu.CompilerParams(vmem_limit_bytes=16 << 20),
        cost_estimate=pl.CostEstimate(
            flops=2 * channels * ROWS * gates * trans * recv,
            bytes_accessed=2 * (gates + channels) * trans * recv,
            transcendentals=0,
        ),
        name="spectra",
    )(in_hbm(table), in_hbm(active.T), in_hbm(records))


def complex_rows(spectra_refs, freq):
    real = jnp.concatenate([ref[freq, 0] for ref in spectra_refs], axis=0)
    imag = jnp.concatenate([ref[freq, 1] for ref in spectra_refs], axis=0)
    return jnp.concatenate(
        [jnp.concatenate([real, -imag], axis=1), jnp.concatenate([-imag, -real], axis=1)], axis=0
    )


def adjoint_kernel(count, green_hbm_ref, *refs):
    spectra_refs, (out_ref, green_ref, arrived) = refs[:count], refs[count:]
    freqs, _, rows, _ = spectra_refs[0].shape

    def fetch(freq):
        return pltpu.make_async_copy(green_hbm_ref.at[freq], green_ref.at[freq], arrived.at[freq])

    for freq in range(freqs):
        fetch(freq).start()

    @pl.loop(0, freqs)
    def _(freq):
        fetch(freq).wait()
        left = complex_rows(spectra_refs, freq)
        sums = jnp.dot(left, green_ref[freq], preferred_element_type=jnp.float32)
        out_ref[freq, :, :count] = sums.reshape(2, count, rows, -1)


def adjoint_rest_kernel(count, half, scalar_ref, green_ref, base_ref, *refs):
    spectra_refs, (out_ref, block_ref) = refs[:count], refs[count:]
    del base_ref
    freqs, _, rows, _ = spectra_refs[0].shape
    block = scalar_ref[FAR_Y]
    group, first = block // 2, pl.multiple_of((block % 2) * half, half)

    @pl.loop(0, freqs)
    def _(freq):
        left = complex_rows(spectra_refs, freq)
        sums = jnp.dot(left, green_ref[freq], preferred_element_type=jnp.float32)
        out_ref[freq, :, count:] = sums.reshape(2, count, rows, -1)
        block_ref[freq] = out_ref[freq, :, group, pl.ds(first, half)].astype(block_ref.dtype)


def in_vmem_all(arrays):
    return [pltpu.with_memory_space_constraint(array, pltpu.VMEM) for array in arrays]


def adjoint_of(pieces, green, groups):
    freqs, _, recv, cells = green.shape
    rows, count = pieces[0].shape[1], len(pieces)
    green = green.reshape(freqs, 2 * recv, cells)
    return pl.pallas_call(
        functools.partial(adjoint_kernel, count),
        in_specs=[pl.BlockSpec(memory_space=pltpu.HBM)]
        + [pl.BlockSpec(memory_space=pltpu.VMEM)] * count,
        out_specs=[pl.BlockSpec(memory_space=pltpu.VMEM)] * 2,
        out_shape=[
            pltpu.VMEM((freqs, 2, groups, rows, cells), jnp.float32),
            pltpu.VMEM(green.shape, green.dtype),
        ],
        scratch_shapes=[pltpu.SemaphoreType.DMA((freqs,))],
        compiler_params=pltpu.CompilerParams(vmem_limit_bytes=4 * count << 20),
        cost_estimate=pl.CostEstimate(
            flops=8 * freqs * count * rows * recv * cells,
            bytes_accessed=4 * freqs * recv * cells,
            transcendentals=0,
        ),
        name="adjoint",
    )(in_hbm(green), *in_vmem_all([piece.reshape(freqs, 2, rows, recv) for piece in pieces]))


def adjoint_rest(scalars, pieces, green, base):
    freqs, _, groups, rows, cells = base.shape
    recv, count = pieces[0].shape[2], len(pieces)
    half = rows // 2
    pieces = [piece.reshape(freqs, 2, rows, recv) for piece in pieces]
    return pl.pallas_call(
        functools.partial(adjoint_rest_kernel, count, half),
        in_specs=[pl.BlockSpec(memory_space=pltpu.SMEM)]
        + [pl.BlockSpec(memory_space=pltpu.VMEM)] * (count + 2),
        out_specs=[pl.BlockSpec(memory_space=pltpu.VMEM)] * 2,
        out_shape=[
            pltpu.VMEM(base.shape, base.dtype),
            pltpu.VMEM((freqs, 2, half, cells), jnp.bfloat16),
        ],
        input_output_aliases={2: 0},
        compiler_params=pltpu.CompilerParams(vmem_limit_bytes=8 << 20),
        cost_estimate=pl.CostEstimate(
            flops=8 * freqs * count * rows * recv * cells,
            bytes_accessed=4 * freqs * recv * cells,
            transcendentals=0,
        ),
        name="adjoint_rest",
    )(scalars, *in_vmem_all([green, base, *pieces]))


def in_vmem(kernel, scalars, operands, shape, dtype, name):
    return pl.pallas_call(
        kernel,
        in_specs=[pl.BlockSpec(memory_space=pltpu.SMEM)]
        + [pl.BlockSpec(memory_space=pltpu.VMEM)] * len(operands),
        out_specs=pl.BlockSpec(memory_space=pltpu.VMEM),
        out_shape=pltpu.VMEM(shape, dtype),
        compiler_params=pltpu.CompilerParams(vmem_limit_bytes=4 << 20),
        cost_estimate=pl.CostEstimate(
            flops=4 * sum(operand.size for operand in operands[1:]),
            bytes_accessed=4 * sum(operand.size for operand in operands[1:]),
            transcendentals=0,
        ),
        name=name,
    )(scalars, *in_vmem_all(operands))


OWN, OWN_Y, NEAR, NEAR_Y, MID, MID_Y, FAR, FAR_Y, MIDDLE = range(9)
RECEIVED = -1


def weigh_kernel(terms, first, last, scalar_ref, adjoint_ref, *refs):
    refs, out_ref = list(refs[:-1]), refs[-1]
    sums = 0.0 if first else refs.pop()[...]
    freqs, parts, _, cells = refs[0].shape
    middle = scalar_ref[MIDDLE] != 0
    for number, choices in terms:
        field_refs = [refs.pop(0) for _ in range(choices)]
        block = refs.pop(0) if number == RECEIVED else adjoint_ref.at[:, :, scalar_ref[number]]
        for freq in range(freqs):
            for part in range(parts):
                field = field_refs[0][freq, part].astype(jnp.float32)
                if choices == 2:
                    other = field_refs[1][freq, part].astype(jnp.float32)
                    field = jnp.where(middle, other, field)
                if number in (FAR_Y, RECEIVED):
                    field = jnp.where(middle, field, 0.0)
                products = block[freq, part].astype(jnp.float32) * field
                sums = sums + jnp.sum(products.reshape(-1, 8, cells), axis=0)
    out_ref[...] = jnp.sum(sums, axis=0, keepdims=True) if last else sums


def pick_kernel(scalar_ref, first_ref, second_ref, out_ref):
    @pl.when(scalar_ref[MIDDLE] == 0)
    def _():
        out_ref[...] = first_ref[...]

    @pl.when(scalar_ref[MIDDLE] != 0)
    def _():
        out_ref[...] = second_ref[...]


def box_shards(records, active, green, background):
    freqs, _, _, cells = green.shape
    along_y = [(r, r ^ 1) for r in range(8)]
    z_pairs = [(r, r ^ 2) for r in range(8)]
    z_middle = [(t * 8 + r, t * 8 + (r ^ 6)) for t in range(4) for r in range(2, 6)]
    z_middle += [(t * 8 + r, (t ^ 1) * 8 + r) for t in range(4) for r in (0, 1, 6, 7)]
    core = [(t, t ^ 1) for t in range(4)]
    along_x = [(t, t ^ 2) for t in range(4)]
    send, tie = lax.ppermute, lax.optimization_barrier

    me_tx, me_rx = lax.axis_index("tx"), lax.axis_index("rx")
    me_z, me_y = me_rx // 2, me_rx % 2
    lower = me_z < 2
    mid_z, far_z = jnp.where(lower, 2, 1), jnp.where(lower, 3, 0)
    scalars = jnp.stack(
        [(z ^ me_tx) * 2 + y for z in (me_z, me_z ^ 1, mid_z, far_z) for y in (me_y, 1 - me_y)]
        + [(me_z == 1) | (me_z == 2)]
    ).astype(jnp.int32)

    own = background.transpose(1, 2, 0, 3)
    own, scalars, records = tie((own, scalars, records))
    spectra = spectra_of(records, active, freqs)
    spectra_x = send(spectra, "tx", along_x)
    spectra_core = send(spectra, "tx", core)
    near = send(own, "rx", z_pairs)
    across = send(own, ("tx", "rx"), z_middle)
    own_y = send(own, "rx", along_y)
    near, across, own_y, spectra = tie((near, across, own_y, spectra))

    across_out = send(across, "rx", z_pairs)
    far = send(near, ("tx", "rx"), z_middle)
    near_y = send(near, "rx", along_y)

    adjoint, green_kept = adjoint_of([spectra, spectra_core], green, 4)
    spectra_both = send(spectra_x, "tx", core)
    adjoint, partial = adjoint_rest(scalars, [spectra_x, spectra_both], green_kept, adjoint)
    across_out, near_y, partial = tie((across_out, near_y, partial))
    adjoint = adjoint.reshape((freqs, 2, 8) + own.shape[2:])

    swap = in_vmem(pick_kernel, scalars, [partial, far], own.shape, own.dtype, "pick")
    swap = send(swap, "rx", z_pairs)
    far_both = send(near_y, ("tx", "rx"), z_middle)
    mid = in_vmem(pick_kernel, scalars, [across_out, across], own.shape, own.dtype, "pick")
    mid_y = send(mid, "rx", along_y)

    early = (OWN, OWN_Y, NEAR, NEAR_Y, MID, MID_Y, FAR_Y)
    sums = in_vmem(
        functools.partial(weigh_kernel, tuple((number, 1) for number in early), True, False),
        scalars,
        [adjoint, own, own_y, near, near_y, mid, mid_y, far_both],
        (8, cells),
        jnp.float32,
        "weigh",
    )
    sums = in_vmem(
        functools.partial(weigh_kernel, ((FAR, 2), (RECEIVED, 1)), False, True),
        scalars,
        [adjoint, swap, far, far_both, swap, sums],
        (1, cells),
        jnp.float32,
        "weigh",
    )
    sums = sums.reshape(cells)
    for bit in (1, 2, 4):
        sums = sums + send(sums, "rx", [(r, r ^ bit) for r in range(8)])
    return sums


def plain_shards(records, active, green, background):
    freqs = green.shape[0]
    spectra = spectra_of(records, active, freqs)
    pieces = lax.all_gather(spectra, "tx", axis=0)
    adjoint, _ = adjoint_of([pieces[t] for t in range(pieces.shape[0])], green, pieces.shape[0])
    freqs, _, groups, rows, cells = adjoint.shape
    adjoint = adjoint.reshape(freqs, 2, groups * rows, cells)
    fields = lax.all_gather(background, "rx", axis=0, tiled=True)
    fields = fields.transpose(1, 2, 0, 3).astype(jnp.float32)
    return lax.psum(jnp.sum(adjoint * fields, axis=(0, 1, 2)), "rx")


def solution(mesh):
    placed = (
        P(None, "tx", "rx"),
        P("tx", "rx"),
        P(None, None, "rx", "tx"),
        P("rx", None, None, "tx"),
    )
    body = box_shards if (mesh.shape["tx"], mesh.shape["rx"]) == (4, 8) else plain_shards
    return jax.shard_map(body, mesh=mesh, in_specs=placed, out_specs=P("tx"), check_vma=False)
```

```python
import functools

import jax
import jax.numpy as jnp
import numpy as np
from jax import lax
from jax.experimental import pallas as pl
from jax.experimental.pallas import tpu as pltpu
from jax.sharding import PartitionSpec as P

ROWS = 16


def spread_table(gate_count, freq_count):
    gates = np.arange(gate_count, dtype=np.float32)
    freqs = np.arange(freq_count, dtype=np.float32)
    phases = (
        np.float32(np.pi)
        * (np.float32(2) * gates[None, :] + np.float32(1))
        * (np.float32(1) + np.float32(3) * freqs[:, None])
        / np.float32(2 * gate_count)
    )
    scale = np.sqrt(np.float32(2.0 / gate_count))
    table = np.stack([np.cos(phases) * scale, -np.sin(phases) * scale], axis=1)
    table = table.reshape(2 * freq_count, gate_count).astype(jnp.bfloat16).astype(np.float32)
    return np.kron(table, np.eye(ROWS, dtype=np.float32)).astype(jnp.bfloat16)


def spectra_kernel(table_hbm, active_hbm, records_hbm, out_ref, table_ref, active_ref, records_ref, mask_ref, arrived):
    gates, trans, recv = records_ref.shape
    blocks, channels = active_ref.shape[0], out_ref.shape[0]
    steps = trans // ROWS

    def rows(step):
        return pl.ds(pl.multiple_of(step * ROWS, ROWS), ROWS)

    def fetch(step):
        return pltpu.make_async_copy(
            records_hbm.at[:, rows(step)], records_ref.at[:, rows(step)], arrived.at[step]
        )

    fetch_active = pltpu.make_async_copy(active_hbm, active_ref, arrived.at[steps])
    fetch_table = pltpu.make_async_copy(table_hbm, table_ref, arrived.at[steps + 1])
    fetch_active.start()
    fetch_table.start()
    for step in range(steps):
        fetch(step).start()

    fetch_active.wait()
    block_of = lax.broadcasted_iota(jnp.int32, (blocks, recv), 1) // (recv // blocks)
    spread = (block_of == lax.broadcasted_iota(jnp.int32, (blocks, recv), 0)).astype(jnp.float32)
    mask_ref[...] = lax.dot_general(
        active_ref[...].astype(jnp.float32),
        spread,
        (((0,), (0,)), ((), ())),
        preferred_element_type=jnp.float32,
    )
    fetch_table.wait()

    @pl.loop(0, steps)
    def _(step):
        fetch(step).wait()
        flat = records_ref[:, rows(step)].reshape(gates * ROWS, recv)
        sums = jnp.dot(table_ref[...], flat, preferred_element_type=jnp.float32)
        masked = sums.reshape(channels, ROWS, recv) * mask_ref[rows(step)][None]
        out_ref[:, rows(step)] = masked.astype(out_ref.dtype)


def in_hbm(array):
    return pltpu.with_memory_space_constraint(array, pltpu.HBM)


def spectra_of(records, active, freq_count):
    gates, trans, recv = records.shape
    blocks = active.shape[1]
    channels = 2 * freq_count
    table = jnp.asarray(spread_table(gates, freq_count))
    return pl.pallas_call(
        spectra_kernel,
        in_specs=[pl.BlockSpec(memory_space=pltpu.HBM)] * 3,
        out_specs=pl.BlockSpec(memory_space=pltpu.VMEM),
        out_shape=pltpu.VMEM((channels, trans, recv), jnp.bfloat16),
        scratch_shapes=[
            pltpu.VMEM(table.shape, table.dtype),
            pltpu.VMEM((blocks, trans), jnp.int32),
            pltpu.VMEM(records.shape, records.dtype),
            pltpu.VMEM((trans, recv), jnp.float32),
            pltpu.SemaphoreType.DMA((trans // ROWS + 2,)),
        ],
        compiler_params=pltpu.CompilerParams(vmem_limit_bytes=16 << 20),
        cost_estimate=pl.CostEstimate(
            flops=2 * channels * ROWS * gates * trans * recv,
            bytes_accessed=2 * (gates + channels) * trans * recv,
            transcendentals=0,
        ),
        name="spectra",
    )(in_hbm(table), in_hbm(active.T), in_hbm(records))


def complex_rows(spectra_refs, freq):
    real = jnp.concatenate([ref[freq, 0] for ref in spectra_refs], axis=0)
    imag = jnp.concatenate([ref[freq, 1] for ref in spectra_refs], axis=0)
    return jnp.concatenate(
        [jnp.concatenate([real, -imag], axis=1), jnp.concatenate([-imag, -real], axis=1)], axis=0
    )


def adjoint_kernel(count, green_hbm_ref, *refs):
    spectra_refs, (out_ref, green_ref, arrived) = refs[:count], refs[count:]
    freqs, _, rows, _ = spectra_refs[0].shape

    def fetch(freq):
        return pltpu.make_async_copy(green_hbm_ref.at[freq], green_ref.at[freq], arrived.at[freq])

    for freq in range(freqs):
        fetch(freq).start()

    @pl.loop(0, freqs)
    def _(freq):
        fetch(freq).wait()
        left = complex_rows(spectra_refs, freq)
        sums = jnp.dot(left, green_ref[freq], preferred_element_type=jnp.float32)
        out_ref[freq, :, :count] = sums.reshape(2, count, rows, -1)


def adjoint_rest_kernel(count, half, scalar_ref, green_ref, base_ref, *refs):
    spectra_refs, (out_ref, block_ref) = refs[:count], refs[count:]
    del base_ref
    freqs, _, rows, _ = spectra_refs[0].shape
    block = scalar_ref[FAR_Y]
    group, first = block // 2, pl.multiple_of((block % 2) * half, half)

    @pl.loop(0, freqs)
    def _(freq):
        left = complex_rows(spectra_refs, freq)
        sums = jnp.dot(left, green_ref[freq], preferred_element_type=jnp.float32)
        out_ref[freq, :, count:] = sums.reshape(2, count, rows, -1)
        block_ref[freq] = out_ref[freq, :, group, pl.ds(first, half)].astype(block_ref.dtype)


def in_vmem_all(arrays):
    return [pltpu.with_memory_space_constraint(array, pltpu.VMEM) for array in arrays]


def adjoint_of(pieces, green, groups):
    freqs, _, recv, cells = green.shape
    rows, count = pieces[0].shape[1], len(pieces)
    green = green.reshape(freqs, 2 * recv, cells)
    return pl.pallas_call(
        functools.partial(adjoint_kernel, count),
        in_specs=[pl.BlockSpec(memory_space=pltpu.HBM)]
        + [pl.BlockSpec(memory_space=pltpu.VMEM)] * count,
        out_specs=[pl.BlockSpec(memory_space=pltpu.VMEM)] * 2,
        out_shape=[
            pltpu.VMEM((freqs, 2, groups, rows, cells), jnp.float32),
            pltpu.VMEM(green.shape, green.dtype),
        ],
        scratch_shapes=[pltpu.SemaphoreType.DMA((freqs,))],
        compiler_params=pltpu.CompilerParams(vmem_limit_bytes=4 * count << 20),
        cost_estimate=pl.CostEstimate(
            flops=8 * freqs * count * rows * recv * cells,
            bytes_accessed=4 * freqs * recv * cells,
            transcendentals=0,
        ),
        name="adjoint",
    )(in_hbm(green), *in_vmem_all([piece.reshape(freqs, 2, rows, recv) for piece in pieces]))


def adjoint_rest(scalars, pieces, green, base):
    freqs, _, groups, rows, cells = base.shape
    recv, count = pieces[0].shape[2], len(pieces)
    half = rows // 2
    pieces = [piece.reshape(freqs, 2, rows, recv) for piece in pieces]
    return pl.pallas_call(
        functools.partial(adjoint_rest_kernel, count, half),
        in_specs=[pl.BlockSpec(memory_space=pltpu.SMEM)]
        + [pl.BlockSpec(memory_space=pltpu.VMEM)] * (count + 2),
        out_specs=[pl.BlockSpec(memory_space=pltpu.VMEM)] * 2,
        out_shape=[
            pltpu.VMEM(base.shape, base.dtype),
            pltpu.VMEM((freqs, 2, half, cells), jnp.bfloat16),
        ],
        input_output_aliases={2: 0},
        compiler_params=pltpu.CompilerParams(vmem_limit_bytes=8 << 20),
        cost_estimate=pl.CostEstimate(
            flops=8 * freqs * count * rows * recv * cells,
            bytes_accessed=4 * freqs * recv * cells,
            transcendentals=0,
        ),
        name="adjoint_rest",
    )(scalars, *in_vmem_all([green, base, *pieces]))


def in_vmem(kernel, scalars, operands, shape, dtype, name):
    return pl.pallas_call(
        kernel,
        in_specs=[pl.BlockSpec(memory_space=pltpu.SMEM)]
        + [pl.BlockSpec(memory_space=pltpu.VMEM)] * len(operands),
        out_specs=pl.BlockSpec(memory_space=pltpu.VMEM),
        out_shape=pltpu.VMEM(shape, dtype),
        compiler_params=pltpu.CompilerParams(vmem_limit_bytes=4 << 20),
        cost_estimate=pl.CostEstimate(
            flops=4 * sum(operand.size for operand in operands[1:]),
            bytes_accessed=4 * sum(operand.size for operand in operands[1:]),
            transcendentals=0,
        ),
        name=name,
    )(scalars, *in_vmem_all(operands))


OWN, OWN_Y, NEAR, NEAR_Y, MID, MID_Y, FAR, FAR_Y, MIDDLE = range(9)
RECEIVED = -1


def weigh_kernel(terms, first, last, scalar_ref, adjoint_ref, *refs):
    refs, out_ref = list(refs[:-1]), refs[-1]
    sums = 0.0 if first else refs.pop()[...]
    freqs, parts, _, cells = refs[0].shape
    middle = scalar_ref[MIDDLE] != 0
    for number, choices in terms:
        field_refs = [refs.pop(0) for _ in range(choices)]
        block = refs.pop(0) if number == RECEIVED else adjoint_ref.at[:, :, scalar_ref[number]]
        for freq in range(freqs):
            for part in range(parts):
                field = field_refs[0][freq, part].astype(jnp.float32)
                if choices == 2:
                    other = field_refs[1][freq, part].astype(jnp.float32)
                    field = jnp.where(middle, other, field)
                if number in (FAR_Y, RECEIVED):
                    field = jnp.where(middle, field, 0.0)
                products = block[freq, part].astype(jnp.float32) * field
                sums = sums + jnp.sum(products.reshape(-1, 8, cells), axis=0)
    out_ref[...] = jnp.sum(sums, axis=0, keepdims=True) if last else sums


def pick_kernel(scalar_ref, first_ref, second_ref, out_ref):
    @pl.when(scalar_ref[MIDDLE] == 0)
    def _():
        out_ref[...] = first_ref[...]

    @pl.when(scalar_ref[MIDDLE] != 0)
    def _():
        out_ref[...] = second_ref[...]


def box_shards(records, active, green, background):
    freqs, _, _, cells = green.shape
    along_y = [(r, r ^ 1) for r in range(8)]
    z_pairs = [(r, r ^ 2) for r in range(8)]
    z_middle = [(t * 8 + r, t * 8 + (r ^ 6)) for t in range(4) for r in range(2, 6)]
    z_middle += [(t * 8 + r, (t ^ 1) * 8 + r) for t in range(4) for r in (0, 1, 6, 7)]
    z_middle_x = [(t * 8 + r, t * 8 + (r ^ 6)) for t in range(4) for r in range(2, 6)]
    z_middle_x += [(t * 8 + r, (t ^ 2) * 8 + r) for t in range(4) for r in (0, 1, 6, 7)]
    core = [(t, t ^ 1) for t in range(4)]
    along_x = [(t, t ^ 2) for t in range(4)]
    send, tie = lax.ppermute, lax.optimization_barrier

    me_tx, me_rx = lax.axis_index("tx"), lax.axis_index("rx")
    me_z, me_y = me_rx // 2, me_rx % 2
    lower = me_z < 2
    mid_z, far_z = jnp.where(lower, 2, 1), jnp.where(lower, 3, 0)
    scalars = jnp.stack(
        [(z ^ me_tx) * 2 + y for z in (me_z, me_z ^ 1, mid_z, far_z) for y in (me_y, 1 - me_y)]
        + [(me_z == 1) | (me_z == 2)]
    ).astype(jnp.int32)

    own = background.transpose(1, 2, 0, 3)
    own, scalars, records = tie((own, scalars, records))
    spectra = spectra_of(records, active, freqs)
    spectra_x = send(spectra, "tx", along_x)
    spectra_core = send(spectra, "tx", core)
    near = send(own, "rx", z_pairs)
    across = send(own, ("tx", "rx"), z_middle)
    own_y = send(own, "rx", along_y)
    near, across, own_y, spectra = tie((near, across, own_y, spectra))

    across_out = send(across, "rx", z_pairs)
    far = send(near, ("tx", "rx"), z_middle_x)
    near_y = send(near, "rx", along_y)

    adjoint, green_kept = adjoint_of([spectra, spectra_core], green, 4)
    spectra_both = send(spectra_x, "tx", core)
    adjoint, partial = adjoint_rest(scalars, [spectra_x, spectra_both], green_kept, adjoint)
    adjoint = adjoint.reshape((freqs, 2, 8) + own.shape[2:])

    swap = in_vmem(pick_kernel, scalars, [partial, far], own.shape, own.dtype, "pick")
    swap = send(swap, "rx", z_pairs)
    far_both = send(near_y, ("tx", "rx"), z_middle_x)
    mid = in_vmem(pick_kernel, scalars, [across_out, across], own.shape, own.dtype, "pick")
    mid_y = send(mid, "rx", along_y)

    early = (OWN, OWN_Y, NEAR, NEAR_Y, MID, MID_Y, FAR_Y)
    sums = in_vmem(
        functools.partial(weigh_kernel, tuple((number, 1) for number in early), True, False),
        scalars,
        [adjoint, own, own_y, near, near_y, mid, mid_y, far_both],
        (8, cells),
        jnp.float32,
        "weigh",
    )
    sums = in_vmem(
        functools.partial(weigh_kernel, ((FAR, 2), (RECEIVED, 1)), False, True),
        scalars,
        [adjoint, swap, far, far_both, swap, sums],
        (1, cells),
        jnp.float32,
        "weigh",
    )
    sums = sums.reshape(cells)
    for bits in ((3, 2, 1), (4,)):
        sums = sums + sum(send(sums, "rx", [(r, r ^ bit) for r in range(8)]) for bit in bits)
    return sums


def plain_shards(records, active, green, background):
    freqs = green.shape[0]
    spectra = spectra_of(records, active, freqs)
    pieces = lax.all_gather(spectra, "tx", axis=0)
    adjoint, _ = adjoint_of([pieces[t] for t in range(pieces.shape[0])], green, pieces.shape[0])
    freqs, _, groups, rows, cells = adjoint.shape
    adjoint = adjoint.reshape(freqs, 2, groups * rows, cells)
    fields = lax.all_gather(background, "rx", axis=0, tiled=True)
    fields = fields.transpose(1, 2, 0, 3).astype(jnp.float32)
    return lax.psum(jnp.sum(adjoint * fields, axis=(0, 1, 2)), "rx")


def solution(mesh):
    placed = (
        P(None, "tx", "rx"),
        P("tx", "rx"),
        P(None, None, "rx", "tx"),
        P("rx", None, None, "tx"),
    )
    body = box_shards if (mesh.shape["tx"], mesh.shape["rx"]) == (4, 8) else plain_shards
    return jax.shard_map(body, mesh=mesh, in_specs=placed, out_specs=P("tx"), check_vma=False)
```

```python
import functools

import jax
import jax.numpy as jnp
import numpy as np
from jax import lax
from jax.experimental import pallas as pl
from jax.experimental.pallas import tpu as pltpu
from jax.sharding import PartitionSpec as P

ROWS = 16


def spread_table(gate_count, freq_count):
    gates = np.arange(gate_count, dtype=np.float32)
    freqs = np.arange(freq_count, dtype=np.float32)
    phases = (
        np.float32(np.pi)
        * (np.float32(2) * gates[None, :] + np.float32(1))
        * (np.float32(1) + np.float32(3) * freqs[:, None])
        / np.float32(2 * gate_count)
    )
    scale = np.sqrt(np.float32(2.0 / gate_count))
    table = np.stack([np.cos(phases) * scale, -np.sin(phases) * scale], axis=1)
    table = table.reshape(2 * freq_count, gate_count).astype(jnp.bfloat16).astype(np.float32)
    return np.kron(table, np.eye(ROWS, dtype=np.float32)).astype(jnp.bfloat16)


def spectra_kernel(table_hbm, active_hbm, records_hbm, out_ref, table_ref, active_ref, records_ref, mask_ref, arrived):
    gates, trans, recv = records_ref.shape
    blocks, channels = active_ref.shape[0], out_ref.shape[0]
    steps = trans // ROWS

    def rows(step):
        return pl.ds(pl.multiple_of(step * ROWS, ROWS), ROWS)

    def fetch(step):
        return pltpu.make_async_copy(
            records_hbm.at[:, rows(step)], records_ref.at[:, rows(step)], arrived.at[step]
        )

    fetch_active = pltpu.make_async_copy(active_hbm, active_ref, arrived.at[steps])
    fetch_table = pltpu.make_async_copy(table_hbm, table_ref, arrived.at[steps + 1])
    fetch_active.start()
    fetch_table.start()
    for step in range(steps):
        fetch(step).start()

    fetch_active.wait()
    block_of = lax.broadcasted_iota(jnp.int32, (blocks, recv), 1) // (recv // blocks)
    spread = (block_of == lax.broadcasted_iota(jnp.int32, (blocks, recv), 0)).astype(jnp.float32)
    mask_ref[...] = lax.dot_general(
        active_ref[...].astype(jnp.float32),
        spread,
        (((0,), (0,)), ((), ())),
        preferred_element_type=jnp.float32,
    )
    fetch_table.wait()

    @pl.loop(0, steps)
    def _(step):
        fetch(step).wait()
        flat = records_ref[:, rows(step)].reshape(gates * ROWS, recv)
        sums = jnp.dot(table_ref[...], flat, preferred_element_type=jnp.float32)
        masked = sums.reshape(channels, ROWS, recv) * mask_ref[rows(step)][None]
        out_ref[:, rows(step)] = masked.astype(out_ref.dtype)


def in_hbm(array):
    return pltpu.with_memory_space_constraint(array, pltpu.HBM)


def spectra_of(records, active, freq_count):
    gates, trans, recv = records.shape
    blocks = active.shape[1]
    channels = 2 * freq_count
    table = jnp.asarray(spread_table(gates, freq_count))
    return pl.pallas_call(
        spectra_kernel,
        in_specs=[pl.BlockSpec(memory_space=pltpu.HBM)] * 3,
        out_specs=pl.BlockSpec(memory_space=pltpu.VMEM),
        out_shape=pltpu.VMEM((channels, trans, recv), jnp.bfloat16),
        scratch_shapes=[
            pltpu.VMEM(table.shape, table.dtype),
            pltpu.VMEM((blocks, trans), jnp.int32),
            pltpu.VMEM(records.shape, records.dtype),
            pltpu.VMEM((trans, recv), jnp.float32),
            pltpu.SemaphoreType.DMA((trans // ROWS + 2,)),
        ],
        compiler_params=pltpu.CompilerParams(vmem_limit_bytes=16 << 20),
        cost_estimate=pl.CostEstimate(
            flops=2 * channels * ROWS * gates * trans * recv,
            bytes_accessed=2 * (gates + channels) * trans * recv,
            transcendentals=0,
        ),
        name="spectra",
    )(in_hbm(table), in_hbm(active.T), in_hbm(records))


def complex_rows(spectra_refs, freq):
    real = jnp.concatenate([ref[freq, 0] for ref in spectra_refs], axis=0)
    imag = jnp.concatenate([ref[freq, 1] for ref in spectra_refs], axis=0)
    return jnp.concatenate(
        [jnp.concatenate([real, -imag], axis=1), jnp.concatenate([-imag, -real], axis=1)], axis=0
    )


def adjoint_kernel(count, green_hbm_ref, *refs):
    spectra_refs, (out_ref, green_ref, arrived) = refs[:count], refs[count:]
    freqs, _, rows, _ = spectra_refs[0].shape

    def fetch(freq):
        return pltpu.make_async_copy(green_hbm_ref.at[freq], green_ref.at[freq], arrived.at[freq])

    for freq in range(freqs):
        fetch(freq).start()

    @pl.loop(0, freqs)
    def _(freq):
        fetch(freq).wait()
        left = complex_rows(spectra_refs, freq)
        sums = jnp.dot(left, green_ref[freq], preferred_element_type=jnp.float32)
        out_ref[freq, :, :count] = sums.reshape(2, count, rows, -1)


def adjoint_rest_kernel(count, half, scalar_ref, green_ref, base_ref, *refs):
    spectra_refs, (out_ref, block_ref) = refs[:count], refs[count:]
    del base_ref
    freqs, _, rows, _ = spectra_refs[0].shape
    block = scalar_ref[FAR_Y]
    group, first = block // 2, pl.multiple_of((block % 2) * half, half)

    @pl.loop(0, freqs)
    def _(freq):
        left = complex_rows(spectra_refs, freq)
        sums = jnp.dot(left, green_ref[freq], preferred_element_type=jnp.float32)
        out_ref[freq, :, count:] = sums.reshape(2, count, rows, -1)
        block_ref[freq] = out_ref[freq, :, group, pl.ds(first, half)].astype(block_ref.dtype)


def in_vmem_all(arrays):
    return [pltpu.with_memory_space_constraint(array, pltpu.VMEM) for array in arrays]


def adjoint_of(pieces, green, groups):
    freqs, _, recv, cells = green.shape
    rows, count = pieces[0].shape[1], len(pieces)
    green = green.reshape(freqs, 2 * recv, cells)
    return pl.pallas_call(
        functools.partial(adjoint_kernel, count),
        in_specs=[pl.BlockSpec(memory_space=pltpu.HBM)]
        + [pl.BlockSpec(memory_space=pltpu.VMEM)] * count,
        out_specs=[pl.BlockSpec(memory_space=pltpu.VMEM)] * 2,
        out_shape=[
            pltpu.VMEM((freqs, 2, groups, rows, cells), jnp.float32),
            pltpu.VMEM(green.shape, green.dtype),
        ],
        scratch_shapes=[pltpu.SemaphoreType.DMA((freqs,))],
        compiler_params=pltpu.CompilerParams(vmem_limit_bytes=4 * count << 20),
        cost_estimate=pl.CostEstimate(
            flops=8 * freqs * count * rows * recv * cells,
            bytes_accessed=4 * freqs * recv * cells,
            transcendentals=0,
        ),
        name="adjoint",
    )(in_hbm(green), *in_vmem_all([piece.reshape(freqs, 2, rows, recv) for piece in pieces]))


def adjoint_rest(scalars, pieces, green, base):
    freqs, _, groups, rows, cells = base.shape
    recv, count = pieces[0].shape[2], len(pieces)
    half = rows // 2
    pieces = [piece.reshape(freqs, 2, rows, recv) for piece in pieces]
    return pl.pallas_call(
        functools.partial(adjoint_rest_kernel, count, half),
        in_specs=[pl.BlockSpec(memory_space=pltpu.SMEM)]
        + [pl.BlockSpec(memory_space=pltpu.VMEM)] * (count + 2),
        out_specs=[pl.BlockSpec(memory_space=pltpu.VMEM)] * 2,
        out_shape=[
            pltpu.VMEM(base.shape, base.dtype),
            pltpu.VMEM((freqs, 2, half, cells), jnp.bfloat16),
        ],
        input_output_aliases={2: 0},
        compiler_params=pltpu.CompilerParams(vmem_limit_bytes=8 << 20),
        cost_estimate=pl.CostEstimate(
            flops=8 * freqs * count * rows * recv * cells,
            bytes_accessed=4 * freqs * recv * cells,
            transcendentals=0,
        ),
        name="adjoint_rest",
    )(scalars, *in_vmem_all([green, base, *pieces]))


def in_vmem(kernel, scalars, operands, shape, dtype, name):
    return pl.pallas_call(
        kernel,
        in_specs=[pl.BlockSpec(memory_space=pltpu.SMEM)]
        + [pl.BlockSpec(memory_space=pltpu.VMEM)] * len(operands),
        out_specs=pl.BlockSpec(memory_space=pltpu.VMEM),
        out_shape=pltpu.VMEM(shape, dtype),
        compiler_params=pltpu.CompilerParams(vmem_limit_bytes=4 << 20),
        cost_estimate=pl.CostEstimate(
            flops=4 * sum(operand.size for operand in operands[1:]),
            bytes_accessed=4 * sum(operand.size for operand in operands[1:]),
            transcendentals=0,
        ),
        name=name,
    )(scalars, *in_vmem_all(operands))


OWN, OWN_Y, NEAR, NEAR_Y, MID, MID_Y, FAR, FAR_Y, MIDDLE = range(9)
RECEIVED = -1


def weigh_kernel(terms, first, last, scalar_ref, adjoint_ref, *refs):
    refs, out_ref = list(refs[:-1]), refs[-1]
    sums = 0.0 if first else refs.pop()[...]
    freqs, parts, _, cells = refs[0].shape
    middle = scalar_ref[MIDDLE] != 0
    for number, choices in terms:
        field_refs = [refs.pop(0) for _ in range(choices)]
        block = refs.pop(0) if number == RECEIVED else adjoint_ref.at[:, :, scalar_ref[number]]
        for freq in range(freqs):
            for part in range(parts):
                field = field_refs[0][freq, part].astype(jnp.float32)
                if choices == 2:
                    other = field_refs[1][freq, part].astype(jnp.float32)
                    field = jnp.where(middle, other, field)
                if number in (FAR_Y, RECEIVED):
                    field = jnp.where(middle, field, 0.0)
                products = block[freq, part].astype(jnp.float32) * field
                sums = sums + jnp.sum(products.reshape(-1, 8, cells), axis=0)
    out_ref[...] = jnp.sum(sums, axis=0, keepdims=True) if last else sums


def pick_kernel(scalar_ref, first_ref, second_ref, out_ref):
    @pl.when(scalar_ref[MIDDLE] == 0)
    def _():
        out_ref[...] = first_ref[...]

    @pl.when(scalar_ref[MIDDLE] != 0)
    def _():
        out_ref[...] = second_ref[...]


def box_shards(records, active, green, background):
    freqs, _, _, cells = green.shape
    along_y = [(r, r ^ 1) for r in range(8)]
    z_pairs = [(r, r ^ 2) for r in range(8)]
    z_middle = [(t * 8 + r, t * 8 + (r ^ 6)) for t in range(4) for r in range(2, 6)]
    z_middle += [(t * 8 + r, (t ^ 1) * 8 + r) for t in range(4) for r in (0, 1, 6, 7)]
    z_middle_x = [(t * 8 + r, t * 8 + (r ^ 6)) for t in range(4) for r in range(2, 6)]
    z_middle_x += [(t * 8 + r, (t ^ 2) * 8 + r) for t in range(4) for r in (0, 1, 6, 7)]
    core = [(t, t ^ 1) for t in range(4)]
    along_x = [(t, t ^ 2) for t in range(4)]
    send, tie = lax.ppermute, lax.optimization_barrier

    me_tx, me_rx = lax.axis_index("tx"), lax.axis_index("rx")
    me_z, me_y = me_rx // 2, me_rx % 2
    lower = me_z < 2
    mid_z, far_z = jnp.where(lower, 2, 1), jnp.where(lower, 3, 0)
    scalars = jnp.stack(
        [(z ^ me_tx) * 2 + y for z in (me_z, me_z ^ 1, mid_z, far_z) for y in (me_y, 1 - me_y)]
        + [(me_z == 1) | (me_z == 2)]
    ).astype(jnp.int32)

    own = background.transpose(1, 2, 0, 3)
    own, scalars, records = tie((own, scalars, records))
    spectra = spectra_of(records, active, freqs)
    spectra_x = send(spectra, "tx", along_x)
    spectra_core = send(spectra, "tx", core)
    near = send(own, "rx", z_pairs)
    across = send(own, ("tx", "rx"), z_middle)
    own_y = send(own, "rx", along_y)
    near, across, own_y, spectra = tie((near, across, own_y, spectra))

    across_out = send(across, "rx", z_pairs)
    far = send(near, ("tx", "rx"), z_middle_x)
    near_y = send(near, "rx", along_y)

    spectra_both = send(spectra_x, "tx", core)
    adjoint, green_kept = adjoint_of([spectra, spectra_core], green, 4)
    adjoint, partial = adjoint_rest(scalars, [spectra_x, spectra_both], green_kept, adjoint)
    adjoint = adjoint.reshape((freqs, 2, 8) + own.shape[2:])

    swap = in_vmem(pick_kernel, scalars, [partial, far], own.shape, own.dtype, "pick")
    swap = send(swap, "rx", z_pairs)
    far_both = send(near_y, ("tx", "rx"), z_middle_x)
    mid = in_vmem(pick_kernel, scalars, [across_out, across], own.shape, own.dtype, "pick")
    mid_y = send(mid, "rx", along_y)

    sums = in_vmem(
        functools.partial(weigh_kernel, ((OWN, 1), (OWN_Y, 1), (NEAR, 1), (NEAR_Y, 1), (MID, 1)), True, False),
        scalars,
        [adjoint, own, own_y, near, near_y, mid],
        (8, cells),
        jnp.float32,
        "weigh",
    )
    sums = in_vmem(
        functools.partial(weigh_kernel, ((MID_Y, 1), (FAR, 2), (FAR_Y, 1), (RECEIVED, 1)), False, True),
        scalars,
        [adjoint, mid_y, swap, far, far_both, far_both, swap, sums],
        (1, cells),
        jnp.float32,
        "weigh",
    )
    sums = sums.reshape(cells)
    for bits in ((3, 2, 1), (4,)):
        sums = sums + sum(send(sums, "rx", [(r, r ^ bit) for r in range(8)]) for bit in bits)
    return sums


def plain_shards(records, active, green, background):
    freqs = green.shape[0]
    spectra = spectra_of(records, active, freqs)
    pieces = lax.all_gather(spectra, "tx", axis=0)
    adjoint, _ = adjoint_of([pieces[t] for t in range(pieces.shape[0])], green, pieces.shape[0])
    freqs, _, groups, rows, cells = adjoint.shape
    adjoint = adjoint.reshape(freqs, 2, groups * rows, cells)
    fields = lax.all_gather(background, "rx", axis=0, tiled=True)
    fields = fields.transpose(1, 2, 0, 3).astype(jnp.float32)
    return lax.psum(jnp.sum(adjoint * fields, axis=(0, 1, 2)), "rx")


def solution(mesh):
    placed = (
        P(None, "tx", "rx"),
        P("tx", "rx"),
        P(None, None, "rx", "tx"),
        P("rx", None, None, "tx"),
    )
    body = box_shards if (mesh.shape["tx"], mesh.shape["rx"]) == (4, 8) else plain_shards
    return jax.shard_map(body, mesh=mesh, in_specs=placed, out_specs=P("tx"), check_vma=False)
```

```python
import functools

import jax
import jax.numpy as jnp
import numpy as np
from jax import lax
from jax.experimental import pallas as pl
from jax.experimental.pallas import tpu as pltpu
from jax.sharding import PartitionSpec as P

ROWS = 16


def spread_table(gate_count, freq_count):
    gates = np.arange(gate_count, dtype=np.float32)
    freqs = np.arange(freq_count, dtype=np.float32)
    phases = (
        np.float32(np.pi)
        * (np.float32(2) * gates[None, :] + np.float32(1))
        * (np.float32(1) + np.float32(3) * freqs[:, None])
        / np.float32(2 * gate_count)
    )
    scale = np.sqrt(np.float32(2.0 / gate_count))
    table = np.stack([np.cos(phases) * scale, -np.sin(phases) * scale], axis=1)
    table = table.reshape(2 * freq_count, gate_count).astype(jnp.bfloat16).astype(np.float32)
    return np.kron(table, np.eye(ROWS, dtype=np.float32)).astype(jnp.bfloat16)


def spectra_kernel(table_hbm, active_hbm, records_hbm, out_ref, table_ref, active_ref, records_ref, mask_ref, arrived):
    gates, trans, recv = records_ref.shape
    blocks, channels = active_ref.shape[0], out_ref.shape[0]
    steps = trans // ROWS

    def rows(step):
        return pl.ds(pl.multiple_of(step * ROWS, ROWS), ROWS)

    def fetch(step):
        return pltpu.make_async_copy(
            records_hbm.at[:, rows(step)], records_ref.at[:, rows(step)], arrived.at[step]
        )

    fetch_active = pltpu.make_async_copy(active_hbm, active_ref, arrived.at[steps])
    fetch_table = pltpu.make_async_copy(table_hbm, table_ref, arrived.at[steps + 1])
    fetch_active.start()
    fetch_table.start()
    for step in range(steps):
        fetch(step).start()

    fetch_active.wait()
    block_of = lax.broadcasted_iota(jnp.int32, (blocks, recv), 1) // (recv // blocks)
    spread = (block_of == lax.broadcasted_iota(jnp.int32, (blocks, recv), 0)).astype(jnp.float32)
    mask_ref[...] = lax.dot_general(
        active_ref[...].astype(jnp.float32),
        spread,
        (((0,), (0,)), ((), ())),
        preferred_element_type=jnp.float32,
    )
    fetch_table.wait()

    @pl.loop(0, steps)
    def _(step):
        fetch(step).wait()
        flat = records_ref[:, rows(step)].reshape(gates * ROWS, recv)
        sums = jnp.dot(table_ref[...], flat, preferred_element_type=jnp.float32)
        masked = sums.reshape(channels, ROWS, recv) * mask_ref[rows(step)][None]
        out_ref[:, rows(step)] = masked.astype(out_ref.dtype)


def in_hbm(array):
    return pltpu.with_memory_space_constraint(array, pltpu.HBM)


def spectra_of(records, active, freq_count):
    gates, trans, recv = records.shape
    blocks = active.shape[1]
    channels = 2 * freq_count
    table = jnp.asarray(spread_table(gates, freq_count))
    return pl.pallas_call(
        spectra_kernel,
        in_specs=[pl.BlockSpec(memory_space=pltpu.HBM)] * 3,
        out_specs=pl.BlockSpec(memory_space=pltpu.VMEM),
        out_shape=pltpu.VMEM((channels, trans, recv), jnp.bfloat16),
        scratch_shapes=[
            pltpu.VMEM(table.shape, table.dtype),
            pltpu.VMEM((blocks, trans), jnp.int32),
            pltpu.VMEM(records.shape, records.dtype),
            pltpu.VMEM((trans, recv), jnp.float32),
            pltpu.SemaphoreType.DMA((trans // ROWS + 2,)),
        ],
        compiler_params=pltpu.CompilerParams(vmem_limit_bytes=16 << 20),
        cost_estimate=pl.CostEstimate(
            flops=2 * channels * ROWS * gates * trans * recv,
            bytes_accessed=2 * (gates + channels) * trans * recv,
            transcendentals=0,
        ),
        name="spectra",
    )(in_hbm(table), in_hbm(active.T), in_hbm(records))


def complex_rows(spectra_refs, freq):
    real = jnp.concatenate([ref[freq, 0] for ref in spectra_refs], axis=0)
    imag = jnp.concatenate([ref[freq, 1] for ref in spectra_refs], axis=0)
    return jnp.concatenate(
        [jnp.concatenate([real, -imag], axis=1), jnp.concatenate([-imag, -real], axis=1)], axis=0
    )


def adjoint_kernel(count, green_hbm_ref, *refs):
    spectra_refs, (out_ref, green_ref, arrived) = refs[:count], refs[count:]
    freqs, _, rows, _ = spectra_refs[0].shape

    def fetch(freq):
        return pltpu.make_async_copy(green_hbm_ref.at[freq], green_ref.at[freq], arrived.at[freq])

    for freq in range(freqs):
        fetch(freq).start()

    @pl.loop(0, freqs)
    def _(freq):
        fetch(freq).wait()
        left = complex_rows(spectra_refs, freq)
        sums = jnp.dot(left, green_ref[freq], preferred_element_type=jnp.float32)
        out_ref[freq, :, :count] = sums.reshape(2, count, rows, -1)


def adjoint_rest_kernel(count, half, scalar_ref, green_ref, base_ref, *refs):
    spectra_refs, (out_ref, block_ref) = refs[:count], refs[count:]
    del base_ref
    freqs, _, rows, _ = spectra_refs[0].shape
    block = scalar_ref[FAR_Y]
    group, first = block // 2, pl.multiple_of((block % 2) * half, half)

    @pl.loop(0, freqs)
    def _(freq):
        left = complex_rows(spectra_refs, freq)
        sums = jnp.dot(left, green_ref[freq], preferred_element_type=jnp.float32)
        out_ref[freq, :, count:] = sums.reshape(2, count, rows, -1)
        block_ref[freq] = out_ref[freq, :, group, pl.ds(first, half)].astype(block_ref.dtype)


def in_vmem_all(arrays):
    return [pltpu.with_memory_space_constraint(array, pltpu.VMEM) for array in arrays]


def adjoint_of(pieces, green, groups):
    freqs, _, recv, cells = green.shape
    rows, count = pieces[0].shape[1], len(pieces)
    green = green.reshape(freqs, 2 * recv, cells)
    return pl.pallas_call(
        functools.partial(adjoint_kernel, count),
        in_specs=[pl.BlockSpec(memory_space=pltpu.HBM)]
        + [pl.BlockSpec(memory_space=pltpu.VMEM)] * count,
        out_specs=[pl.BlockSpec(memory_space=pltpu.VMEM)] * 2,
        out_shape=[
            pltpu.VMEM((freqs, 2, groups, rows, cells), jnp.float32),
            pltpu.VMEM(green.shape, green.dtype),
        ],
        scratch_shapes=[pltpu.SemaphoreType.DMA((freqs,))],
        compiler_params=pltpu.CompilerParams(vmem_limit_bytes=4 * count << 20),
        cost_estimate=pl.CostEstimate(
            flops=8 * freqs * count * rows * recv * cells,
            bytes_accessed=4 * freqs * recv * cells,
            transcendentals=0,
        ),
        name="adjoint",
    )(in_hbm(green), *in_vmem_all([piece.reshape(freqs, 2, rows, recv) for piece in pieces]))


def adjoint_rest(scalars, pieces, green, base):
    freqs, _, groups, rows, cells = base.shape
    recv, count = pieces[0].shape[2], len(pieces)
    half = rows // 2
    pieces = [piece.reshape(freqs, 2, rows, recv) for piece in pieces]
    return pl.pallas_call(
        functools.partial(adjoint_rest_kernel, count, half),
        in_specs=[pl.BlockSpec(memory_space=pltpu.SMEM)]
        + [pl.BlockSpec(memory_space=pltpu.VMEM)] * (count + 2),
        out_specs=[pl.BlockSpec(memory_space=pltpu.VMEM)] * 2,
        out_shape=[
            pltpu.VMEM(base.shape, base.dtype),
            pltpu.VMEM((freqs, 2, half, cells), jnp.bfloat16),
        ],
        input_output_aliases={2: 0},
        compiler_params=pltpu.CompilerParams(vmem_limit_bytes=8 << 20),
        cost_estimate=pl.CostEstimate(
            flops=8 * freqs * count * rows * recv * cells,
            bytes_accessed=4 * freqs * recv * cells,
            transcendentals=0,
        ),
        name="adjoint_rest",
    )(scalars, *in_vmem_all([green, base, *pieces]))


def in_vmem(kernel, scalars, operands, shape, dtype, name):
    return pl.pallas_call(
        kernel,
        in_specs=[pl.BlockSpec(memory_space=pltpu.SMEM)]
        + [pl.BlockSpec(memory_space=pltpu.VMEM)] * len(operands),
        out_specs=pl.BlockSpec(memory_space=pltpu.VMEM),
        out_shape=pltpu.VMEM(shape, dtype),
        compiler_params=pltpu.CompilerParams(vmem_limit_bytes=4 << 20),
        cost_estimate=pl.CostEstimate(
            flops=4 * sum(operand.size for operand in operands[1:]),
            bytes_accessed=4 * sum(operand.size for operand in operands[1:]),
            transcendentals=0,
        ),
        name=name,
    )(scalars, *in_vmem_all(operands))


OWN, OWN_Y, NEAR, NEAR_Y, MID, MID_Y, FAR, FAR_Y, MIDDLE = range(9)
RECEIVED = -1


def weigh_kernel(terms, first, last, scalar_ref, adjoint_ref, *refs):
    refs, out_ref = list(refs[:-1]), refs[-1]
    sums = 0.0 if first else refs.pop()[...]
    freqs, parts, _, cells = refs[0].shape
    middle = scalar_ref[MIDDLE] != 0
    for number, choices in terms:
        field_refs = [refs.pop(0) for _ in range(choices)]
        block = refs.pop(0) if number == RECEIVED else adjoint_ref.at[:, :, scalar_ref[number]]
        for freq in range(freqs):
            for part in range(parts):
                field = field_refs[0][freq, part].astype(jnp.float32)
                if choices == 2:
                    other = field_refs[1][freq, part].astype(jnp.float32)
                    field = jnp.where(middle, other, field)
                if number in (FAR_Y, RECEIVED):
                    field = jnp.where(middle, field, 0.0)
                products = block[freq, part].astype(jnp.float32) * field
                sums = sums + jnp.sum(products.reshape(-1, 8, cells), axis=0)
    out_ref[...] = jnp.sum(sums, axis=0, keepdims=True) if last else sums


def pick_kernel(scalar_ref, first_ref, second_ref, out_ref):
    @pl.when(scalar_ref[MIDDLE] == 0)
    def _():
        out_ref[...] = first_ref[...]

    @pl.when(scalar_ref[MIDDLE] != 0)
    def _():
        out_ref[...] = second_ref[...]


def box_shards(records, active, green, background):
    freqs, _, _, cells = green.shape
    along_y = [(r, r ^ 1) for r in range(8)]
    z_pairs = [(r, r ^ 2) for r in range(8)]
    z_middle = [(t * 8 + r, t * 8 + (r ^ 6)) for t in range(4) for r in range(2, 6)]
    z_middle += [(t * 8 + r, (t ^ 1) * 8 + r) for t in range(4) for r in (0, 1, 6, 7)]
    z_middle_x = [(t * 8 + r, t * 8 + (r ^ 6)) for t in range(4) for r in range(2, 6)]
    z_middle_x += [(t * 8 + r, (t ^ 2) * 8 + r) for t in range(4) for r in (0, 1, 6, 7)]
    core = [(t, t ^ 1) for t in range(4)]
    along_x = [(t, t ^ 2) for t in range(4)]
    send, tie = lax.ppermute, lax.optimization_barrier

    me_tx, me_rx = lax.axis_index("tx"), lax.axis_index("rx")
    me_z, me_y = me_rx // 2, me_rx % 2
    lower = me_z < 2
    middle = (me_z == 1) | (me_z == 2)
    mid_z, far_z = jnp.where(lower, 2, 1), jnp.where(lower, 3, 0)
    scalars = jnp.stack(
        [(z ^ me_tx) * 2 + y for z in (me_z, me_z ^ 1, mid_z, far_z) for y in (me_y, 1 - me_y)]
        + [(me_z == 1) | (me_z == 2)]
    ).astype(jnp.int32)

    own = background.transpose(1, 2, 0, 3)
    own, scalars, records = tie((own, scalars, records))
    spectra = spectra_of(records, active, freqs)
    spectra_x = send(spectra, "tx", along_x)
    spectra_core = send(spectra, "tx", core)
    near = send(own, "rx", z_pairs)
    across = send(own, ("tx", "rx"), z_middle)
    own_y = send(own, "rx", along_y)
    near, across, own_y, spectra = tie((near, across, own_y, spectra))

    across_out = send(across, "rx", z_pairs)
    far = send(near, ("tx", "rx"), z_middle_x)
    near_y = send(near, "rx", along_y)

    spectra_both = send(spectra_x, "tx", core)
    adjoint, green_kept = adjoint_of([spectra, spectra_core], green, 4)
    adjoint, partial = adjoint_rest(scalars, [spectra_x, spectra_both], green_kept, adjoint)
    adjoint = adjoint.reshape((freqs, 2, 8) + own.shape[2:])

    swap = jnp.where(middle, far, partial)
    swap = send(swap, "rx", z_pairs)
    far_both = send(near_y, ("tx", "rx"), z_middle)
    mid = jnp.where(middle, across, across_out)
    mid_y = send(mid, "rx", along_y)

    sums = in_vmem(
        functools.partial(weigh_kernel, ((OWN, 1), (OWN_Y, 1), (NEAR, 1), (NEAR_Y, 1), (MID, 1)), True, False),
        scalars,
        [adjoint, own, own_y, near, near_y, mid],
        (8, cells),
        jnp.float32,
        "weigh",
    )
    sums = in_vmem(
        functools.partial(weigh_kernel, ((MID_Y, 1), (FAR, 2), (FAR_Y, 1), (RECEIVED, 1)), False, True),
        scalars,
        [adjoint, mid_y, swap, far, far_both, far_both, swap, sums],
        (1, cells),
        jnp.float32,
        "weigh",
    )
    sums = sums.reshape(cells)
    for bits in ((3, 2, 1), (4,)):
        sums = sums + sum(send(sums, "rx", [(r, r ^ bit) for r in range(8)]) for bit in bits)
    return sums


def plain_shards(records, active, green, background):
    freqs = green.shape[0]
    spectra = spectra_of(records, active, freqs)
    pieces = lax.all_gather(spectra, "tx", axis=0)
    adjoint, _ = adjoint_of([pieces[t] for t in range(pieces.shape[0])], green, pieces.shape[0])
    freqs, _, groups, rows, cells = adjoint.shape
    adjoint = adjoint.reshape(freqs, 2, groups * rows, cells)
    fields = lax.all_gather(background, "rx", axis=0, tiled=True)
    fields = fields.transpose(1, 2, 0, 3).astype(jnp.float32)
    return lax.psum(jnp.sum(adjoint * fields, axis=(0, 1, 2)), "rx")


def solution(mesh):
    placed = (
        P(None, "tx", "rx"),
        P("tx", "rx"),
        P(None, None, "rx", "tx"),
        P("rx", None, None, "tx"),
    )
    body = box_shards if (mesh.shape["tx"], mesh.shape["rx"]) == (4, 8) else plain_shards
    return jax.shard_map(body, mesh=mesh, in_specs=placed, out_specs=P("tx"), check_vma=False)
```

```python
import functools

import jax
import jax.numpy as jnp
import numpy as np
from jax import lax
from jax.experimental import pallas as pl
from jax.experimental.pallas import tpu as pltpu
from jax.sharding import PartitionSpec as P

ROWS = 16


def spread_table(gate_count, freq_count):
    gates = np.arange(gate_count, dtype=np.float32)
    freqs = np.arange(freq_count, dtype=np.float32)
    phases = (
        np.float32(np.pi)
        * (np.float32(2) * gates[None, :] + np.float32(1))
        * (np.float32(1) + np.float32(3) * freqs[:, None])
        / np.float32(2 * gate_count)
    )
    scale = np.sqrt(np.float32(2.0 / gate_count))
    table = np.stack([np.cos(phases) * scale, -np.sin(phases) * scale], axis=1)
    table = table.reshape(2 * freq_count, gate_count).astype(jnp.bfloat16).astype(np.float32)
    return np.kron(table, np.eye(ROWS, dtype=np.float32)).astype(jnp.bfloat16)


def spectra_kernel(table_hbm, active_hbm, records_hbm, out_ref, table_ref, active_ref, records_ref, mask_ref, arrived):
    gates, trans, recv = records_ref.shape
    blocks, channels = active_ref.shape[0], out_ref.shape[0]
    steps = trans // ROWS

    def rows(step):
        return pl.ds(pl.multiple_of(step * ROWS, ROWS), ROWS)

    def fetch(step):
        return pltpu.make_async_copy(
            records_hbm.at[:, rows(step)], records_ref.at[:, rows(step)], arrived.at[step]
        )

    fetch_active = pltpu.make_async_copy(active_hbm, active_ref, arrived.at[steps])
    fetch_table = pltpu.make_async_copy(table_hbm, table_ref, arrived.at[steps + 1])
    fetch_active.start()
    fetch_table.start()
    for step in range(steps):
        fetch(step).start()

    fetch_active.wait()
    block_of = lax.broadcasted_iota(jnp.int32, (blocks, recv), 1) // (recv // blocks)
    spread = (block_of == lax.broadcasted_iota(jnp.int32, (blocks, recv), 0)).astype(jnp.float32)
    mask_ref[...] = lax.dot_general(
        active_ref[...].astype(jnp.float32),
        spread,
        (((0,), (0,)), ((), ())),
        preferred_element_type=jnp.float32,
    )
    fetch_table.wait()

    @pl.loop(0, steps)
    def _(step):
        fetch(step).wait()
        flat = records_ref[:, rows(step)].reshape(gates * ROWS, recv)
        sums = jnp.dot(table_ref[...], flat, preferred_element_type=jnp.float32)
        masked = sums.reshape(channels, ROWS, recv) * mask_ref[rows(step)][None]
        out_ref[:, rows(step)] = masked.astype(out_ref.dtype)


def in_hbm(array):
    return pltpu.with_memory_space_constraint(array, pltpu.HBM)


def spectra_of(records, active, freq_count):
    gates, trans, recv = records.shape
    blocks = active.shape[1]
    channels = 2 * freq_count
    table = jnp.asarray(spread_table(gates, freq_count))
    return pl.pallas_call(
        spectra_kernel,
        in_specs=[pl.BlockSpec(memory_space=pltpu.HBM)] * 3,
        out_specs=pl.BlockSpec(memory_space=pltpu.VMEM),
        out_shape=pltpu.VMEM((channels, trans, recv), jnp.bfloat16),
        scratch_shapes=[
            pltpu.VMEM(table.shape, table.dtype),
            pltpu.VMEM((blocks, trans), jnp.int32),
            pltpu.VMEM(records.shape, records.dtype),
            pltpu.VMEM((trans, recv), jnp.float32),
            pltpu.SemaphoreType.DMA((trans // ROWS + 2,)),
        ],
        compiler_params=pltpu.CompilerParams(vmem_limit_bytes=16 << 20),
        cost_estimate=pl.CostEstimate(
            flops=2 * channels * ROWS * gates * trans * recv,
            bytes_accessed=2 * (gates + channels) * trans * recv,
            transcendentals=0,
        ),
        name="spectra",
    )(in_hbm(table), in_hbm(active.T), in_hbm(records))


def complex_rows(spectra_refs, freq):
    real = jnp.concatenate([ref[freq, 0] for ref in spectra_refs], axis=0)
    imag = jnp.concatenate([ref[freq, 1] for ref in spectra_refs], axis=0)
    return jnp.concatenate(
        [jnp.concatenate([real, -imag], axis=1), jnp.concatenate([-imag, -real], axis=1)], axis=0
    )


def adjoint_kernel(count, green_hbm_ref, *refs):
    spectra_refs, (out_ref, green_ref, arrived) = refs[:count], refs[count:]
    freqs, _, rows, _ = spectra_refs[0].shape

    def fetch(freq):
        return pltpu.make_async_copy(green_hbm_ref.at[freq], green_ref.at[freq], arrived.at[freq])

    for freq in range(freqs):
        fetch(freq).start()

    @pl.loop(0, freqs)
    def _(freq):
        fetch(freq).wait()
        left = complex_rows(spectra_refs, freq)
        sums = jnp.dot(left, green_ref[freq], preferred_element_type=jnp.float32)
        out_ref[freq, :, :count] = sums.reshape(2, count, rows, -1)


def adjoint_rest_kernel(count, half, scalar_ref, green_ref, base_ref, *refs):
    spectra_refs, (out_ref, block_ref) = refs[:count], refs[count:]
    del base_ref
    freqs, _, rows, _ = spectra_refs[0].shape
    block = scalar_ref[FAR_Y]
    group, first = block // 2, pl.multiple_of((block % 2) * half, half)

    @pl.loop(0, freqs)
    def _(freq):
        left = complex_rows(spectra_refs, freq)
        sums = jnp.dot(left, green_ref[freq], preferred_element_type=jnp.float32)
        out_ref[freq, :, count:] = sums.reshape(2, count, rows, -1)
        block_ref[freq] = out_ref[freq, :, group, pl.ds(first, half)].astype(block_ref.dtype)


def in_vmem_all(arrays):
    return [pltpu.with_memory_space_constraint(array, pltpu.VMEM) for array in arrays]


def adjoint_of(pieces, green, groups):
    freqs, _, recv, cells = green.shape
    rows, count = pieces[0].shape[1], len(pieces)
    green = green.reshape(freqs, 2 * recv, cells)
    return pl.pallas_call(
        functools.partial(adjoint_kernel, count),
        in_specs=[pl.BlockSpec(memory_space=pltpu.HBM)]
        + [pl.BlockSpec(memory_space=pltpu.VMEM)] * count,
        out_specs=[pl.BlockSpec(memory_space=pltpu.VMEM)] * 2,
        out_shape=[
            pltpu.VMEM((freqs, 2, groups, rows, cells), jnp.float32),
            pltpu.VMEM(green.shape, green.dtype),
        ],
        scratch_shapes=[pltpu.SemaphoreType.DMA((freqs,))],
        compiler_params=pltpu.CompilerParams(vmem_limit_bytes=4 * count << 20),
        cost_estimate=pl.CostEstimate(
            flops=8 * freqs * count * rows * recv * cells,
            bytes_accessed=4 * freqs * recv * cells,
            transcendentals=0,
        ),
        name="adjoint",
    )(in_hbm(green), *in_vmem_all([piece.reshape(freqs, 2, rows, recv) for piece in pieces]))


def adjoint_rest(scalars, pieces, green, base):
    freqs, _, groups, rows, cells = base.shape
    recv, count = pieces[0].shape[2], len(pieces)
    half = rows // 2
    pieces = [piece.reshape(freqs, 2, rows, recv) for piece in pieces]
    return pl.pallas_call(
        functools.partial(adjoint_rest_kernel, count, half),
        in_specs=[pl.BlockSpec(memory_space=pltpu.SMEM)]
        + [pl.BlockSpec(memory_space=pltpu.VMEM)] * (count + 2),
        out_specs=[pl.BlockSpec(memory_space=pltpu.VMEM)] * 2,
        out_shape=[
            pltpu.VMEM(base.shape, base.dtype),
            pltpu.VMEM((freqs, 2, half, cells), jnp.bfloat16),
        ],
        input_output_aliases={2: 0},
        compiler_params=pltpu.CompilerParams(vmem_limit_bytes=8 << 20),
        cost_estimate=pl.CostEstimate(
            flops=8 * freqs * count * rows * recv * cells,
            bytes_accessed=4 * freqs * recv * cells,
            transcendentals=0,
        ),
        name="adjoint_rest",
    )(scalars, *in_vmem_all([green, base, *pieces]))


def in_vmem(kernel, scalars, operands, shape, dtype, name):
    return pl.pallas_call(
        kernel,
        in_specs=[pl.BlockSpec(memory_space=pltpu.SMEM)]
        + [pl.BlockSpec(memory_space=pltpu.VMEM)] * len(operands),
        out_specs=pl.BlockSpec(memory_space=pltpu.VMEM),
        out_shape=pltpu.VMEM(shape, dtype),
        compiler_params=pltpu.CompilerParams(vmem_limit_bytes=4 << 20),
        cost_estimate=pl.CostEstimate(
            flops=4 * sum(operand.size for operand in operands[1:]),
            bytes_accessed=4 * sum(operand.size for operand in operands[1:]),
            transcendentals=0,
        ),
        name=name,
    )(scalars, *in_vmem_all(operands))


OWN, OWN_Y, NEAR, NEAR_Y, MID, MID_Y, FAR, FAR_Y, MIDDLE = range(9)
RECEIVED = -1


def weigh_kernel(terms, first, last, scalar_ref, adjoint_ref, *refs):
    refs, out_ref = list(refs[:-1]), refs[-1]
    sums = 0.0 if first else refs.pop()[...]
    freqs, parts, _, cells = refs[0].shape
    middle = scalar_ref[MIDDLE] != 0
    for number, choices in terms:
        field_refs = [refs.pop(0) for _ in range(choices)]
        block = refs.pop(0) if number == RECEIVED else adjoint_ref.at[:, :, scalar_ref[number]]
        for freq in range(freqs):
            for part in range(parts):
                field = field_refs[0][freq, part].astype(jnp.float32)
                if choices == 2:
                    other = field_refs[1][freq, part].astype(jnp.float32)
                    field = jnp.where(middle, other, field)
                if number in (FAR_Y, RECEIVED):
                    field = jnp.where(middle, field, 0.0)
                products = block[freq, part].astype(jnp.float32) * field
                sums = sums + jnp.sum(products.reshape(-1, 8, cells), axis=0)
    out_ref[...] = jnp.sum(sums, axis=0, keepdims=True) if last else sums


def pick_kernel(scalar_ref, first_ref, second_ref, out_ref):
    @pl.when(scalar_ref[MIDDLE] == 0)
    def _():
        out_ref[...] = first_ref[...]

    @pl.when(scalar_ref[MIDDLE] != 0)
    def _():
        out_ref[...] = second_ref[...]


def box_shards(records, active, green, background):
    freqs, _, _, cells = green.shape
    along_y = [(r, r ^ 1) for r in range(8)]
    z_pairs = [(r, r ^ 2) for r in range(8)]
    z_middle = [(t * 8 + r, t * 8 + (r ^ 6)) for t in range(4) for r in range(2, 6)]
    z_middle += [(t * 8 + r, (t ^ 1) * 8 + r) for t in range(4) for r in (0, 1, 6, 7)]
    z_middle_x = [(t * 8 + r, t * 8 + (r ^ 6)) for t in range(4) for r in range(2, 6)]
    z_middle_x += [(t * 8 + r, (t ^ 2) * 8 + r) for t in range(4) for r in (0, 1, 6, 7)]
    core = [(t, t ^ 1) for t in range(4)]
    along_x = [(t, t ^ 2) for t in range(4)]
    send, tie = lax.ppermute, lax.optimization_barrier

    me_tx, me_rx = lax.axis_index("tx"), lax.axis_index("rx")
    me_z, me_y = me_rx // 2, me_rx % 2
    lower = me_z < 2
    middle = (me_z == 1) | (me_z == 2)
    mid_z, far_z = jnp.where(lower, 2, 1), jnp.where(lower, 3, 0)
    scalars = jnp.stack(
        [(z ^ me_tx) * 2 + y for z in (me_z, me_z ^ 1, mid_z, far_z) for y in (me_y, 1 - me_y)]
        + [(me_z == 1) | (me_z == 2)]
    ).astype(jnp.int32)

    own = background.transpose(1, 2, 0, 3)
    own, scalars, records = tie((own, scalars, records))
    spectra = spectra_of(records, active, freqs)
    spectra_x = send(spectra, "tx", along_x)
    spectra_core = send(spectra, "tx", core)
    near = send(own, "rx", z_pairs)
    across = send(own, ("tx", "rx"), z_middle)
    own_y = send(own, "rx", along_y)
    near, across, own_y, spectra = tie((near, across, own_y, spectra))

    across_out = send(across, "rx", z_pairs)
    far = send(near, ("tx", "rx"), z_middle_x)
    near_y = send(near, "rx", along_y)

    adjoint, green_kept = adjoint_of([spectra, spectra_core], green, 4)
    spectra_both = send(spectra_x, "tx", core)
    adjoint, partial = adjoint_rest(scalars, [spectra_x, spectra_both], green_kept, adjoint)
    adjoint = adjoint.reshape((freqs, 2, 8) + own.shape[2:])

    swap = jnp.where(middle, far, partial)
    swap = send(swap, "rx", z_pairs)
    far_both = send(near_y, ("tx", "rx"), z_middle)
    mid = jnp.where(middle, across, across_out)
    mid_y = send(mid, "rx", along_y)

    sums = in_vmem(
        functools.partial(weigh_kernel, ((OWN, 1), (OWN_Y, 1), (NEAR, 1), (NEAR_Y, 1), (MID, 1)), True, False),
        scalars,
        [adjoint, own, own_y, near, near_y, mid],
        (8, cells),
        jnp.float32,
        "weigh",
    )
    sums = in_vmem(
        functools.partial(weigh_kernel, ((MID_Y, 1), (FAR, 2), (FAR_Y, 1), (RECEIVED, 1)), False, True),
        scalars,
        [adjoint, mid_y, swap, far, far_both, far_both, swap, sums],
        (1, cells),
        jnp.float32,
        "weigh",
    )
    sums = sums.reshape(cells)
    for bits in ((3, 2, 1), (4,)):
        sums = sums + sum(send(sums, "rx", [(r, r ^ bit) for r in range(8)]) for bit in bits)
    return sums


def plain_shards(records, active, green, background):
    freqs = green.shape[0]
    spectra = spectra_of(records, active, freqs)
    pieces = lax.all_gather(spectra, "tx", axis=0)
    adjoint, _ = adjoint_of([pieces[t] for t in range(pieces.shape[0])], green, pieces.shape[0])
    freqs, _, groups, rows, cells = adjoint.shape
    adjoint = adjoint.reshape(freqs, 2, groups * rows, cells)
    fields = lax.all_gather(background, "rx", axis=0, tiled=True)
    fields = fields.transpose(1, 2, 0, 3).astype(jnp.float32)
    return lax.psum(jnp.sum(adjoint * fields, axis=(0, 1, 2)), "rx")


def solution(mesh):
    placed = (
        P(None, "tx", "rx"),
        P("tx", "rx"),
        P(None, None, "rx", "tx"),
        P("rx", None, None, "tx"),
    )
    body = box_shards if (mesh.shape["tx"], mesh.shape["rx"]) == (4, 8) else plain_shards
    return jax.shard_map(body, mesh=mesh, in_specs=placed, out_specs=P("tx"), check_vma=False)
```

```python
import functools

import jax
import jax.numpy as jnp
import numpy as np
from jax import lax
from jax.experimental import pallas as pl
from jax.experimental.pallas import tpu as pltpu
from jax.sharding import PartitionSpec as P

ROWS = 16


def spread_table(gate_count, freq_count):
    gates = np.arange(gate_count, dtype=np.float32)
    freqs = np.arange(freq_count, dtype=np.float32)
    phases = (
        np.float32(np.pi)
        * (np.float32(2) * gates[None, :] + np.float32(1))
        * (np.float32(1) + np.float32(3) * freqs[:, None])
        / np.float32(2 * gate_count)
    )
    scale = np.sqrt(np.float32(2.0 / gate_count))
    table = np.stack([np.cos(phases) * scale, -np.sin(phases) * scale], axis=1)
    table = table.reshape(2 * freq_count, gate_count).astype(jnp.bfloat16).astype(np.float32)
    return np.kron(table, np.eye(ROWS, dtype=np.float32)).astype(jnp.bfloat16)


def spectra_kernel(table_hbm, active_hbm, records_hbm, out_ref, table_ref, active_ref, records_ref, mask_ref, arrived):
    gates, trans, recv = records_ref.shape
    blocks, channels = active_ref.shape[0], out_ref.shape[0]
    steps = trans // ROWS

    def rows(step):
        return pl.ds(pl.multiple_of(step * ROWS, ROWS), ROWS)

    def fetch(step):
        return pltpu.make_async_copy(
            records_hbm.at[:, rows(step)], records_ref.at[:, rows(step)], arrived.at[step]
        )

    fetch_active = pltpu.make_async_copy(active_hbm, active_ref, arrived.at[steps])
    fetch_table = pltpu.make_async_copy(table_hbm, table_ref, arrived.at[steps + 1])
    fetch_active.start()
    fetch_table.start()
    for step in range(steps):
        fetch(step).start()

    fetch_active.wait()
    block_of = lax.broadcasted_iota(jnp.int32, (blocks, recv), 1) // (recv // blocks)
    spread = (block_of == lax.broadcasted_iota(jnp.int32, (blocks, recv), 0)).astype(jnp.float32)
    mask_ref[...] = lax.dot_general(
        active_ref[...].astype(jnp.float32),
        spread,
        (((0,), (0,)), ((), ())),
        preferred_element_type=jnp.float32,
    )
    fetch_table.wait()

    @pl.loop(0, steps)
    def _(step):
        fetch(step).wait()
        flat = records_ref[:, rows(step)].reshape(gates * ROWS, recv)
        sums = jnp.dot(table_ref[...], flat, preferred_element_type=jnp.float32)
        masked = sums.reshape(channels, ROWS, recv) * mask_ref[rows(step)][None]
        out_ref[:, rows(step)] = masked.astype(out_ref.dtype)


def in_hbm(array):
    return pltpu.with_memory_space_constraint(array, pltpu.HBM)


def spectra_of(records, active, freq_count):
    gates, trans, recv = records.shape
    blocks = active.shape[1]
    channels = 2 * freq_count
    table = jnp.asarray(spread_table(gates, freq_count))
    return pl.pallas_call(
        spectra_kernel,
        in_specs=[pl.BlockSpec(memory_space=pltpu.HBM)] * 3,
        out_specs=pl.BlockSpec(memory_space=pltpu.VMEM),
        out_shape=pltpu.VMEM((channels, trans, recv), jnp.bfloat16),
        scratch_shapes=[
            pltpu.VMEM(table.shape, table.dtype),
            pltpu.VMEM((blocks, trans), jnp.int32),
            pltpu.VMEM(records.shape, records.dtype),
            pltpu.VMEM((trans, recv), jnp.float32),
            pltpu.SemaphoreType.DMA((trans // ROWS + 2,)),
        ],
        compiler_params=pltpu.CompilerParams(vmem_limit_bytes=16 << 20),
        cost_estimate=pl.CostEstimate(
            flops=2 * channels * ROWS * gates * trans * recv,
            bytes_accessed=2 * (gates + channels) * trans * recv,
            transcendentals=0,
        ),
        name="spectra",
    )(in_hbm(table), in_hbm(active.T), in_hbm(records))


def complex_rows(spectra_refs, freq):
    real = jnp.concatenate([ref[freq, 0] for ref in spectra_refs], axis=0)
    imag = jnp.concatenate([ref[freq, 1] for ref in spectra_refs], axis=0)
    return jnp.concatenate(
        [jnp.concatenate([real, -imag], axis=1), jnp.concatenate([-imag, -real], axis=1)], axis=0
    )


def adjoint_kernel(count, green_hbm_ref, *refs):
    spectra_refs, (out_ref, green_ref, arrived) = refs[:count], refs[count:]
    freqs, _, rows, _ = spectra_refs[0].shape

    def fetch(freq):
        return pltpu.make_async_copy(green_hbm_ref.at[freq], green_ref.at[freq], arrived.at[freq])

    for freq in range(freqs):
        fetch(freq).start()

    @pl.loop(0, freqs)
    def _(freq):
        fetch(freq).wait()
        left = complex_rows(spectra_refs, freq)
        sums = jnp.dot(left, green_ref[freq], preferred_element_type=jnp.float32)
        out_ref[freq, :, :count] = sums.reshape(2, count, rows, -1)


def adjoint_rest_kernel(count, half, scalar_ref, green_ref, base_ref, *refs):
    spectra_refs, (out_ref, block_ref) = refs[:count], refs[count:]
    del base_ref
    freqs, _, rows, _ = spectra_refs[0].shape
    block = scalar_ref[FAR_Y]
    group, first = block // 2, pl.multiple_of((block % 2) * half, half)

    @pl.loop(0, freqs)
    def _(freq):
        left = complex_rows(spectra_refs, freq)
        sums = jnp.dot(left, green_ref[freq], preferred_element_type=jnp.float32)
        out_ref[freq, :, count:] = sums.reshape(2, count, rows, -1)
        block_ref[freq] = out_ref[freq, :, group, pl.ds(first, half)].astype(block_ref.dtype)


def in_vmem_all(arrays):
    return [pltpu.with_memory_space_constraint(array, pltpu.VMEM) for array in arrays]


def adjoint_of(pieces, green, groups):
    freqs, _, recv, cells = green.shape
    rows, count = pieces[0].shape[1], len(pieces)
    green = green.reshape(freqs, 2 * recv, cells)
    return pl.pallas_call(
        functools.partial(adjoint_kernel, count),
        in_specs=[pl.BlockSpec(memory_space=pltpu.HBM)]
        + [pl.BlockSpec(memory_space=pltpu.VMEM)] * count,
        out_specs=[pl.BlockSpec(memory_space=pltpu.VMEM)] * 2,
        out_shape=[
            pltpu.VMEM((freqs, 2, groups, rows, cells), jnp.float32),
            pltpu.VMEM(green.shape, green.dtype),
        ],
        scratch_shapes=[pltpu.SemaphoreType.DMA((freqs,))],
        compiler_params=pltpu.CompilerParams(vmem_limit_bytes=4 * count << 20),
        cost_estimate=pl.CostEstimate(
            flops=8 * freqs * count * rows * recv * cells,
            bytes_accessed=4 * freqs * recv * cells,
            transcendentals=0,
        ),
        name="adjoint",
    )(in_hbm(green), *in_vmem_all([piece.reshape(freqs, 2, rows, recv) for piece in pieces]))


def adjoint_rest(scalars, pieces, green, base):
    freqs, _, groups, rows, cells = base.shape
    recv, count = pieces[0].shape[2], len(pieces)
    half = rows // 2
    pieces = [piece.reshape(freqs, 2, rows, recv) for piece in pieces]
    return pl.pallas_call(
        functools.partial(adjoint_rest_kernel, count, half),
        in_specs=[pl.BlockSpec(memory_space=pltpu.SMEM)]
        + [pl.BlockSpec(memory_space=pltpu.VMEM)] * (count + 2),
        out_specs=[pl.BlockSpec(memory_space=pltpu.VMEM)] * 2,
        out_shape=[
            pltpu.VMEM(base.shape, base.dtype),
            pltpu.VMEM((freqs, 2, half, cells), jnp.bfloat16),
        ],
        input_output_aliases={2: 0},
        compiler_params=pltpu.CompilerParams(vmem_limit_bytes=8 << 20),
        cost_estimate=pl.CostEstimate(
            flops=8 * freqs * count * rows * recv * cells,
            bytes_accessed=4 * freqs * recv * cells,
            transcendentals=0,
        ),
        name="adjoint_rest",
    )(scalars, *in_vmem_all([green, base, *pieces]))


def in_vmem(kernel, scalars, operands, shape, dtype, name):
    return pl.pallas_call(
        kernel,
        in_specs=[pl.BlockSpec(memory_space=pltpu.SMEM)]
        + [pl.BlockSpec(memory_space=pltpu.VMEM)] * len(operands),
        out_specs=pl.BlockSpec(memory_space=pltpu.VMEM),
        out_shape=pltpu.VMEM(shape, dtype),
        compiler_params=pltpu.CompilerParams(vmem_limit_bytes=4 << 20),
        cost_estimate=pl.CostEstimate(
            flops=4 * sum(operand.size for operand in operands[1:]),
            bytes_accessed=4 * sum(operand.size for operand in operands[1:]),
            transcendentals=0,
        ),
        name=name,
    )(scalars, *in_vmem_all(operands))


OWN, OWN_Y, NEAR, NEAR_Y, MID, MID_Y, FAR, FAR_Y, MIDDLE = range(9)
RECEIVED = -1


def weigh_kernel(terms, first, last, scalar_ref, adjoint_ref, *refs):
    refs, out_ref = list(refs[:-1]), refs[-1]
    sums = 0.0 if first else refs.pop()[...]
    freqs, parts, _, cells = refs[0].shape
    middle = scalar_ref[MIDDLE] != 0
    for number, choices in terms:
        field_refs = [refs.pop(0) for _ in range(choices)]
        block = refs.pop(0) if number == RECEIVED else adjoint_ref.at[:, :, scalar_ref[number]]
        for freq in range(freqs):
            for part in range(parts):
                field = field_refs[0][freq, part].astype(jnp.float32)
                if choices == 2:
                    other = field_refs[1][freq, part].astype(jnp.float32)
                    field = jnp.where(middle, other, field)
                if number in (FAR_Y, RECEIVED):
                    field = jnp.where(middle, field, 0.0)
                products = block[freq, part].astype(jnp.float32) * field
                sums = sums + jnp.sum(products.reshape(-1, 8, cells), axis=0)
    out_ref[...] = jnp.sum(sums, axis=0, keepdims=True) if last else sums


def pick_kernel(scalar_ref, first_ref, second_ref, out_ref):
    @pl.when(scalar_ref[MIDDLE] == 0)
    def _():
        out_ref[...] = first_ref[...]

    @pl.when(scalar_ref[MIDDLE] != 0)
    def _():
        out_ref[...] = second_ref[...]


def box_shards(records, active, green, background):
    freqs, _, _, cells = green.shape
    along_y = [(r, r ^ 1) for r in range(8)]
    z_pairs = [(r, r ^ 2) for r in range(8)]
    z_middle = [(t * 8 + r, t * 8 + (r ^ 6)) for t in range(4) for r in range(2, 6)]
    z_middle += [(t * 8 + r, (t ^ 1) * 8 + r) for t in range(4) for r in (0, 1, 6, 7)]
    z_middle_x = [(t * 8 + r, t * 8 + (r ^ 6)) for t in range(4) for r in range(2, 6)]
    z_middle_x += [(t * 8 + r, (t ^ 2) * 8 + r) for t in range(4) for r in (0, 1, 6, 7)]
    core = [(t, t ^ 1) for t in range(4)]
    along_x = [(t, t ^ 2) for t in range(4)]
    send, tie = lax.ppermute, lax.optimization_barrier

    me_tx, me_rx = lax.axis_index("tx"), lax.axis_index("rx")
    me_z, me_y = me_rx // 2, me_rx % 2
    lower = me_z < 2
    middle = (me_z == 1) | (me_z == 2)
    mid_z, far_z = jnp.where(lower, 2, 1), jnp.where(lower, 3, 0)
    scalars = jnp.stack(
        [(z ^ me_tx) * 2 + y for z in (me_z, me_z ^ 1, mid_z, far_z) for y in (me_y, 1 - me_y)]
        + [(me_z == 1) | (me_z == 2)]
    ).astype(jnp.int32)

    own = background.transpose(1, 2, 0, 3)
    own, scalars = tie((own, scalars))
    spectra = spectra_of(records, active, freqs)
    spectra_x = send(spectra, "tx", along_x)
    spectra_core = send(spectra, "tx", core)
    near = send(own, "rx", z_pairs)
    across = send(own, ("tx", "rx"), z_middle)
    own_y = send(own, "rx", along_y)
    near, across, own_y, spectra = tie((near, across, own_y, spectra))

    across_out = send(across, "rx", z_pairs)
    far = send(near, ("tx", "rx"), z_middle_x)
    near_y = send(near, "rx", along_y)

    spectra_both = send(spectra_x, "tx", core)
    adjoint, green_kept = adjoint_of([spectra, spectra_core], green, 4)
    adjoint, partial = adjoint_rest(scalars, [spectra_x, spectra_both], green_kept, adjoint)
    adjoint = adjoint.reshape((freqs, 2, 8) + own.shape[2:])

    swap = jnp.where(middle, far, partial)
    swap = send(swap, "rx", z_pairs)
    far_both = send(near_y, ("tx", "rx"), z_middle)
    mid = jnp.where(middle, across, across_out)
    mid_y = send(mid, "rx", along_y)

    sums = in_vmem(
        functools.partial(weigh_kernel, ((OWN, 1), (OWN_Y, 1), (NEAR, 1), (NEAR_Y, 1), (MID, 1)), True, False),
        scalars,
        [adjoint, own, own_y, near, near_y, mid],
        (8, cells),
        jnp.float32,
        "weigh",
    )
    sums = in_vmem(
        functools.partial(weigh_kernel, ((MID_Y, 1), (FAR, 2), (FAR_Y, 1), (RECEIVED, 1)), False, True),
        scalars,
        [adjoint, mid_y, swap, far, far_both, far_both, swap, sums],
        (1, cells),
        jnp.float32,
        "weigh",
    )
    sums = sums.reshape(cells)
    for bits in ((3, 2, 1), (4,)):
        sums = sums + sum(send(sums, "rx", [(r, r ^ bit) for r in range(8)]) for bit in bits)
    return sums


def plain_shards(records, active, green, background):
    freqs = green.shape[0]
    spectra = spectra_of(records, active, freqs)
    pieces = lax.all_gather(spectra, "tx", axis=0)
    adjoint, _ = adjoint_of([pieces[t] for t in range(pieces.shape[0])], green, pieces.shape[0])
    freqs, _, groups, rows, cells = adjoint.shape
    adjoint = adjoint.reshape(freqs, 2, groups * rows, cells)
    fields = lax.all_gather(background, "rx", axis=0, tiled=True)
    fields = fields.transpose(1, 2, 0, 3).astype(jnp.float32)
    return lax.psum(jnp.sum(adjoint * fields, axis=(0, 1, 2)), "rx")


def solution(mesh):
    placed = (
        P(None, "tx", "rx"),
        P("tx", "rx"),
        P(None, None, "rx", "tx"),
        P("rx", None, None, "tx"),
    )
    body = box_shards if (mesh.shape["tx"], mesh.shape["rx"]) == (4, 8) else plain_shards
    return jax.shard_map(body, mesh=mesh, in_specs=placed, out_specs=P("tx"), check_vma=False)
```
